512 devices in a mesh: shot: 16 (over z_hi, y, core), mesh: 32 (over z_lo, x).
Axes of the slice: x: 4, y: 4, z: 16 (z_hi: 2, z_lo: 8; z = z_hi * 8 + z_lo), core: 2. Of those that a mesh axis runs over, the one named last changes fastest.
Arguments:
- adjoint_state: float32 [16, 13, 35, 4096], P('shot', None, None, 'mesh'), may hold values from -6 to 6
- forward_states: float32 [16, 2, 13, 35, 4096], P('shot', None, None, None, 'mesh'), may hold values from -6 to 6
- material: float32 [6, 35, 4096], P(None, None, 'mesh'), may hold values from 0.5 to 2
- coupling: float32 [3, 6, 13, 13], replicated, may hold values from -0.375 to 0.375
- metric: float32 [3, 3, 4096], P(None, None, 'mesh'), may hold values from -4 to 4
- face_normals: float32 [3, 4, 4096], P(None, None, 'mesh'), may hold values from -4 to 4
- face_scale: float32 [4, 4096], P(None, 'mesh'), may hold values from 1 to 3
- face_neighbours: int32 [4, 4096], P(None, 'mesh'), may hold values from 0 to 639, as said below
- face_orientation: int32 [4, 4096], P(None, 'mesh'), may hold values from 0 to 5
- send_faces: int32 [4096], P('mesh'), may hold values from 0 to 511, as said below
- history_steps: float32 [5, 6, 35, 4096], P(None, None, None, 'mesh')
- history_changes: float32 [5, 6, 35, 4096], P(None, None, None, 'mesh'), as said below
Outputs:
- adjoint_final: float32 [16, 13, 35, 4096], P('shot', None, None, 'mesh')
- direction: float32 [6, 35, 4096], P(None, None, ('mesh', 'shot'))
The draws below stay inside these ranges and needn't reach their ends.
Inputs may be any that keep to these rules, and one draw needn't show every extreme that they name: `face_neighbours`: local faces of a partition are numbered x * 128 + e. Each face either forms a pair with another local face (each names the other) or reads exactly one of the 128 ghost slots, and every ghost slot is read by exactly one face; on every partition the face that reads slot 512 + j is send_faces[j] and the face that reads slot 576 + j is send_faces[64 + j]. `send_faces`: the 128 entries of one partition are distinct local face numbers. `history_changes`: for every stored pair, s_i . y_i is positive.
All inputs are finite; a program needn't handle non-finite values.
Results may differ from the reference program's by a relative error of at most 0.0003.
Values sent between devices are 32-bit elements; how exact they have to be, the bound alone decides.
A program may use at most 64 MiB of HBM per device.

```python
import math
import jax
import jax.numpy as jnp
import numpy as np
from jax import lax

NF = 13
NB = 35
NFN = 15
NM = 6
HIST = 5
STEPS = 2
E_DEV = 128
BFACE = 64
SHOTS = 16
ELEMS = 4096
N_MESH = 32


def face_tables(key):
    face_count = 4 * E_DEV
    border = E_DEV // 2

    def one_partition(part_key):
        shuffled = jax.random.permutation(part_key, face_count).astype(jnp.int32)
        position = jnp.arange(face_count, dtype=jnp.int32)
        partner = 2 * border + jnp.bitwise_xor(jnp.maximum(position - 2 * border, 0), 1)
        paired = shuffled[jnp.clip(partner, 0, face_count - 1)]
        ghost_slot = face_count + position
        slot_values = jnp.where(position < 2 * border, ghost_slot, paired)
        result_table = jnp.zeros((face_count,), jnp.int32).at[shuffled].set(slot_values)
        return (result_table.reshape(4, E_DEV), shuffled[:2 * border])
    part_keys = jax.random.split(key, N_MESH)
    tables, send_lists = jax.vmap(one_partition)(part_keys)
    return (tables.transpose(1, 0, 2).reshape(4, E_DEV * N_MESH), send_lists.reshape(-1))


def draw_face_neighbours(key, part):
    return face_tables(jax.random.fold_in(key, 17))[0]


def draw_send_faces(key, part):
    return face_tables(jax.random.fold_in(key, 17))[1]


def history_pair(key):
    total_elems = E_DEV * N_MESH
    array_shape = (HIST, NM, NB, total_elems)
    pair_keys = jax.random.split(key, 6)
    base_draw = jax.random.normal(pair_keys[0], array_shape, jnp.float32)
    row_scale = jnp.exp(jax.random.uniform(pair_keys[2], (HIST, NM, NB, 1), jnp.float32, 0.0, math.log(10.0)))
    column_scale = jnp.exp(jax.random.uniform(pair_keys[3], (1, 1, 1, total_elems), jnp.float32, 0.0, math.log(10.0)))
    position = jnp.arange(total_elems, dtype=jnp.float32) / (total_elems - 1)
    rising = jnp.sqrt(1.0 + 2.0 * position)
    step_draw = 0.3 * base_draw * row_scale * column_scale * rising
    curvature = jnp.exp(jax.random.uniform(pair_keys[4], (HIST, 1, 1, 1), jnp.float32, math.log(0.3), math.log(3.0)))
    ratio_draw = jax.random.uniform(pair_keys[5], array_shape, jnp.float32, 0.5, 2.0) * (1.0 + 2.0 * position)
    return (step_draw, step_draw * ratio_draw * curvature)


def draw_history_steps(key, part):
    return history_pair(jax.random.fold_in(key, 29))[0]


def draw_history_changes(key, part):
    return history_pair(jax.random.fold_in(key, 29))[1]


def touch_ends(values, stream_key, smallest, top_value):
    extent = values.shape
    place = [jax.random.randint(jax.random.fold_in(stream_key, axis), (), 0, extent[axis]) for axis in range(len(extent))]
    values = values.at[tuple(place)].set(smallest)
    longest = extent.index(max(extent))
    place[longest] = (place[longest] + 1) % extent[longest]
    return values.at[tuple(place)].set(top_value)


def shard_levels(own_key, extent, cuts, smallest, high):
    def one(dim, parts):
        steps = jax.random.uniform(jax.random.fold_in(jax.random.fold_in(own_key, 6), dim), (parts,), jnp.float32, smallest / len(cuts), high / len(cuts))
        return jnp.repeat(jnp.exp(steps), extent[dim] // parts).reshape((-1,) + (1,) * (len(extent) - dim - 1))

    level = one(*cuts[0])
    for cut in cuts[1:]:
        level = level * one(*cut)
    return level


def centred(rng, shape, spread, reach, cuts=(), kind=jnp.bfloat16):
    level = shard_levels(rng, shape, cuts, -0.22, 0.18) if cuts else 1.0
    values = jax.random.normal(rng, shape, jnp.float32) * spread * level
    return jnp.minimum(jnp.maximum(values, -reach), reach).astype(kind)


def setup_inputs(seed: int = 0) -> dict:
    key_of = jax.random.split(jax.random.key(seed), 13)
    return {
        "adjoint_state": centred(key_of[0], (SHOTS, NF, NB, ELEMS), 1.0, 6.0, ((0, 16), (3, 32)), jnp.float32),
        "forward_states": centred(key_of[1], (SHOTS, STEPS, NF, NB, ELEMS), 1.0, 6.0, ((0, 16), (4, 32)), jnp.float32),
        "material": jnp.clip(jnp.exp(math.log(2.0) - 1.3862944 * jax.random.uniform(key_of[2], (NM, NB, ELEMS), jnp.float32) ** shard_levels(key_of[2], (NM, NB, ELEMS), ((2, 32),), -0.2, 0.2)), 0.5, 2.0),
        "coupling": centred(key_of[3], (3, NM, NF, NF), (3 * NM * NF) ** -0.5, 0.375, (), jnp.float32),
        "metric": centred(key_of[4], (3, 3, ELEMS), 1.0, 4.0, ((2, 32),), jnp.float32),
        "face_normals": centred(key_of[5], (3, 4, ELEMS), 1.0, 4.0, ((2, 32),), jnp.float32),
        "face_scale": jnp.clip(jnp.exp(math.log(3.0) - 1.0986123 * jax.random.uniform(key_of[6], (4, ELEMS), jnp.float32) ** shard_levels(key_of[6], (4, ELEMS), ((1, 32),), -0.2, 0.2)), 1.0, 3.0),
        "face_neighbours": draw_face_neighbours(jax.random.fold_in(key_of[12], 71), 0),
        "face_orientation": touch_ends(jax.random.randint(key_of[8], (4, ELEMS), 0, 6), jax.random.fold_in(key_of[8], 1), 0, 5).astype(jnp.int32),
        "send_faces": draw_send_faces(jax.random.fold_in(key_of[12], 71), 0),
        "history_steps": draw_history_steps(jax.random.fold_in(key_of[12], 71), 0),
        "history_changes": draw_history_changes(jax.random.fold_in(key_of[12], 71), 0),
    }


HIGH = lax.Precision.HIGHEST
STEP_SIZE = 0.02


def invert_matrix(matrix):
    order_count = matrix.shape[0]
    working = np.concatenate([matrix * 1.0, np.eye(order_count)], axis=1)
    for column in range(order_count):
        pivot_row = column + int(np.argmax(np.abs(working[column:, column])))
        working[[column, pivot_row]] = working[[pivot_row, column]]
        working[column] = working[column] / working[column, column]
        for target in range(order_count):
            if target != column:
                working[target] = working[target] - working[target, column] * working[column]
    return working[:, order_count:]


def basis_tables():
    points = [(across, along, upward) for upward in range(5) for along in range(5 - upward) for across in range(5 - upward - along)]
    exponents = np.array(points) * 1.0
    coords = exponents / 4.0
    vander = np.prod(coords[:, None, :] ** exponents[None, :, :], axis=2)
    inverse = invert_matrix(vander)
    derivs = []
    for direction_axis in range(3):
        lowered = np.maximum(exponents - np.eye(3)[direction_axis], 0.0)
        slopes = exponents[None, :, direction_axis] * np.prod(coords[:, None, :] ** lowered[None, :, :], axis=2)
        derivs.append(slopes @ inverse)
    moments = np.array([[math.factorial(first[0] + second[0]) * math.factorial(first[1] + second[1]) * math.factorial(first[2] + second[2]) / math.factorial(sum(first) + sum(second) + 3) for second in points] for first in points])
    mass_matrix = inverse.T @ moments @ inverse
    lattice = [(across, along) for along in range(5) for across in range(5 - along)]
    lattice_powers = np.array(lattice) * 1.0
    face_vander = np.prod((lattice_powers / 4.0)[:, None, :] ** lattice_powers[None, :, :], axis=2)
    face_inverse = invert_matrix(face_vander)
    face_moments = np.array([[math.factorial(first[0] + second[0]) * math.factorial(first[1] + second[1]) / math.factorial(sum(first) + sum(second) + 2) for second in lattice] for first in lattice])
    face_mass = face_inverse.T @ face_moments @ face_inverse
    numbers = {point: number for number, point in enumerate(points)}
    face_points = [
        [(across, along, 0) for across, along in lattice],
        [(across, 0, along) for across, along in lattice],
        [(0, across, along) for across, along in lattice],
        [(across, along, 4 - across - along) for across, along in lattice]]
    face_nodes = np.array([[numbers[point] for point in listing] for listing in face_points], np.int32)
    mass_inverse = invert_matrix(mass_matrix)
    lift_tables = []
    for face_number in range(4):
        selector = np.eye(35)[face_nodes[face_number]]
        lift_tables.append(mass_inverse @ selector.T @ face_mass)
    orderings = [(0, 1, 2), (1, 2, 0), (2, 0, 1), (1, 0, 2), (0, 2, 1), (2, 1, 0)]
    lattice_numbers = {point: number for number, point in enumerate(lattice)}
    triples = [(across, along, 4 - across - along) for across, along in lattice]
    turn_nodes = np.array([[lattice_numbers[(triple[ordering[0]], triple[ordering[1]])] for triple in triples] for ordering in orderings], np.int32)
    return (jnp.asarray(np.stack(derivs), jnp.float32), jnp.asarray(np.stack(lift_tables), jnp.float32), face_nodes, turn_nodes)


def volume_term(adjoint, material, coupling, metric, derivs):
    reference_grads = jnp.einsum("rab,fbe->rfae", derivs, adjoint, precision=HIGH)
    spatial = jnp.einsum("rde,rfae->dfae", metric, reference_grads, precision=HIGH)
    mixing = jnp.einsum("dpfg,dfae->pgae", coupling, spatial, precision=HIGH)
    return jnp.sum(material[:, None] * mixing, axis=0)


def kernel_term(adjoint, forward, coupling, metric, derivs):
    reference_grads = jnp.einsum("rab,fbe->rfae", derivs, forward, precision=HIGH)
    spatial = jnp.einsum("rde,rfae->dfae", metric, reference_grads, precision=HIGH)
    mixing = jnp.einsum("dpfg,dgae->pfae", coupling, spatial, precision=HIGH)
    return jnp.sum(mixing * adjoint[None], axis=1)


def surface_term(jump_trace, face_material, face_normals, face_scale, coupling, lift_tables):
    weighted = face_normals[:, None, None] * jump_trace[None]
    mixing = jnp.einsum("dpfg,dfnxe->pgnxe", coupling, weighted, precision=HIGH)
    face_flux = 0.5 * jnp.sum(face_material[:, None] * mixing, axis=0) + 0.5 * jump_trace
    return jnp.einsum("xan,fnxe->fae", lift_tables, face_flux * face_scale[None, None], precision=HIGH)


def two_loop(total_grad, history_steps, history_changes):
    curvature = [jnp.sum(history_steps[slot] * history_changes[slot]) for slot in range(HIST)]
    alphas = [None] * HIST
    work = total_grad
    for slot in reversed(range(HIST)):
        alphas[slot] = jnp.sum(history_steps[slot] * work) / curvature[slot]
        work = work - alphas[slot] * history_changes[slot]
    scaling = curvature[HIST - 1] / jnp.sum(history_changes[HIST - 1] * history_changes[HIST - 1])
    work = scaling * work
    for slot in range(HIST):
        beta_now = jnp.sum(history_changes[slot] * work) / curvature[slot]
        work = work + (alphas[slot] - beta_now) * history_steps[slot]
    return -work


def reference(adjoint_state, forward_states, material, coupling, metric, face_normals, face_scale, face_neighbours, face_orientation, send_faces, history_steps, history_changes):
    derivs, lift_tables, face_nodes, turn_nodes = basis_tables()
    face_material = material[:, face_nodes.T, :]
    neighbours = face_neighbours.reshape(4, N_MESH, E_DEV).transpose(1, 0, 2).reshape(N_MESH, 4 * E_DEV)
    orient = face_orientation.reshape(4, N_MESH, E_DEV).transpose(1, 0, 2).reshape(N_MESH, 4 * E_DEV)
    sends = send_faces.reshape(N_MESH, 2 * BFACE)

    def outer_traces(inner_trace):
        partitioned = inner_trace.reshape(NF, NFN, 4, N_MESH, E_DEV).transpose(3, 0, 1, 2, 4).reshape(N_MESH, NF, NFN, 4 * E_DEV)
        sent_traces = jax.vmap(lambda traces, listing: traces[:, :, listing])(partitioned, sends)
        empty = jnp.zeros((1, NF, NFN, BFACE), jnp.float32)
        from_below = jnp.concatenate([empty, sent_traces[:-1, :, :, BFACE:]], axis=0)
        from_above = jnp.concatenate([sent_traces[1:, :, :, :BFACE], empty], axis=0)
        extended = jnp.concatenate([partitioned, from_below, from_above], axis=3)
        gathered = jax.vmap(lambda traces, listing: traces[:, :, listing])(extended, neighbours)
        turned = gathered
        for option in range(6):
            turned = jnp.where((orient == option)[:, None, None, :], gathered[:, :, turn_nodes[option], :], turned)
        return turned.reshape(N_MESH, NF, NFN, 4, E_DEV).transpose(1, 2, 3, 0, 4).reshape(NF, NFN, 4, ELEMS)

    def one_shot(operands):
        adjoint, forwards = operands
        gradient = jnp.zeros((NM, NB, ELEMS), jnp.float32)
        for step_index in range(STEPS):
            inner_trace = adjoint[:, face_nodes.T, :]
            jump_trace = outer_traces(inner_trace) - inner_trace
            change = volume_term(adjoint, material, coupling, metric, derivs) + surface_term(jump_trace, face_material, face_normals, face_scale, coupling, lift_tables)
            adjoint = adjoint + STEP_SIZE * change
            gradient = gradient + STEP_SIZE * kernel_term(adjoint, forwards[step_index], coupling, metric, derivs)
        return adjoint, gradient

    finals, gradients = lax.map(one_shot, (adjoint_state, forward_states))
    total_grad = jnp.sum(gradients, axis=0)
    return finals, two_loop(total_grad, history_steps, history_changes)
```

```python
import functools
import math

import jax
import jax.numpy as jnp
import ml_dtypes
import numpy as np
from jax import lax
from jax.experimental import pallas as pl
from jax.experimental.pallas import tpu as pltpu
from jax.sharding import PartitionSpec as P

F32 = jnp.float32
BF16 = jnp.bfloat16
HIGH = lax.Precision.HIGHEST
STEP_SIZE = 0.02
MESH = pl.DeviceIdType.MESH

NF = 13
FP = 16
NB = 35
AP = 40
KP = 48
NFN = 15
NM = 6
NE = 128
HIST = 5


def invert_matrix(matrix):
    order_count = matrix.shape[0]
    working = np.concatenate([matrix * 1.0, np.eye(order_count)], axis=1)
    for column in range(order_count):
        pivot_row = column + int(np.argmax(np.abs(working[column:, column])))
        working[[column, pivot_row]] = working[[pivot_row, column]]
        working[column] = working[column] / working[column, column]
        for target in range(order_count):
            if target != column:
                working[target] = working[target] - working[target, column] * working[column]
    return working[:, order_count:]


def basis_tables():
    points = [
        (across, along, upward)
        for upward in range(5)
        for along in range(5 - upward)
        for across in range(5 - upward - along)
    ]
    exponents = np.array(points) * 1.0
    coords = exponents / 4.0
    vander = np.prod(coords[:, None, :] ** exponents[None, :, :], axis=2)
    inverse = invert_matrix(vander)
    derivs = []
    for direction_axis in range(3):
        lowered = np.maximum(exponents - np.eye(3)[direction_axis], 0.0)
        slopes = exponents[None, :, direction_axis] * np.prod(
            coords[:, None, :] ** lowered[None, :, :], axis=2
        )
        derivs.append(slopes @ inverse)
    moments = np.array(
        [
            [
                math.factorial(first[0] + second[0])
                * math.factorial(first[1] + second[1])
                * math.factorial(first[2] + second[2])
                / math.factorial(sum(first) + sum(second) + 3)
                for second in points
            ]
            for first in points
        ]
    )
    mass_matrix = inverse.T @ moments @ inverse
    lattice = [(across, along) for along in range(5) for across in range(5 - along)]
    lattice_powers = np.array(lattice) * 1.0
    face_vander = np.prod((lattice_powers / 4.0)[:, None, :] ** lattice_powers[None, :, :], axis=2)
    face_inverse = invert_matrix(face_vander)
    face_moments = np.array(
        [
            [
                math.factorial(first[0] + second[0])
                * math.factorial(first[1] + second[1])
                / math.factorial(sum(first) + sum(second) + 2)
                for second in lattice
            ]
            for first in lattice
        ]
    )
    face_mass = face_inverse.T @ face_moments @ face_inverse
    numbers = {point: number for number, point in enumerate(points)}
    face_points = [
        [(across, along, 0) for across, along in lattice],
        [(across, 0, along) for across, along in lattice],
        [(0, across, along) for across, along in lattice],
        [(across, along, 4 - across - along) for across, along in lattice],
    ]
    face_nodes = np.array(
        [[numbers[point] for point in listing] for listing in face_points], np.int32
    )
    mass_inverse = invert_matrix(mass_matrix)
    lift_tables = []
    for face_number in range(4):
        selector = np.eye(35)[face_nodes[face_number]]
        lift_tables.append(mass_inverse @ selector.T @ face_mass)
    orderings = [(0, 1, 2), (1, 2, 0), (2, 0, 1), (1, 0, 2), (0, 2, 1), (2, 1, 0)]
    lattice_numbers = {point: number for number, point in enumerate(lattice)}
    triples = [(across, along, 4 - across - along) for across, along in lattice]
    turn_nodes = np.array(
        [
            [lattice_numbers[triple[ordering[0]], triple[ordering[1]]] for triple in triples]
            for ordering in orderings
        ],
        np.int32,
    )
    return (
        np.stack(derivs).astype(np.float32),
        np.stack(lift_tables).astype(np.float32),
        face_nodes,
        turn_nodes,
    )


DERIVS, LIFTS, FACE_NODES, TURN = basis_tables()


def np_split(table):
    high = table.astype(ml_dtypes.bfloat16)
    low = (table - high.astype(np.float32)).astype(ml_dtypes.bfloat16)
    return np.concatenate([high, high, low], axis=1)


def deriv_table():
    table = np.zeros((128, KP), np.float32)
    for r in range(3):
        table[r * AP : r * AP + NB, :NB] = DERIVS[r]
    return np_split(table)


def lift_table():
    table = np.zeros((KP, 64), np.float32)
    for x in range(4):
        table[:NB, x * 16 : x * 16 + NFN] = LIFTS[x]
    return np_split(table)


def split(x):
    high = x.astype(BF16)
    low = (x - high.astype(F32)).astype(BF16)
    return high, low


def stack3(x):
    high, low = split(x)
    return jnp.concatenate([high, low, high], axis=0)


def mm(a, b):
    return jnp.dot(a, b, preferred_element_type=F32)


def body(
    dims,
    adj_hbm, fwd_hbm, mat_hbm, hs_hbm, hy_hbm,
    cpl, metric, normals, scale, nbr, orient, send, deriv3, lift3,
    fin_hbm, dir_ref,
    adj, fwd, mat, hs, hy, fin,
    lam_b, fwd_b, lam_a, spat, mixg, vol, flux, matp,
    trace, oh_send, oh_nbr, outer,
    msg_d, msg_u, got_d, got_u,
    ct32, ct_v, ct_g,
    grads, gt, rs_got, rs_mid, rs_last, prods, ar_a, ar_a_got, ar_b, ar_b_got, scal,
    load_sem, fin_sem, halo_send, halo_recv, rs_send, rs_recv, ar_send, ar_recv,
):
    n_hi, n_q, n_x, n_zl = dims
    n_shot, n_mesh = n_hi * n_q, n_x * n_zl
    share = NE // n_shot
    s_id = lax.axis_index("shot")
    m_id = lax.axis_index("mesh")
    hi_id, q_id = s_id // n_q, s_id % n_q
    zl_id, x_id = m_id // n_x, m_id % n_x
    has_below = m_id > 0
    has_above = m_id < n_mesh - 1

    def load(src, dst, k):
        return pltpu.make_async_copy(src, dst, load_sem.at[k])

    loads = [
        load(adj_hbm.at[0], adj, 0),
        load(mat_hbm, mat, 1),
        load(fwd_hbm.at[0], fwd, 2),
        load(hs_hbm, hs, 3),
        load(hy_hbm, hy, 4),
    ]
    for one in loads:
        one.start()

    q_peers = [hi_id * n_q + (q_id + o) % n_q for o in range(1, n_q)]
    hi_peers = [((hi_id + o) % n_hi) * n_q + q_id for o in range(1, n_hi)]
    x_peers = [zl_id * n_x + (x_id + o) % n_x for o in range(1, n_x)]
    zl_peers = [((zl_id + o) % n_zl) * n_x + x_id for o in range(1, n_zl)]

    barrier = pltpu.get_barrier_semaphore()
    for peer in q_peers + hi_peers:
        pl.semaphore_signal(barrier, inc=1, device_id={"shot": peer}, device_id_type=MESH)
    for peer in x_peers + zl_peers:
        pl.semaphore_signal(barrier, inc=1, device_id={"mesh": peer}, device_id_type=MESH)

    @pl.when(has_below)
    def _():
        pl.semaphore_signal(barrier, inc=1, device_id={"mesh": m_id - 1}, device_id_type=MESH)

    @pl.when(has_above)
    def _():
        pl.semaphore_signal(barrier, inc=1, device_id={"mesh": m_id + 1}, device_id_type=MESH)

    for f in range(NF):
        lam_b[f, 32:KP, :] = jnp.zeros((KP - 32, NE), F32)
        fwd_b[f, 32:KP, :] = jnp.zeros((KP - 32, NE), F32)
    matp[:, 32:AP, :] = jnp.zeros((NM, AP - 32, NE), F32)
    lam_a[...] = jnp.zeros(lam_a.shape, F32)

    def clear(i, carry):
        spat[pl.ds(pl.multiple_of(i * KP, KP), KP), :] = jnp.zeros((KP, NE), F32)
        return carry

    lax.fori_loop(0, AP, clear, 0)
    ct32[...] = jnp.zeros(ct32.shape, F32)
    for x in range(4):
        flux[(x * 16 + 15) * FP : (x * 16 + 16) * FP, :] = jnp.zeros((FP, NE), F32)
    prods[...] = jnp.zeros(prods.shape, F32)
    grads[240:256, :] = jnp.zeros((16, NE), F32)

    @pl.when(jnp.logical_not(has_below))
    def _():
        got_u[...] = jnp.zeros(got_u.shape, F32)

    @pl.when(jnp.logical_not(has_above))
    def _():
        got_d[...] = jnp.zeros(got_d.shape, F32)

    rows_s = lax.broadcasted_iota(jnp.int32, (512, NE), 0)
    oh_send[...] = jnp.where(rows_s == send[...], 1.0, 0.0).astype(BF16)
    rows_n = lax.broadcasted_iota(jnp.int32, (640, NE), 0)
    for x in range(4):
        oh_nbr[:, x * NE : (x + 1) * NE] = jnp.where(rows_n == nbr[x : x + 1, :], 1.0, 0.0).astype(BF16)

    cols = lax.broadcasted_iota(jnp.int32, (NF, 3 * KP), 1)
    rows = lax.broadcasted_iota(jnp.int32, (NF, 3 * KP), 0)
    places = [
        jnp.where(
            (cols == d * FP + rows) | (cols == KP + d * FP + rows) | (cols == 2 * KP + d * FP + rows), 1.0, 0.0
        )
        for d in range(3)
    ]
    table_cols = lax.broadcasted_iota(jnp.int32, (NM * FP, 3 * KP), 1)

    def to_table(dst):
        whole = ct32[...]
        high = whole.astype(BF16)
        low = whole - high.astype(F32)
        dst[...] = jnp.where(table_cols < 2 * KP, high.astype(F32), low).astype(BF16)

    for p in range(NM):
        total = None
        for d in range(3):
            part = lax.dot_general(
                cpl[d, p], places[d], (((0,), (0,)), ((), ())), precision=HIGH, preferred_element_type=F32
            )
            total = part if total is None else total + part
        ct32[p * FP : p * FP + NF, :] = total
    to_table(ct_v)
    for p in range(NM):
        total = None
        for d in range(3):
            part = lax.dot_general(
                cpl[d, p], places[d], (((1,), (0,)), ((), ())), precision=HIGH, preferred_element_type=F32
            )
            total = part if total is None else total + part
        ct32[p * FP : p * FP + NF, :] = total
    to_table(ct_g)

    lane = lax.broadcasted_iota(jnp.int32, (FP, NE), 1)
    low_half = lane < 64

    loads[0].wait()
    for f in range(NF):
        lam_b[f, 0:NB, :] = adj[f]
        lam_a[pl.ds(f, AP, stride=FP), :] = lam_b[f, 0:AP, :]
    loads[1].wait()
    matp[:, 0:NB, :] = mat[...]

    def derivative(field):
        for first in range(0, NF, 2):
            group = range(first, min(first + 2, NF))
            out = mm(deriv3[...], jnp.concatenate([stack3(field[f]) for f in group], axis=1))
            for i, f in enumerate(group):
                slab = [out[r * AP : (r + 1) * AP, i * NE : (i + 1) * NE] for r in range(3)]
                for d in range(3):
                    s = metric[0, d : d + 1, :] * slab[0]
                    s = s + metric[1, d : d + 1, :] * slab[1]
                    s = s + metric[2, d : d + 1, :] * slab[2]
                    spat[pl.ds(d * FP + f, AP, stride=KP), :] = s

    def mixed(table, base):
        parts = []
        for j in range(8):
            at = pl.multiple_of((base + j) * KP, KP)
            parts.append(stack3(spat[pl.ds(at, KP), :]))
        return mm(table[...], jnp.concatenate(parts, axis=1))

    def volume():
        derivative(lam_b)

        def block(i, carry):
            base = pl.multiple_of(i * 8, 8)
            mix = mixed(ct_v, base)
            params = [matp[p, pl.ds(base, 8), :] for p in range(NM)]
            for j in range(8):
                acc = params[0][j : j + 1, :] * mix[0:FP, j * NE : (j + 1) * NE]
                for p in range(1, NM):
                    acc = acc + params[p][j : j + 1, :] * mix[p * FP : (p + 1) * FP, j * NE : (j + 1) * NE]
                vol[pl.ds(pl.multiple_of((base + j) * FP, FP), FP), :] = acc
            return carry

        lax.fori_loop(0, AP // 8, block, 0)

    def forward_mix(t):
        for f in range(NF):
            fwd_b[f, 0:NB, :] = fwd[t, f]
        derivative(fwd_b)

        def block(i, carry):
            base = pl.multiple_of(i * 8, 8)
            mix = mixed(ct_g, base)
            for j in range(8):
                at = pl.multiple_of((base + j) * NM * FP, NM * FP)
                mixg[t, pl.ds(at, NM * FP), :] = mix[:, j * NE : (j + 1) * NE]
            return carry

        lax.fori_loop(0, AP // 8, block, 0)

    def times_lam(i, carry):
        lam = lam_a[pl.ds(pl.multiple_of(i * FP, FP), FP), :]
        for p in range(NM):
            at = pl.ds(pl.multiple_of(i * NM * FP + p * FP, FP), FP)
            mixg[0, at, :] = mixg[0, at, :] * lam
        return carry

    def kernel_sum(i, carry):
        lam = lam_a[pl.ds(pl.multiple_of(i * FP, FP), FP), :]
        rows_out = []
        for p in range(NM):
            at = pl.ds(pl.multiple_of(i * NM * FP + p * FP, FP), FP)
            both = mixg[0, at, :] + mixg[1, at, :] * lam
            rows_out.append(jnp.sum(both, axis=0, keepdims=True))
        for p in range(NM):
            grads[pl.ds(i + p * AP, 1), :] = rows_out[p] * STEP_SIZE
        return carry

    def inner_of(n, x):
        at = int(FACE_NODES[x][n]) * FP
        return lam_a[at : at + FP, :]

    def halo_copies(t):
        down = pltpu.make_async_remote_copy(
            src_ref=msg_d.at[t], dst_ref=got_d.at[t], send_sem=halo_send.at[t, 0], recv_sem=halo_recv.at[t, 0],
            device_id={"mesh": m_id - 1}, device_id_type=MESH,
        )
        up = pltpu.make_async_remote_copy(
            src_ref=msg_u.at[t], dst_ref=got_u.at[t], send_sem=halo_send.at[t, 1], recv_sem=halo_recv.at[t, 1],
            device_id={"mesh": m_id + 1}, device_id_type=MESH,
        )
        return down, up

    def send_traces(t):
        for n in range(NFN):
            for x in range(4):
                high, low = split(inner_of(n, x))
                trace[n * FP : (n + 1) * FP, x * NE : (x + 1) * NE] = high
                trace[240 + n * FP : 240 + (n + 1) * FP, x * NE : (x + 1) * NE] = low
        both = mm(trace[...], oh_send[...])
        picked = both[0:240] + both[240:480]
        for j in range(8):
            first = picked[j * FP : (j + 1) * FP]
            if j < 7:
                second = picked[(j + 8) * FP : (j + 9) * FP]
            else:
                second = jnp.zeros((FP, NE), F32)
            msg_d[t, j * FP : (j + 1) * FP, :] = jnp.where(low_half, first, pltpu.roll(second, 64, 1))
            msg_u[t, j * FP : (j + 1) * FP, :] = jnp.where(low_half, pltpu.roll(first, 64, 1), second)
        if t == 0:
            n_wait = n_q + n_hi + n_x + n_zl - 4
            pl.semaphore_wait(barrier, n_wait + has_below.astype(jnp.int32) + has_above.astype(jnp.int32))
        down, up = halo_copies(t)

        @pl.when(has_below)
        def _():
            down.start()

        @pl.when(has_above)
        def _():
            up.start()

        local = mm(trace[...], oh_nbr[0:512, :])
        outer[...] = local[0:240] + local[240:480]

    def surface(t):
        down, up = halo_copies(t)

        @pl.when(has_below)
        def _():
            down.wait_send()

        @pl.when(has_above)
        def _():
            up.wait_send()

        @pl.when(has_above)
        def _():
            down.wait_recv()

        @pl.when(has_below)
        def _():
            up.wait_recv()

        tops, bottoms = [], []
        for j in range(8):
            above = got_d[t, j * FP : (j + 1) * FP, :]
            below = got_u[t, j * FP : (j + 1) * FP, :]
            tops.append(jnp.where(low_half, below, pltpu.roll(above, 64, 1)))
            bottoms.append(jnp.where(low_half, pltpu.roll(below, 64, 1), above))
        ghosts = jnp.concatenate(tops + bottoms[:7], axis=0)
        high, low = split(ghosts)
        part = mm(jnp.concatenate([high, low], axis=0), oh_nbr[512:640, :])
        outer[...] = outer[...] + (part[0:240] + part[240:480])

        turns = [jnp.broadcast_to(orient[x : x + 1, :], (FP, NE)) for x in range(4)]
        halves = [0.5 * scale[x : x + 1, :] for x in range(4)]
        for n in range(NFN):
            sources = {}
            for o in range(6):
                sources.setdefault(int(TURN[o][n]), []).append(o)
            sources = list(sources.items())
            jumps, weighted = [], []
            for x in range(4):
                at = sources[0][0] * FP
                value = outer[at : at + FP, x * NE : (x + 1) * NE]
                for node, options in sources[1:]:
                    mask = turns[x] == options[0]
                    for o in options[1:]:
                        mask = mask | (turns[x] == o)
                    value = jnp.where(mask, outer[node * FP : (node + 1) * FP, x * NE : (x + 1) * NE], value)
                jump = value - inner_of(n, x)
                jumps.append(jump)
                weighted.append(
                    stack3(jnp.concatenate([normals[d, x : x + 1, :] * jump for d in range(3)], axis=0))
                )
            mix = mm(ct_v[...], jnp.concatenate(weighted, axis=1))
            for x in range(4):
                node = int(FACE_NODES[x][n])
                acc = jumps[x]
                for p in range(NM):
                    acc = acc + matp[p, node : node + 1, :] * mix[p * FP : (p + 1) * FP, x * NE : (x + 1) * NE]
                at = (x * 16 + n) * FP
                flux[at : at + FP, :] = acc * halves[x]

        for first in range(0, NF, 2):
            group = range(first, min(first + 2, NF))
            rhs = [stack3(flux[pl.ds(g, 64, stride=FP), :]) for g in group]
            out = mm(lift3[...], jnp.concatenate(rhs, axis=1))
            for i, g in enumerate(group):
                change = out[0:AP, i * NE : (i + 1) * NE] + vol[pl.ds(g, AP, stride=FP), :]
                new = lam_b[g, 0:AP, :] + STEP_SIZE * change
                if t == 0:
                    lam_b[g, 0:AP, :] = new
                else:
                    fin[g] = new[0:NB]
                lam_a[pl.ds(g, AP, stride=FP), :] = new

    yy_row = {}
    for i in range(HIST):
        for j in range(i, HIST):
            yy_row[i, j] = yy_row[j, i] = 25 + len([k for k in yy_row if k[0] <= k[1]])

    def dot_rows(a, i, b, j):
        acc = a[i, 0] * b[j, 0]
        for p in range(1, NM):
            acc = acc + a[i, p] * b[j, p]
        return jnp.sum(acc, axis=0, keepdims=True)

    def history():
        for i in range(HIST):
            for j in range(HIST):
                row = i * HIST + j
                prods[row : row + 1, :] = dot_rows(hs, i, hy, j)
                if j >= i:
                    row = yy_row[i, j]
                    prods[row : row + 1, :] = dot_rows(hy, i, hy, j)

    send_traces(0)
    volume()
    loads[2].wait()
    forward_mix(0)
    surface(0)
    send_traces(1)
    volume()
    forward_mix(1)
    lax.fori_loop(0, AP, times_lam, 0)
    loads[3].wait()
    loads[4].wait()
    history()
    surface(1)
    final_out = pltpu.make_async_copy(fin, fin_hbm.at[0], fin_sem.at[0])
    final_out.start()

    lax.fori_loop(0, AP, kernel_sum, 0)
    for i in range(HIST):
        for h, hist in enumerate((hs, hy)):
            acc = hist[i, 0] * grads[0:NB, :]
            for p in range(1, NM):
                acc = acc + hist[i, p] * grads[p * AP : p * AP + NB, :]
            row = 240 + h * HIST + i
            grads[row : row + 1, :] = jnp.sum(acc, axis=0, keepdims=True)
    left = jnp.transpose(grads[0:128, :])
    right = jnp.transpose(grads[128:256, :])
    wide = lax.broadcasted_iota(jnp.int32, (NE, NE), 1)
    right = jnp.where(wide >= 112, jnp.sum(right, axis=0, keepdims=True), right)
    half = n_q * share
    for h in range(n_hi):
        gt[h, :, 0:128] = left[h * half : (h + 1) * half]
        gt[h, :, 128:256] = right[h * half : (h + 1) * half]

    firsts = []
    for o in range(1, n_q):
        peer_q = (q_id + o) % n_q
        firsts.append(
            pltpu.make_async_remote_copy(
                src_ref=gt.at[:, pl.ds(pl.multiple_of(peer_q * share, share), share), :],
                dst_ref=rs_got.at[o - 1],
                send_sem=rs_send.at[o - 1], recv_sem=rs_recv.at[o - 1],
                device_id={"shot": q_peers[o - 1]}, device_id_type=MESH,
            )
        )
    for one in firsts:
        one.start()
    gram = jnp.sum(jnp.transpose(prods[...]), axis=0, keepdims=True)
    mine = gt[:, pl.ds(pl.multiple_of(q_id * share, share), share), :]
    for o, one in enumerate(firsts):
        one.wait_recv()
        mine = mine + rs_got[o]
    rs_mid[...] = mine
    seconds = []
    for o in range(1, n_hi):
        seconds.append(
            pltpu.make_async_remote_copy(
                src_ref=rs_mid.at[(hi_id + o) % n_hi],
                dst_ref=rs_last.at[o - 1],
                send_sem=rs_send.at[n_q - 2 + o], recv_sem=rs_recv.at[n_q - 2 + o],
                device_id={"shot": hi_peers[o - 1]}, device_id_type=MESH,
            )
        )
    for one in seconds:
        one.start()
    total = rs_mid[hi_id]
    for o, one in enumerate(seconds):
        one.wait_recv()
        total = total + rs_last[o]

    narrow = lax.broadcasted_iota(jnp.int32, (8, NE), 1)
    vector = jnp.where(narrow >= 112, jnp.broadcast_to(total[0:1, 128:256], (8, NE)), jnp.broadcast_to(gram, (8, NE)))

    def exchange(value, src, got, peers, first):
        src[...] = value
        copies = [
            pltpu.make_async_remote_copy(
                src_ref=src, dst_ref=got.at[k], send_sem=ar_send.at[first + k], recv_sem=ar_recv.at[first + k],
                device_id={"mesh": peer}, device_id_type=MESH,
            )
            for k, peer in enumerate(peers)
        ]
        for one in copies:
            one.start()
        for k, one in enumerate(copies):
            one.wait_recv()
            value = value + got[k]
        return value, copies

    vector, sent_a = exchange(vector, ar_a, ar_a_got, x_peers, 0)
    vector, sent_b = exchange(vector, ar_b, ar_b_got, zl_peers, n_x - 1)

    scal[...] = jnp.transpose(jnp.broadcast_to(vector[0:1, :], (NE, NE)))

    def num(k):
        return scal[k : k + 1, :]

    def sy(i, j):
        return num(i * HIST + j)

    alphas = [None] * HIST
    for i in reversed(range(HIST)):
        value = num(112 + i)
        for j in range(i + 1, HIST):
            value = value - alphas[j] * sy(i, j)
        alphas[i] = value / sy(i, i)
    gamma = sy(HIST - 1, HIST - 1) / num(yy_row[HIST - 1, HIST - 1])
    rest = []
    for i in range(HIST):
        value = num(112 + HIST + i)
        for j in range(HIST):
            value = value - alphas[j] * num(yy_row[i, j])
        value = gamma * value
        for j in range(i):
            value = value + rest[j] * sy(j, i)
        rest.append(alphas[i] - value / sy(i, i))
    scaled = [gamma * alpha for alpha in alphas]

    shift = (NE - s_id * share) % NE
    turned_total = [jnp.transpose(total[:, 0:128]), jnp.transpose(total[:, 128:256])]
    turned_total = jnp.concatenate(turned_total, axis=0)
    for p in range(NM):
        acc = scaled[0] * hy[0, p] - rest[0] * hs[0, p]
        for i in range(1, HIST):
            acc = acc + scaled[i] * hy[i, p]
            acc = acc - rest[i] * hs[i, p]
        acc = pltpu.roll(acc, shift, 1)
        dir_ref[p] = acc[:, 0:share] - gamma[:, 0:share] * turned_total[p * AP : p * AP + NB, :]

    for one in firsts + seconds + sent_a + sent_b:
        one.wait_send()
    final_out.wait()


def shards(
    dims,
    adjoint_state,
    forward_states,
    material,
    coupling,
    metric,
    face_normals,
    face_scale,
    face_neighbours,
    face_orientation,
    send_faces,
    history_steps,
    history_changes,
):
    n_hi, n_q, n_x, n_zl = dims
    share = NE // (n_hi * n_q)
    vmem = pl.BlockSpec(memory_space=pltpu.VMEM)
    hbm = pl.BlockSpec(memory_space=pl.ANY)
    dma = pltpu.SemaphoreType.DMA
    return pl.pallas_call(
        functools.partial(body, dims),
        out_shape=(
            jax.ShapeDtypeStruct((1, NF, NB, NE), F32),
            jax.ShapeDtypeStruct((NM, NB, share), F32),
        ),
        in_specs=[hbm] * 5 + [vmem] * 9,
        out_specs=(hbm, vmem),
        scratch_shapes=[
            pltpu.VMEM((NF, NB, NE), F32),
            pltpu.VMEM((2, NF, NB, NE), F32),
            pltpu.VMEM((NM, NB, NE), F32),
            pltpu.VMEM((HIST, NM, NB, NE), F32),
            pltpu.VMEM((HIST, NM, NB, NE), F32),
            pltpu.VMEM((NF, NB, NE), F32),
            pltpu.VMEM((NF, KP, NE), F32),
            pltpu.VMEM((NF, KP, NE), F32),
            pltpu.VMEM((AP * FP, NE), F32),
            pltpu.VMEM((AP * KP, NE), F32),
            pltpu.VMEM((2, AP * NM * FP, NE), F32),
            pltpu.VMEM((AP * FP, NE), F32),
            pltpu.VMEM((64 * FP, NE), F32),
            pltpu.VMEM((NM, AP, NE), F32),
            pltpu.VMEM((480, 512), BF16),
            pltpu.VMEM((512, NE), BF16),
            pltpu.VMEM((640, 512), BF16),
            pltpu.VMEM((240, 512), F32),
            pltpu.VMEM((2, NE, NE), F32),
            pltpu.VMEM((2, NE, NE), F32),
            pltpu.VMEM((2, NE, NE), F32),
            pltpu.VMEM((2, NE, NE), F32),
            pltpu.VMEM((NM * FP, 3 * KP), F32),
            pltpu.VMEM((NM * FP, 3 * KP), BF16),
            pltpu.VMEM((NM * FP, 3 * KP), BF16),
            pltpu.VMEM((256, NE), F32),
            pltpu.VMEM((n_hi, n_q * share, 256), F32),
            pltpu.VMEM((n_q - 1, n_hi, share, 256), F32),
            pltpu.VMEM((n_hi, share, 256), F32),
            pltpu.VMEM((n_hi - 1, share, 256), F32),
            pltpu.VMEM((NE, NE), F32),
            pltpu.VMEM((8, NE), F32),
            pltpu.VMEM((n_x - 1, 8, NE), F32),
            pltpu.VMEM((8, NE), F32),
            pltpu.VMEM((n_zl - 1, 8, NE), F32),
            pltpu.VMEM((NE, NE), F32),
            dma((5,)),
            dma((1,)),
            dma((2, 2)),
            dma((2, 2)),
            dma((n_q + n_hi - 2,)),
            dma((n_q + n_hi - 2,)),
            dma((n_x + n_zl - 2,)),
            dma((n_x + n_zl - 2,)),
        ],
        compiler_params=pltpu.CompilerParams(
            collective_id=0, has_side_effects=True, vmem_limit_bytes=40 * 2**20
        ),
    )(
        adjoint_state, forward_states, material, history_steps, history_changes,
        coupling, metric, face_normals, face_scale, face_neighbours, face_orientation,
        send_faces.reshape(1, -1), jnp.asarray(deriv_table()), jnp.asarray(lift_table()),
    )


def dims_of(mesh):
    n_shot, n_mesh = mesh.shape["shot"], mesh.shape["mesh"]
    n_x = 4 if n_mesh >= 16 else 2
    return 2, n_shot // 2, n_x, n_mesh // n_x


def solution(mesh):
    placed = (
        P("shot", None, None, "mesh"),
        P("shot", None, None, None, "mesh"),
        P(None, None, "mesh"),
        P(),
        P(None, None, "mesh"),
        P(None, None, "mesh"),
        P(None, "mesh"),
        P(None, "mesh"),
        P(None, "mesh"),
        P("mesh"),
        P(None, None, None, "mesh"),
        P(None, None, None, "mesh"),
    )
    return jax.shard_map(
        functools.partial(shards, dims_of(mesh)),
        mesh=mesh,
        in_specs=placed,
        out_specs=(P("shot", None, None, "mesh"), P(None, None, ("mesh", "shot"))),
        check_vma=False,
    )
```

```python
import functools
import math

import jax
import jax.numpy as jnp
import ml_dtypes
import numpy as np
from jax import lax
from jax.experimental import pallas as pl
from jax.experimental.pallas import tpu as pltpu
from jax.sharding import PartitionSpec as P

F32 = jnp.float32
BF16 = jnp.bfloat16
HIGH = lax.Precision.HIGHEST
STEP_SIZE = 0.02
MESH = pl.DeviceIdType.MESH

NF = 13
FP = 16
NB = 35
AP = 40
KP = 48
NFN = 15
NM = 6
NE = 128
HIST = 5


def invert_matrix(matrix):
    order_count = matrix.shape[0]
    working = np.concatenate([matrix * 1.0, np.eye(order_count)], axis=1)
    for column in range(order_count):
        pivot_row = column + int(np.argmax(np.abs(working[column:, column])))
        working[[column, pivot_row]] = working[[pivot_row, column]]
        working[column] = working[column] / working[column, column]
        for target in range(order_count):
            if target != column:
                working[target] = working[target] - working[target, column] * working[column]
    return working[:, order_count:]


def basis_tables():
    points = [
        (across, along, upward)
        for upward in range(5)
        for along in range(5 - upward)
        for across in range(5 - upward - along)
    ]
    exponents = np.array(points) * 1.0
    coords = exponents / 4.0
    vander = np.prod(coords[:, None, :] ** exponents[None, :, :], axis=2)
    inverse = invert_matrix(vander)
    derivs = []
    for direction_axis in range(3):
        lowered = np.maximum(exponents - np.eye(3)[direction_axis], 0.0)
        slopes = exponents[None, :, direction_axis] * np.prod(
            coords[:, None, :] ** lowered[None, :, :], axis=2
        )
        derivs.append(slopes @ inverse)
    moments = np.array(
        [
            [
                math.factorial(first[0] + second[0])
                * math.factorial(first[1] + second[1])
                * math.factorial(first[2] + second[2])
                / math.factorial(sum(first) + sum(second) + 3)
                for second in points
            ]
            for first in points
        ]
    )
    mass_matrix = inverse.T @ moments @ inverse
    lattice = [(across, along) for along in range(5) for across in range(5 - along)]
    lattice_powers = np.array(lattice) * 1.0
    face_vander = np.prod((lattice_powers / 4.0)[:, None, :] ** lattice_powers[None, :, :], axis=2)
    face_inverse = invert_matrix(face_vander)
    face_moments = np.array(
        [
            [
                math.factorial(first[0] + second[0])
                * math.factorial(first[1] + second[1])
                / math.factorial(sum(first) + sum(second) + 2)
                for second in lattice
            ]
            for first in lattice
        ]
    )
    face_mass = face_inverse.T @ face_moments @ face_inverse
    numbers = {point: number for number, point in enumerate(points)}
    face_points = [
        [(across, along, 0) for across, along in lattice],
        [(across, 0, along) for across, along in lattice],
        [(0, across, along) for across, along in lattice],
        [(across, along, 4 - across - along) for across, along in lattice],
    ]
    face_nodes = np.array(
        [[numbers[point] for point in listing] for listing in face_points], np.int32
    )
    mass_inverse = invert_matrix(mass_matrix)
    lift_tables = []
    for face_number in range(4):
        selector = np.eye(35)[face_nodes[face_number]]
        lift_tables.append(mass_inverse @ selector.T @ face_mass)
    orderings = [(0, 1, 2), (1, 2, 0), (2, 0, 1), (1, 0, 2), (0, 2, 1), (2, 1, 0)]
    lattice_numbers = {point: number for number, point in enumerate(lattice)}
    triples = [(across, along, 4 - across - along) for across, along in lattice]
    turn_nodes = np.array(
        [
            [lattice_numbers[triple[ordering[0]], triple[ordering[1]]] for triple in triples]
            for ordering in orderings
        ],
        np.int32,
    )
    return (
        np.stack(derivs).astype(np.float32),
        np.stack(lift_tables).astype(np.float32),
        face_nodes,
        turn_nodes,
    )


DERIVS, LIFTS, FACE_NODES, TURN = basis_tables()


def np_split(table):
    high = table.astype(ml_dtypes.bfloat16)
    low = (table - high.astype(np.float32)).astype(ml_dtypes.bfloat16)
    return np.concatenate([high, high, low], axis=1)


def deriv_table():
    table = np.zeros((128, KP), np.float32)
    for r in range(3):
        table[r * AP : r * AP + NB, :NB] = DERIVS[r]
    return np_split(table)


def lift_table():
    table = np.zeros((KP, 64), np.float32)
    for x in range(4):
        table[:NB, x * 16 : x * 16 + NFN] = LIFTS[x]
    return np_split(table)


def split(x):
    high = x.astype(BF16)
    low = (x - high.astype(F32)).astype(BF16)
    return high, low


def stack3(x):
    high, low = split(x)
    return jnp.concatenate([high, low, high], axis=0)


def mm(a, b):
    return jnp.dot(a, b, preferred_element_type=F32)


def grad_row(p):
    return (p // 3) * 128 + (p % 3) * AP


def body(
    dims,
    adj_hbm, fwd_hbm, mat_hbm, hs_hbm, hy_hbm,
    cpl_hbm, metric_hbm, normals_hbm, scale_hbm, nbr_hbm, orient_hbm, send_hbm, deriv3_hbm, lift3_hbm,
    fin_hbm, dir_ref,
    hist, fin, cpl, metric, normals, scale, nbr, orient, send, deriv3, lift3,
    lam_b, fwd_b, lam_a, spat, mixg, vol, flux, matp,
    trace, oh_send, oh_nbr, outer,
    msg_d, msg_u, got_d, got_u,
    ct32, ct_v, ct_g,
    grads, gt, rs_got, rs_mid, rs_last, prods, turned, hist_t,
    plane_src, plane_got, line_src, line_got, scal,
    load_sem, fin_sem, halo_send, halo_recv, rs_send, rs_recv, plane_send, plane_recv, line_send, line_recv,
):
    n_hi, n_q, n_x, n_zl = dims
    n_shot, n_mesh = n_hi * n_q, n_x * n_zl
    n_plane, n_line = n_q * n_x, n_hi * n_zl
    share = NE // n_shot
    s_id = lax.axis_index("shot")
    m_id = lax.axis_index("mesh")
    hi_id, q_id = s_id // n_q, s_id % n_q
    zl_id, x_id = m_id // n_x, m_id % n_x
    has_below = m_id > 0
    has_above = m_id < n_mesh - 1

    plane_peers, line_peers = [], []
    for k in range(1, n_plane):
        other = (q_id * n_x + x_id + k) % n_plane
        plane_peers.append({"shot": hi_id * n_q + other // n_x, "mesh": zl_id * n_x + other % n_x})
    for k in range(1, n_line):
        other = (hi_id * n_zl + zl_id + k) % n_line
        line_peers.append({"shot": (other // n_zl) * n_q + q_id, "mesh": (other % n_zl) * n_x + x_id})

    barrier = pltpu.get_barrier_semaphore()

    @pl.when(has_below)
    def _():
        pl.semaphore_signal(barrier, inc=1, device_id={"mesh": m_id - 1}, device_id_type=MESH)

    @pl.when(has_above)
    def _():
        pl.semaphore_signal(barrier, inc=1, device_id={"mesh": m_id + 1}, device_id_type=MESH)

    for peer in line_peers[::-1] + plane_peers:
        pl.semaphore_signal(barrier, inc=1, device_id=peer, device_id_type=MESH)

    for f in range(NF):
        lam_b[f, 32:KP, :] = jnp.zeros((KP - 32, NE), F32)
    pairs = [
        (adj_hbm.at[:, :, 0], lam_b.at[:, 0:NB]),
        (send_hbm, send),
        (deriv3_hbm, deriv3),
        (metric_hbm, metric),
        (cpl_hbm, cpl),
        (mat_hbm, matp.at[:, 0:NB]),
        (nbr_hbm, nbr),
        (orient_hbm, orient),
        (normals_hbm, normals),
        (scale_hbm, scale),
        (fwd_hbm.at[:, :, 0], fwd_b.at[0, :, 0:NB]),
        (lift3_hbm, lift3),
        (fwd_hbm.at[:, :, 1], fwd_b.at[1, :, 0:NB]),
        (hs_hbm, hist.at[0:HIST, :, 0:NB]),
        (hy_hbm, hist.at[HIST : 2 * HIST, :, 0:NB]),
    ]
    loads = [pltpu.make_async_copy(src, dst, load_sem.at[k]) for k, (src, dst) in enumerate(pairs)]
    loads[0].start()
    loads[1].start()
    matp[:, 32:AP, :] = jnp.zeros((NM, AP - 32, NE), F32)
    for t in range(2):
        for f in range(NF):
            fwd_b[t, f, 32:KP, :] = jnp.zeros((KP - 32, NE), F32)
    for k in range(2 * HIST):
        hist[k, :, 32:AP, :] = jnp.zeros((NM, AP - 32, NE), F32)
    for one in loads[2:]:
        one.start()

    lam_a[...] = jnp.zeros(lam_a.shape, F32)

    @pl.when(jnp.logical_not(has_below))
    def _():
        got_u[...] = jnp.zeros(got_u.shape, F32)

    @pl.when(jnp.logical_not(has_above))
    def _():
        got_d[...] = jnp.zeros(got_d.shape, F32)

    lane = lax.broadcasted_iota(jnp.int32, (FP, NE), 1)
    low_half = lane < 64

    def derivative(field):
        for first in range(0, NF, 2):
            group = range(first, min(first + 2, NF))
            out = mm(deriv3[...], jnp.concatenate([stack3(field[f]) for f in group], axis=1))
            for i, f in enumerate(group):
                slab = [out[r * AP : (r + 1) * AP, i * NE : (i + 1) * NE] for r in range(3)]
                for d in range(3):
                    s = metric[0, d : d + 1, :] * slab[0]
                    s = s + metric[1, d : d + 1, :] * slab[1]
                    s = s + metric[2, d : d + 1, :] * slab[2]
                    spat[pl.ds(d * FP + f, AP, stride=KP), :] = s

    def mixed(table, base):
        parts = []
        for j in range(8):
            at = pl.multiple_of((base + j) * KP, KP)
            parts.append(stack3(spat[pl.ds(at, KP), :]))
        return mm(table[...], jnp.concatenate(parts, axis=1))

    def volume():
        derivative(lam_b)

        def block(i, carry):
            base = pl.multiple_of(i * 8, 8)
            mix = mixed(ct_v, base)
            params = [matp[p, pl.ds(base, 8), :] for p in range(NM)]
            for j in range(8):
                acc = params[0][j : j + 1, :] * mix[0:FP, j * NE : (j + 1) * NE]
                for p in range(1, NM):
                    acc = acc + params[p][j : j + 1, :] * mix[p * FP : (p + 1) * FP, j * NE : (j + 1) * NE]
                vol[pl.ds(pl.multiple_of((base + j) * FP, FP), FP), :] = acc
            return carry

        lax.fori_loop(0, AP // 8, block, 0)

    def forward_mix(t):
        derivative(fwd_b.at[t])

        def block(i, carry):
            base = pl.multiple_of(i * 8, 8)
            mix = mixed(ct_g, base)
            for j in range(8):
                at = pl.multiple_of((base + j) * NM * FP, NM * FP)
                mixg[t, pl.ds(at, NM * FP), :] = mix[:, j * NE : (j + 1) * NE]
            return carry

        lax.fori_loop(0, AP // 8, block, 0)

    def times_lam(i, carry):
        lam = lam_a[pl.ds(pl.multiple_of(i * FP, FP), FP), :]
        for p in range(NM):
            at = pl.ds(pl.multiple_of(i * NM * FP + p * FP, FP), FP)
            mixg[0, at, :] = mixg[0, at, :] * lam
        return carry

    def kernel_sum(i, carry):
        base = pl.multiple_of(i * 8, 8)
        for p in range(NM):
            rows_out = []
            for j in range(8):
                lam = lam_a[pl.ds(pl.multiple_of((base + j) * FP, FP), FP), :]
                at = pl.ds(pl.multiple_of((base + j) * NM * FP + p * FP, FP), FP)
                both = mixg[0, at, :] + mixg[1, at, :] * lam
                rows_out.append(jnp.sum(both, axis=0, keepdims=True))
            at = pl.ds(pl.multiple_of(grad_row(p) + base, 8), 8)
            grads[at, :] = jnp.concatenate(rows_out, axis=0) * STEP_SIZE
        return carry

    def inner_of(n, x):
        at = int(FACE_NODES[x][n]) * FP
        return lam_a[at : at + FP, :]

    def halo_copies(t):
        down = pltpu.make_async_remote_copy(
            src_ref=msg_d.at[t], dst_ref=got_d.at[t], send_sem=halo_send.at[t, 0], recv_sem=halo_recv.at[t, 0],
            device_id={"mesh": m_id - 1}, device_id_type=MESH,
        )
        up = pltpu.make_async_remote_copy(
            src_ref=msg_u.at[t], dst_ref=got_u.at[t], send_sem=halo_send.at[t, 1], recv_sem=halo_recv.at[t, 1],
            device_id={"mesh": m_id + 1}, device_id_type=MESH,
        )
        return down, up

    def send_traces(t):
        for n in range(NFN):
            for x in range(4):
                high, low = split(inner_of(n, x))
                trace[n * FP : (n + 1) * FP, x * NE : (x + 1) * NE] = high
                trace[240 + n * FP : 240 + (n + 1) * FP, x * NE : (x + 1) * NE] = low
        both = mm(trace[...], oh_send[...])
        picked = both[0:240] + both[240:480]
        for j in range(8):
            first = picked[j * FP : (j + 1) * FP]
            if j < 7:
                second = picked[(j + 8) * FP : (j + 9) * FP]
            else:
                second = jnp.zeros((FP, NE), F32)
            msg_d[t, j * FP : (j + 1) * FP, :] = jnp.where(low_half, first, pltpu.roll(second, 64, 1))
            msg_u[t, j * FP : (j + 1) * FP, :] = jnp.where(low_half, pltpu.roll(first, 64, 1), second)
        if t == 0:
            n_wait = n_plane + n_line - 2
            pl.semaphore_wait(barrier, n_wait + has_below.astype(jnp.int32) + has_above.astype(jnp.int32))
        down, up = halo_copies(t)

        @pl.when(has_below)
        def _():
            down.start()

        @pl.when(has_above)
        def _():
            up.start()

    def gather_local():
        local = mm(trace[...], oh_nbr[0:512, :])
        outer[...] = local[0:240] + local[240:480]

    def surface(t):
        down, up = halo_copies(t)

        @pl.when(has_above)
        def _():
            down.wait_recv()

        @pl.when(has_below)
        def _():
            up.wait_recv()

        tops, bottoms = [], []
        for j in range(8):
            above = got_d[t, j * FP : (j + 1) * FP, :]
            below = got_u[t, j * FP : (j + 1) * FP, :]
            tops.append(jnp.where(low_half, below, pltpu.roll(above, 64, 1)))
            bottoms.append(jnp.where(low_half, pltpu.roll(below, 64, 1), above))
        ghosts = jnp.concatenate(tops + bottoms[:7], axis=0)
        high, low = split(ghosts)
        part = mm(jnp.concatenate([high, low], axis=0), oh_nbr[512:640, :])
        outer[...] = outer[...] + (part[0:240] + part[240:480])

        turns = [jnp.broadcast_to(orient[x : x + 1, :], (FP, NE)) for x in range(4)]
        halves = [0.5 * scale[x : x + 1, :] for x in range(4)]
        for n in range(NFN):
            sources = {}
            for o in range(6):
                sources.setdefault(int(TURN[o][n]), []).append(o)
            sources = list(sources.items())
            jumps, weighted = [], []
            for x in range(4):
                at = sources[0][0] * FP
                value = outer[at : at + FP, x * NE : (x + 1) * NE]
                for node, options in sources[1:]:
                    mask = turns[x] == options[0]
                    for o in options[1:]:
                        mask = mask | (turns[x] == o)
                    value = jnp.where(mask, outer[node * FP : (node + 1) * FP, x * NE : (x + 1) * NE], value)
                jump = value - inner_of(n, x)
                jumps.append(jump)
                weighted.append(
                    stack3(jnp.concatenate([normals[d, x : x + 1, :] * jump for d in range(3)], axis=0))
                )
            mix = mm(ct_v[...], jnp.concatenate(weighted, axis=1))
            for x in range(4):
                node = int(FACE_NODES[x][n])
                acc = jumps[x]
                for p in range(NM):
                    acc = acc + matp[p, node : node + 1, :] * mix[p * FP : (p + 1) * FP, x * NE : (x + 1) * NE]
                at = (x * 16 + n) * FP
                flux[at : at + FP, :] = acc * halves[x]

        for first in range(0, NF, 2):
            group = range(first, min(first + 2, NF))
            rhs = [stack3(flux[pl.ds(g, 64, stride=FP), :]) for g in group]
            out = mm(lift3[...], jnp.concatenate(rhs, axis=1))
            for i, g in enumerate(group):
                change = out[0:AP, i * NE : (i + 1) * NE] + vol[pl.ds(g, AP, stride=FP), :]
                new = lam_b[g, 0:AP, :] + STEP_SIZE * change
                if t == 0:
                    lam_b[g, 0:AP, :] = new
                else:
                    fin[g] = new
                lam_a[pl.ds(g, AP, stride=FP), :] = new

    yy_row = {}
    for i in range(HIST):
        for j in range(i, HIST):
            yy_row[i, j] = yy_row[j, i] = 25 + len([k for k in yy_row if k[0] <= k[1]])

    def dot_rows(i, j):
        acc = hist[i, 0] * hist[j, 0]
        for p in range(1, NM):
            acc = acc + hist[i, p] * hist[j, p]
        return jnp.sum(acc, axis=0, keepdims=True)

    def history():
        prods[...] = jnp.zeros(prods.shape, F32)
        for i in range(HIST):
            for j in range(HIST):
                row = i * HIST + j
                prods[row : row + 1, :] = dot_rows(i, HIST + j)
                if j >= i:
                    row = yy_row[i, j]
                    prods[row : row + 1, :] = dot_rows(HIST + i, HIST + j)

    def selections():
        for k in (6, 7):
            loads[k].wait()
        rows_n = lax.broadcasted_iota(jnp.int32, (640, NE), 0)
        for x in range(4):
            oh_nbr[:, x * NE : (x + 1) * NE] = jnp.where(rows_n == nbr[x : x + 1, :], 1.0, 0.0).astype(BF16)

    def tables():
        loads[4].wait()
        ct32[...] = jnp.zeros(ct32.shape, F32)
        cols = lax.broadcasted_iota(jnp.int32, (NF, 3 * KP), 1)
        rows = lax.broadcasted_iota(jnp.int32, (NF, 3 * KP), 0)
        places = [
            jnp.where(
                (cols == d * FP + rows) | (cols == KP + d * FP + rows) | (cols == 2 * KP + d * FP + rows), 1.0, 0.0
            )
            for d in range(3)
        ]
        table_cols = lax.broadcasted_iota(jnp.int32, (NM * FP, 3 * KP), 1)
        for side, dst in ((0, ct_v), (1, ct_g)):
            for p in range(NM):
                total = None
                for d in range(3):
                    part = lax.dot_general(
                        cpl[d, p], places[d], (((side,), (0,)), ((), ())), precision=HIGH, preferred_element_type=F32
                    )
                    total = part if total is None else total + part
                ct32[p * FP : p * FP + NF, :] = total
            whole = ct32[...]
            high = whole.astype(BF16)
            low = whole - high.astype(F32)
            dst[...] = jnp.where(table_cols < 2 * KP, high.astype(F32), low).astype(BF16)

    def clear(i, carry):
        spat[pl.ds(pl.multiple_of(i * KP, KP), KP), :] = jnp.zeros((KP, NE), F32)
        return carry

    loads[1].wait()
    rows_s = lax.broadcasted_iota(jnp.int32, (512, NE), 0)
    oh_send[...] = jnp.where(rows_s == send[...], 1.0, 0.0).astype(BF16)
    loads[0].wait()
    for f in range(NF):
        lam_a[pl.ds(f, AP, stride=FP), :] = lam_b[f, 0:AP, :]
    send_traces(0)
    tables()
    lax.fori_loop(0, AP, clear, 0)
    for x in range(4):
        flux[(x * 16 + 15) * FP : (x * 16 + 16) * FP, :] = jnp.zeros((FP, NE), F32)
    for k in (2, 3, 5):
        loads[k].wait()
    volume()
    selections()
    gather_local()
    loads[10].wait()
    forward_mix(0)
    for k in (8, 9, 11):
        loads[k].wait()
    surface(0)
    send_traces(1)
    gather_local()
    volume()
    loads[12].wait()
    forward_mix(1)
    lax.fori_loop(0, AP, times_lam, 0)
    for k in (13, 14):
        loads[k].wait()
    history()
    gram = jnp.sum(jnp.transpose(prods[...]), axis=0, keepdims=True) * (1.0 / n_shot)
    surface(1)

    lax.fori_loop(0, AP // 8, kernel_sum, 0)
    for k in range(2 * HIST):
        acc = hist[k, 0] * grads[0:AP, :]
        for p in range(1, NM):
            acc = acc + hist[k, p] * grads[grad_row(p) : grad_row(p) + AP, :]
        row = 120 + (k // HIST) * 128 + k % HIST
        grads[row : row + 1, :] = jnp.sum(acc, axis=0, keepdims=True)
    left = jnp.transpose(grads[0:128, :])
    right = jnp.transpose(grads[128:256, :])
    row_lane = lax.broadcasted_iota(jnp.int32, (1, NE), 1)
    vector = jnp.where(
        row_lane >= 120,
        jnp.sum(left, axis=0, keepdims=True),
        jnp.where(row_lane >= 112, pltpu.roll(jnp.sum(right, axis=0, keepdims=True), 120, 1), gram),
    )
    plane_src[...] = vector
    planes = [
        pltpu.make_async_remote_copy(
            src_ref=plane_src, dst_ref=plane_got.at[k], send_sem=plane_send.at[k], recv_sem=plane_recv.at[k],
            device_id=peer, device_id_type=MESH,
        )
        for k, peer in enumerate(plane_peers)
    ]
    for one in planes:
        one.start()

    half = n_q * share
    for h in range(n_hi):
        gt[h, :, 0:128] = left[h * half : (h + 1) * half]
        gt[h, :, 128:256] = right[h * half : (h + 1) * half]
    firsts = []
    for o in range(1, n_q):
        peer_q = (q_id + o) % n_q
        firsts.append(
            pltpu.make_async_remote_copy(
                src_ref=gt.at[:, pl.ds(pl.multiple_of(peer_q * share, share), share), :],
                dst_ref=rs_got.at[o - 1],
                send_sem=rs_send.at[o - 1], recv_sem=rs_recv.at[o - 1],
                device_id={"shot": hi_id * n_q + peer_q}, device_id_type=MESH,
            )
        )
    for one in firsts:
        one.start()
    final_out = pltpu.make_async_copy(fin.at[:, 0:NB], fin_hbm.at[:, :, 0], fin_sem.at[0])
    final_out.start()

    def turn_history(k, carry):
        for side in range(2):
            block = [hist[k, side * 3 + p] for p in range(3)] + [jnp.zeros((8, NE), F32)]
            turned[:, side * 128 : (side + 1) * 128] = jnp.transpose(jnp.concatenate(block, axis=0))
        hist_t[k] = turned[pl.ds(pl.multiple_of(s_id * share, share), share), :]
        return carry

    lax.fori_loop(0, 2 * HIST, turn_history, 0)

    mine = gt[:, pl.ds(pl.multiple_of(q_id * share, share), share), :]
    for o, one in enumerate(firsts):
        one.wait_recv()
        mine = mine + rs_got[o]
    rs_mid[...] = mine
    seconds = []
    for o in range(1, n_hi):
        seconds.append(
            pltpu.make_async_remote_copy(
                src_ref=rs_mid.at[(hi_id + o) % n_hi],
                dst_ref=rs_last.at[o - 1],
                send_sem=rs_send.at[n_q - 2 + o], recv_sem=rs_recv.at[n_q - 2 + o],
                device_id={"shot": ((hi_id + o) % n_hi) * n_q + q_id}, device_id_type=MESH,
            )
        )
    for one in seconds:
        one.start()

    def collected(value, copies, got):
        sums = [value, None, None, None]
        for k, one in enumerate(copies):
            one.wait_recv()
            at = (k + 1) % 4
            sums[at] = got[k] if sums[at] is None else sums[at] + got[k]
        sums = [one for one in sums if one is not None]
        while len(sums) > 1:
            sums = sums[2:] + [sums[0] + sums[1]]
        return sums[0]

    vector = collected(vector, planes, plane_got)
    line_src[...] = vector
    lines = [
        pltpu.make_async_remote_copy(
            src_ref=line_src, dst_ref=line_got.at[k], send_sem=line_send.at[k], recv_sem=line_recv.at[k],
            device_id=peer, device_id_type=MESH,
        )
        for k, peer in enumerate(line_peers)
    ]
    for one in lines:
        one.start()
    total = rs_mid[hi_id]
    for t in range(2):
        down, up = halo_copies(t)

        @pl.when(has_below)
        def _():
            down.wait_send()

        @pl.when(has_above)
        def _():
            up.wait_send()

    for one in planes + firsts:
        one.wait_send()
    final_out.wait()
    for o, one in enumerate(seconds):
        one.wait_recv()
        total = total + rs_last[o]
    vector = collected(vector, lines, line_got)

    scal[...] = jnp.transpose(jnp.broadcast_to(vector, (NE, NE)))

    def num(k):
        return scal[k : k + 1, :]

    def sy(i, j):
        return num(i * HIST + j)

    over = [1.0 / sy(i, i) for i in range(HIST)]
    gamma = sy(HIST - 1, HIST - 1) / num(yy_row[HIST - 1, HIST - 1])
    alphas = [None] * HIST
    for i in reversed(range(HIST)):
        value = num(120 + i)
        for j in reversed(range(i + 1, HIST)):
            value = value - alphas[j] * sy(i, j)
        alphas[i] = value * over[i]
    rest = []
    for i in range(HIST):
        value = num(112 + i)
        for j in range(HIST):
            value = value - alphas[j] * num(yy_row[i, j])
        value = gamma * value
        for j in range(i):
            value = value + rest[j] * sy(j, i)
        rest.append(alphas[i] - value * over[i])

    sides = []
    for side in range(2):
        lanes = slice(side * 128, (side + 1) * 128)
        acc = -total[:, lanes]
        for i in range(HIST):
            acc = acc + alphas[i] * hist_t[HIST + i, :, lanes]
        acc = gamma * acc
        for i in range(HIST):
            acc = acc - rest[i] * hist_t[i, :, lanes]
        sides.append(acc)
    for p in range(NM):
        at = (p % 3) * AP
        dir_ref[p] = sides[p // 3][:, at : at + NB]

    for one in seconds + lines:
        one.wait_send()


def shards(
    dims,
    adjoint_state,
    forward_states,
    material,
    coupling,
    metric,
    face_normals,
    face_scale,
    face_neighbours,
    face_orientation,
    send_faces,
    history_steps,
    history_changes,
):
    n_hi, n_q, n_x, n_zl = dims
    share = NE // (n_hi * n_q)
    n_plane, n_line = n_q * n_x, n_hi * n_zl
    vmem = pl.BlockSpec(memory_space=pltpu.VMEM)
    hbm = pl.BlockSpec(memory_space=pltpu.HBM)
    dma = pltpu.SemaphoreType.DMA
    i32 = jnp.int32
    final, direction = pl.pallas_call(
        functools.partial(body, dims),
        out_shape=(
            jax.ShapeDtypeStruct((NF, NB, 1, NE), F32),
            jax.ShapeDtypeStruct((NM, share, NB), F32),
        ),
        in_specs=[hbm] * 14,
        out_specs=(hbm, vmem),
        scratch_shapes=[
            pltpu.VMEM((2 * HIST, NM, AP, NE), F32),
            pltpu.VMEM((NF, AP, NE), F32),
            pltpu.VMEM((3, NM, NF, NF), F32),
            pltpu.VMEM((3, 3, NE), F32),
            pltpu.VMEM((3, 4, NE), F32),
            pltpu.VMEM((4, NE), F32),
            pltpu.VMEM((4, NE), i32),
            pltpu.VMEM((4, NE), i32),
            pltpu.VMEM((1, NE), i32),
            pltpu.VMEM((128, 3 * KP), BF16),
            pltpu.VMEM((KP, 192), BF16),
            pltpu.VMEM((NF, KP, NE), F32),
            pltpu.VMEM((2, NF, KP, NE), F32),
            pltpu.VMEM((AP * FP, NE), F32),
            pltpu.VMEM((AP * KP, NE), F32),
            pltpu.VMEM((2, AP * NM * FP, NE), F32),
            pltpu.VMEM((AP * FP, NE), F32),
            pltpu.VMEM((64 * FP, NE), F32),
            pltpu.VMEM((NM, AP, NE), F32),
            pltpu.VMEM((480, 512), BF16),
            pltpu.VMEM((512, NE), BF16),
            pltpu.VMEM((640, 512), BF16),
            pltpu.VMEM((240, 512), F32),
            pltpu.VMEM((2, NE, NE), F32),
            pltpu.VMEM((2, NE, NE), F32),
            pltpu.VMEM((2, NE, NE), F32),
            pltpu.VMEM((2, NE, NE), F32),
            pltpu.VMEM((NM * FP, 3 * KP), F32),
            pltpu.VMEM((NM * FP, 3 * KP), BF16),
            pltpu.VMEM((NM * FP, 3 * KP), BF16),
            pltpu.VMEM((256, NE), F32),
            pltpu.VMEM((n_hi, n_q * share, 256), F32),
            pltpu.VMEM((n_q - 1, n_hi, share, 256), F32),
            pltpu.VMEM((n_hi, share, 256), F32),
            pltpu.VMEM((n_hi - 1, share, 256), F32),
            pltpu.VMEM((NE, NE), F32),
            pltpu.VMEM((NE, 256), F32),
            pltpu.VMEM((2 * HIST, share, 256), F32),
            pltpu.VMEM((1, NE), F32),
            pltpu.VMEM((n_plane - 1, 1, NE), F32),
            pltpu.VMEM((1, NE), F32),
            pltpu.VMEM((n_line - 1, 1, NE), F32),
            pltpu.VMEM((NE, NE), F32),
            dma((15,)),
            dma((1,)),
            dma((2, 2)),
            dma((2, 2)),
            dma((n_q + n_hi - 2,)),
            dma((n_q + n_hi - 2,)),
            dma((n_plane - 1,)),
            dma((n_plane - 1,)),
            dma((n_line - 1,)),
            dma((n_line - 1,)),
        ],
        compiler_params=pltpu.CompilerParams(
            collective_id=0, has_side_effects=True, vmem_limit_bytes=63 * 2**20
        ),
    )(
        jnp.transpose(adjoint_state, (1, 2, 0, 3)), jnp.transpose(forward_states[0], (1, 2, 0, 3)),
        material, history_steps, history_changes,
        coupling, metric, face_normals, face_scale, face_neighbours, face_orientation,
        send_faces.reshape(1, -1), jnp.asarray(deriv_table()), jnp.asarray(lift_table()),
    )
    return jnp.transpose(final, (2, 0, 1, 3)), jnp.transpose(direction, (0, 2, 1))


def dims_of(mesh):
    n_shot, n_mesh = mesh.shape["shot"], mesh.shape["mesh"]
    n_x = 4 if n_mesh >= 16 else 2
    return 2, n_shot // 2, n_x, n_mesh // n_x


def solution(mesh):
    placed = (
        P("shot", None, None, "mesh"),
        P("shot", None, None, None, "mesh"),
        P(None, None, "mesh"),
        P(),
        P(None, None, "mesh"),
        P(None, None, "mesh"),
        P(None, "mesh"),
        P(None, "mesh"),
        P(None, "mesh"),
        P("mesh"),
        P(None, None, None, "mesh"),
        P(None, None, None, "mesh"),
    )
    return jax.shard_map(
        functools.partial(shards, dims_of(mesh)),
        mesh=mesh,
        in_specs=placed,
        out_specs=(P("shot", None, None, "mesh"), P(None, None, ("mesh", "shot"))),
        check_vma=False,
    )
```

```python
import functools
import math

import jax
import jax.numpy as jnp
import ml_dtypes
import numpy as np
from jax import lax
from jax.experimental import pallas as pl
from jax.experimental.pallas import tpu as pltpu
from jax.sharding import PartitionSpec as P

F32 = jnp.float32
BF16 = jnp.bfloat16
HIGH = lax.Precision.HIGHEST
STEP_SIZE = 0.02
MESH = pl.DeviceIdType.MESH

NF = 13
FP = 16
NB = 35
AP = 40
KP = 48
NFN = 15
NM = 6
NE = 128
HIST = 5


def invert_matrix(matrix):
    order_count = matrix.shape[0]
    working = np.concatenate([matrix * 1.0, np.eye(order_count)], axis=1)
    for column in range(order_count):
        pivot_row = column + int(np.argmax(np.abs(working[column:, column])))
        working[[column, pivot_row]] = working[[pivot_row, column]]
        working[column] = working[column] / working[column, column]
        for target in range(order_count):
            if target != column:
                working[target] = working[target] - working[target, column] * working[column]
    return working[:, order_count:]


def basis_tables():
    points = [
        (across, along, upward)
        for upward in range(5)
        for along in range(5 - upward)
        for across in range(5 - upward - along)
    ]
    exponents = np.array(points) * 1.0
    coords = exponents / 4.0
    vander = np.prod(coords[:, None, :] ** exponents[None, :, :], axis=2)
    inverse = invert_matrix(vander)
    derivs = []
    for direction_axis in range(3):
        lowered = np.maximum(exponents - np.eye(3)[direction_axis], 0.0)
        slopes = exponents[None, :, direction_axis] * np.prod(
            coords[:, None, :] ** lowered[None, :, :], axis=2
        )
        derivs.append(slopes @ inverse)
    moments = np.array(
        [
            [
                math.factorial(first[0] + second[0])
                * math.factorial(first[1] + second[1])
                * math.factorial(first[2] + second[2])
                / math.factorial(sum(first) + sum(second) + 3)
                for second in points
            ]
            for first in points
        ]
    )
    mass_matrix = inverse.T @ moments @ inverse
    lattice = [(across, along) for along in range(5) for across in range(5 - along)]
    lattice_powers = np.array(lattice) * 1.0
    face_vander = np.prod((lattice_powers / 4.0)[:, None, :] ** lattice_powers[None, :, :], axis=2)
    face_inverse = invert_matrix(face_vander)
    face_moments = np.array(
        [
            [
                math.factorial(first[0] + second[0])
                * math.factorial(first[1] + second[1])
                / math.factorial(sum(first) + sum(second) + 2)
                for second in lattice
            ]
            for first in lattice
        ]
    )
    face_mass = face_inverse.T @ face_moments @ face_inverse
    numbers = {point: number for number, point in enumerate(points)}
    face_points = [
        [(across, along, 0) for across, along in lattice],
        [(across, 0, along) for across, along in lattice],
        [(0, across, along) for across, along in lattice],
        [(across, along, 4 - across - along) for across, along in lattice],
    ]
    face_nodes = np.array(
        [[numbers[point] for point in listing] for listing in face_points], np.int32
    )
    mass_inverse = invert_matrix(mass_matrix)
    lift_tables = []
    for face_number in range(4):
        selector = np.eye(35)[face_nodes[face_number]]
        lift_tables.append(mass_inverse @ selector.T @ face_mass)
    orderings = [(0, 1, 2), (1, 2, 0), (2, 0, 1), (1, 0, 2), (0, 2, 1), (2, 1, 0)]
    lattice_numbers = {point: number for number, point in enumerate(lattice)}
    triples = [(across, along, 4 - across - along) for across, along in lattice]
    turn_nodes = np.array(
        [
            [lattice_numbers[triple[ordering[0]], triple[ordering[1]]] for triple in triples]
            for ordering in orderings
        ],
        np.int32,
    )
    return (
        np.stack(derivs).astype(np.float32),
        np.stack(lift_tables).astype(np.float32),
        face_nodes,
        turn_nodes,
    )


DERIVS, LIFTS, FACE_NODES, TURN = basis_tables()


def np_split(table):
    high = table.astype(ml_dtypes.bfloat16)
    low = (table - high.astype(np.float32)).astype(ml_dtypes.bfloat16)
    return np.concatenate([high, high, low], axis=1)


def deriv_table():
    table = np.zeros((128, KP), np.float32)
    for r in range(3):
        table[r * AP : r * AP + NB, :NB] = DERIVS[r]
    return np_split(table)


def lift_table():
    table = np.zeros((KP, 64), np.float32)
    for x in range(4):
        table[:NB, x * 16 : x * 16 + NFN] = LIFTS[x]
    return np_split(table)


def split(x):
    high = x.astype(BF16)
    low = (x - high.astype(F32)).astype(BF16)
    return high, low


def stack3(x):
    high, low = split(x)
    return jnp.concatenate([high, low, high], axis=0)


def mm(a, b):
    return jnp.dot(a, b, preferred_element_type=F32)


def grad_row(p):
    return (p // 3) * 128 + (p % 3) * AP


def body(
    dims,
    adj_hbm, fwd_hbm, mat_hbm, hs_hbm, hy_hbm,
    cpl_hbm, metric_hbm, normals_hbm, scale_hbm, nbr_hbm, orient_hbm, send_hbm, deriv3_hbm, lift3_hbm,
    fin_hbm, dir_ref,
    hist, fin, cpl, metric, normals, scale, nbr, orient, send, deriv3, lift3,
    lam_b, fwd_b, lam_a, spat, mixg, vol, flux, matp,
    trace, oh_send, oh_nbr, outer,
    msg_d, msg_u, got_d, got_u,
    ct32, ct_v, ct_g,
    grads, gt, rs_got, rs_mid, rs_last, prods, turned, hist_t,
    plane_src, plane_got, line_src, line_got, scal,
    load_sem, fin_sem, halo_send, halo_recv, rs_send, rs_recv, known, plane_send, plane_recv, line_send, line_recv,
):
    n_hi, n_q, n_x, n_zl = dims
    n_shot, n_mesh = n_hi * n_q, n_x * n_zl
    n_plane, n_line = n_q * n_x, n_hi * n_zl
    share = NE // n_shot
    s_id = lax.axis_index("shot")
    m_id = lax.axis_index("mesh")
    hi_id, q_id = s_id // n_q, s_id % n_q
    zl_id, x_id = m_id // n_x, m_id % n_x
    has_below = m_id > 0
    has_above = m_id < n_mesh - 1

    plane_peers, line_peers = [], []
    for k in range(1, n_plane):
        other = (q_id * n_x + x_id + k) % n_plane
        plane_peers.append({"shot": hi_id * n_q + other // n_x, "mesh": zl_id * n_x + other % n_x})
    for k in range(1, n_line):
        other = (hi_id * n_zl + zl_id + k) % n_line
        line_peers.append({"shot": (other // n_zl) * n_q + q_id, "mesh": (other % n_zl) * n_x + x_id})

    barrier = pltpu.get_barrier_semaphore()

    @pl.when(has_below)
    def _():
        pl.semaphore_signal(barrier, inc=1, device_id={"mesh": m_id - 1}, device_id_type=MESH)

    @pl.when(has_above)
    def _():
        pl.semaphore_signal(barrier, inc=1, device_id={"mesh": m_id + 1}, device_id_type=MESH)

    def at_plane(step_x, step_q, flip):
        y_id, c_id = q_id // 2, q_id % 2
        other_q = ((y_id + step_q) % (n_q // 2)) * 2 + (c_id + flip) % 2
        return {"shot": hi_id * n_q + other_q, "mesh": zl_id * n_x + (x_id + step_x) % n_x}

    def at_line(step):
        return line_peers[step % n_line - 1]

    core = at_plane(0, 0, 1)
    rounds = [
        [core, at_plane(1, 0, 0), at_plane(n_x - 1, 0, 0), at_plane(0, 1, 0), at_plane(0, n_q // 2 - 1, 0), at_line(1), at_line(-1)],
        [at_plane(2, 0, 0), at_plane(0, 2, 0), at_line(2), at_line(-2)],
        [core, at_line(4), at_line(-4)],
    ]
    for peer in rounds[0]:
        pl.semaphore_signal(barrier, inc=1, device_id=peer, device_id_type=MESH)

    def tell(k):
        for peer in rounds[k]:
            pl.semaphore_signal(known.at[k], inc=1, device_id=peer, device_id_type=MESH)

    def hear(k):
        pl.semaphore_wait(known.at[k], len(rounds[k]))

    for f in range(NF):
        lam_b[f, 32:KP, :] = jnp.zeros((KP - 32, NE), F32)
    pairs = [
        (adj_hbm.at[:, :, 0], lam_b.at[:, 0:NB]),
        (send_hbm, send),
        (deriv3_hbm, deriv3),
        (metric_hbm, metric),
        (cpl_hbm, cpl),
        (mat_hbm, matp.at[:, 0:NB]),
        (nbr_hbm, nbr),
        (orient_hbm, orient),
        (normals_hbm, normals),
        (scale_hbm, scale),
        (fwd_hbm.at[:, :, 0], fwd_b.at[0, :, 0:NB]),
        (lift3_hbm, lift3),
        (fwd_hbm.at[:, :, 1], fwd_b.at[1, :, 0:NB]),
        (hs_hbm, hist.at[0:HIST, :, 0:NB]),
        (hy_hbm, hist.at[HIST : 2 * HIST, :, 0:NB]),
    ]
    loads = [pltpu.make_async_copy(src, dst, load_sem.at[k]) for k, (src, dst) in enumerate(pairs)]
    loads[0].start()
    loads[1].start()
    matp[:, 32:AP, :] = jnp.zeros((NM, AP - 32, NE), F32)
    for t in range(2):
        for f in range(NF):
            fwd_b[t, f, 32:KP, :] = jnp.zeros((KP - 32, NE), F32)
    for k in range(2 * HIST):
        hist[k, :, 32:AP, :] = jnp.zeros((NM, AP - 32, NE), F32)
    for one in loads[2:]:
        one.start()

    lam_a[...] = jnp.zeros(lam_a.shape, F32)

    @pl.when(jnp.logical_not(has_below))
    def _():
        got_u[...] = jnp.zeros(got_u.shape, F32)

    @pl.when(jnp.logical_not(has_above))
    def _():
        got_d[...] = jnp.zeros(got_d.shape, F32)

    lane = lax.broadcasted_iota(jnp.int32, (FP, NE), 1)
    low_half = lane < 64

    def derivative(field):
        for first in range(0, NF, 2):
            group = range(first, min(first + 2, NF))
            out = mm(deriv3[...], jnp.concatenate([stack3(field[f]) for f in group], axis=1))
            for i, f in enumerate(group):
                slab = [out[r * AP : (r + 1) * AP, i * NE : (i + 1) * NE] for r in range(3)]
                for d in range(3):
                    s = metric[0, d : d + 1, :] * slab[0]
                    s = s + metric[1, d : d + 1, :] * slab[1]
                    s = s + metric[2, d : d + 1, :] * slab[2]
                    spat[pl.ds(d * FP + f, AP, stride=KP), :] = s

    def mixed(table, base):
        parts = []
        for j in range(8):
            at = pl.multiple_of((base + j) * KP, KP)
            parts.append(stack3(spat[pl.ds(at, KP), :]))
        return mm(table[...], jnp.concatenate(parts, axis=1))

    def volume():
        derivative(lam_b)

        def block(i, carry):
            base = pl.multiple_of(i * 8, 8)
            mix = mixed(ct_v, base)
            params = [matp[p, pl.ds(base, 8), :] for p in range(NM)]
            for j in range(8):
                acc = params[0][j : j + 1, :] * mix[0:FP, j * NE : (j + 1) * NE]
                for p in range(1, NM):
                    acc = acc + params[p][j : j + 1, :] * mix[p * FP : (p + 1) * FP, j * NE : (j + 1) * NE]
                vol[pl.ds(pl.multiple_of((base + j) * FP, FP), FP), :] = acc
            return carry

        lax.fori_loop(0, AP // 8, block, 0)

    def forward_mix(t):
        derivative(fwd_b.at[t])

        def block(i, carry):
            base = pl.multiple_of(i * 8, 8)
            mix = mixed(ct_g, base)
            for j in range(8):
                at = pl.multiple_of((base + j) * NM * FP, NM * FP)
                mixg[t, pl.ds(at, NM * FP), :] = mix[:, j * NE : (j + 1) * NE]
            return carry

        lax.fori_loop(0, AP // 8, block, 0)

    def times_lam(i, carry):
        lam = lam_a[pl.ds(pl.multiple_of(i * FP, FP), FP), :]
        for p in range(NM):
            at = pl.ds(pl.multiple_of(i * NM * FP + p * FP, FP), FP)
            mixg[0, at, :] = mixg[0, at, :] * lam
        return carry

    def kernel_sum(i, carry):
        base = pl.multiple_of(i * 8, 8)
        for p in range(NM):
            rows_out = []
            for j in range(8):
                lam = lam_a[pl.ds(pl.multiple_of((base + j) * FP, FP), FP), :]
                at = pl.ds(pl.multiple_of((base + j) * NM * FP + p * FP, FP), FP)
                both = mixg[0, at, :] + mixg[1, at, :] * lam
                rows_out.append(jnp.sum(both, axis=0, keepdims=True))
            at = pl.ds(pl.multiple_of(grad_row(p) + base, 8), 8)
            grads[at, :] = jnp.concatenate(rows_out, axis=0) * STEP_SIZE
        return carry

    def inner_of(n, x):
        at = int(FACE_NODES[x][n]) * FP
        return lam_a[at : at + FP, :]

    def halo_copies(t):
        down = pltpu.make_async_remote_copy(
            src_ref=msg_d.at[t], dst_ref=got_d.at[t], send_sem=halo_send.at[t, 0], recv_sem=halo_recv.at[t, 0],
            device_id={"mesh": m_id - 1}, device_id_type=MESH,
        )
        up = pltpu.make_async_remote_copy(
            src_ref=msg_u.at[t], dst_ref=got_u.at[t], send_sem=halo_send.at[t, 1], recv_sem=halo_recv.at[t, 1],
            device_id={"mesh": m_id + 1}, device_id_type=MESH,
        )
        return down, up

    def send_traces(t):
        for n in range(NFN):
            for x in range(4):
                high, low = split(inner_of(n, x))
                trace[n * FP : (n + 1) * FP, x * NE : (x + 1) * NE] = high
                trace[240 + n * FP : 240 + (n + 1) * FP, x * NE : (x + 1) * NE] = low
        both = mm(trace[...], oh_send[...])
        picked = both[0:240] + both[240:480]
        for j in range(8):
            first = picked[j * FP : (j + 1) * FP]
            if j < 7:
                second = picked[(j + 8) * FP : (j + 9) * FP]
            else:
                second = jnp.zeros((FP, NE), F32)
            msg_d[t, j * FP : (j + 1) * FP, :] = jnp.where(low_half, first, pltpu.roll(second, 64, 1))
            msg_u[t, j * FP : (j + 1) * FP, :] = jnp.where(low_half, pltpu.roll(first, 64, 1), second)
        if t == 0:
            n_wait = len(rounds[0])
            pl.semaphore_wait(barrier, n_wait + has_below.astype(jnp.int32) + has_above.astype(jnp.int32))
        down, up = halo_copies(t)

        @pl.when(has_below)
        def _():
            down.start()

        @pl.when(has_above)
        def _():
            up.start()

        if t == 0:
            tell(0)

    def gather_local():
        local = mm(trace[...], oh_nbr[0:512, :])
        outer[...] = local[0:240] + local[240:480]

    def surface(t):
        down, up = halo_copies(t)

        @pl.when(has_above)
        def _():
            down.wait_recv()

        @pl.when(has_below)
        def _():
            up.wait_recv()

        tops, bottoms = [], []
        for j in range(8):
            above = got_d[t, j * FP : (j + 1) * FP, :]
            below = got_u[t, j * FP : (j + 1) * FP, :]
            tops.append(jnp.where(low_half, below, pltpu.roll(above, 64, 1)))
            bottoms.append(jnp.where(low_half, pltpu.roll(below, 64, 1), above))
        ghosts = jnp.concatenate(tops + bottoms[:7], axis=0)
        high, low = split(ghosts)
        part = mm(jnp.concatenate([high, low], axis=0), oh_nbr[512:640, :])
        outer[...] = outer[...] + (part[0:240] + part[240:480])

        turns = [jnp.broadcast_to(orient[x : x + 1, :], (FP, NE)) for x in range(4)]
        halves = [0.5 * scale[x : x + 1, :] for x in range(4)]
        for n in range(NFN):
            sources = {}
            for o in range(6):
                sources.setdefault(int(TURN[o][n]), []).append(o)
            sources = list(sources.items())
            jumps, weighted = [], []
            for x in range(4):
                at = sources[0][0] * FP
                value = outer[at : at + FP, x * NE : (x + 1) * NE]
                for node, options in sources[1:]:
                    mask = turns[x] == options[0]
                    for o in options[1:]:
                        mask = mask | (turns[x] == o)
                    value = jnp.where(mask, outer[node * FP : (node + 1) * FP, x * NE : (x + 1) * NE], value)
                jump = value - inner_of(n, x)
                jumps.append(jump)
                weighted.append(
                    stack3(jnp.concatenate([normals[d, x : x + 1, :] * jump for d in range(3)], axis=0))
                )
            mix = mm(ct_v[...], jnp.concatenate(weighted, axis=1))
            for x in range(4):
                node = int(FACE_NODES[x][n])
                acc = jumps[x]
                for p in range(NM):
                    acc = acc + matp[p, node : node + 1, :] * mix[p * FP : (p + 1) * FP, x * NE : (x + 1) * NE]
                at = (x * 16 + n) * FP
                flux[at : at + FP, :] = acc * halves[x]

        for first in range(0, NF, 2):
            group = range(first, min(first + 2, NF))
            rhs = [stack3(flux[pl.ds(g, 64, stride=FP), :]) for g in group]
            out = mm(lift3[...], jnp.concatenate(rhs, axis=1))
            for i, g in enumerate(group):
                change = out[0:AP, i * NE : (i + 1) * NE] + vol[pl.ds(g, AP, stride=FP), :]
                new = lam_b[g, 0:AP, :] + STEP_SIZE * change
                if t == 0:
                    lam_b[g, 0:AP, :] = new
                else:
                    fin[g] = new
                lam_a[pl.ds(g, AP, stride=FP), :] = new

    yy_row = {}
    for i in range(HIST):
        for j in range(i, HIST):
            yy_row[i, j] = yy_row[j, i] = 25 + len([k for k in yy_row if k[0] <= k[1]])

    def dot_rows(i, j):
        acc = hist[i, 0] * hist[j, 0]
        for p in range(1, NM):
            acc = acc + hist[i, p] * hist[j, p]
        return jnp.sum(acc, axis=0, keepdims=True)

    def history():
        prods[...] = jnp.zeros(prods.shape, F32)
        for i in range(HIST):
            for j in range(HIST):
                row = i * HIST + j
                prods[row : row + 1, :] = dot_rows(i, HIST + j)
                if j >= i:
                    row = yy_row[i, j]
                    prods[row : row + 1, :] = dot_rows(HIST + i, HIST + j)

    def selections():
        for k in (6, 7):
            loads[k].wait()
        rows_n = lax.broadcasted_iota(jnp.int32, (640, NE), 0)
        for x in range(4):
            oh_nbr[:, x * NE : (x + 1) * NE] = jnp.where(rows_n == nbr[x : x + 1, :], 1.0, 0.0).astype(BF16)

    def tables():
        loads[4].wait()
        ct32[...] = jnp.zeros(ct32.shape, F32)
        cols = lax.broadcasted_iota(jnp.int32, (NF, 3 * KP), 1)
        rows = lax.broadcasted_iota(jnp.int32, (NF, 3 * KP), 0)
        places = [
            jnp.where(
                (cols == d * FP + rows) | (cols == KP + d * FP + rows) | (cols == 2 * KP + d * FP + rows), 1.0, 0.0
            )
            for d in range(3)
        ]
        table_cols = lax.broadcasted_iota(jnp.int32, (NM * FP, 3 * KP), 1)
        for side, dst in ((0, ct_v), (1, ct_g)):
            for p in range(NM):
                total = None
                for d in range(3):
                    part = lax.dot_general(
                        cpl[d, p], places[d], (((side,), (0,)), ((), ())), precision=HIGH, preferred_element_type=F32
                    )
                    total = part if total is None else total + part
                ct32[p * FP : p * FP + NF, :] = total
            whole = ct32[...]
            high = whole.astype(BF16)
            low = whole - high.astype(F32)
            dst[...] = jnp.where(table_cols < 2 * KP, high.astype(F32), low).astype(BF16)

    def clear(i, carry):
        spat[pl.ds(pl.multiple_of(i * KP, KP), KP), :] = jnp.zeros((KP, NE), F32)
        return carry

    loads[1].wait()
    rows_s = lax.broadcasted_iota(jnp.int32, (512, NE), 0)
    oh_send[...] = jnp.where(rows_s == send[...], 1.0, 0.0).astype(BF16)
    loads[0].wait()
    for f in range(NF):
        lam_a[pl.ds(f, AP, stride=FP), :] = lam_b[f, 0:AP, :]
    send_traces(0)
    tables()
    lax.fori_loop(0, AP, clear, 0)
    for x in range(4):
        flux[(x * 16 + 15) * FP : (x * 16 + 16) * FP, :] = jnp.zeros((FP, NE), F32)
    for k in (2, 3, 5):
        loads[k].wait()
    volume()
    selections()
    gather_local()
    loads[10].wait()
    forward_mix(0)
    for k in (8, 9, 11):
        loads[k].wait()
    surface(0)
    send_traces(1)
    hear(0)
    tell(1)
    gather_local()
    volume()
    hear(1)
    tell(2)
    loads[12].wait()
    forward_mix(1)
    lax.fori_loop(0, AP, times_lam, 0)
    for k in (13, 14):
        loads[k].wait()
    history()
    gram = jnp.sum(jnp.transpose(prods[...]), axis=0, keepdims=True) * (1.0 / n_shot)
    surface(1)

    lax.fori_loop(0, AP // 8, kernel_sum, 0)
    for k in range(2 * HIST):
        acc = hist[k, 0] * grads[0:AP, :]
        for p in range(1, NM):
            acc = acc + hist[k, p] * grads[grad_row(p) : grad_row(p) + AP, :]
        row = 120 + (k // HIST) * 128 + k % HIST
        grads[row : row + 1, :] = jnp.sum(acc, axis=0, keepdims=True)
    left = jnp.transpose(grads[0:128, :])
    right = jnp.transpose(grads[128:256, :])
    row_lane = lax.broadcasted_iota(jnp.int32, (1, NE), 1)
    vector = jnp.where(
        row_lane >= 120,
        jnp.sum(left, axis=0, keepdims=True),
        jnp.where(row_lane >= 112, pltpu.roll(jnp.sum(right, axis=0, keepdims=True), 120, 1), gram),
    )
    plane_src[...] = vector
    hear(2)
    planes = [
        pltpu.make_async_remote_copy(
            src_ref=plane_src, dst_ref=plane_got.at[k], send_sem=plane_send.at[k], recv_sem=plane_recv.at[k],
            device_id=peer, device_id_type=MESH,
        )
        for k, peer in enumerate(plane_peers)
    ]
    for one in planes:
        one.start()

    half = n_q * share
    for h in range(n_hi):
        gt[h, :, 0:128] = left[h * half : (h + 1) * half]
        gt[h, :, 128:256] = right[h * half : (h + 1) * half]
    firsts = []
    for o in range(1, n_q):
        peer_q = (q_id + o) % n_q
        firsts.append(
            pltpu.make_async_remote_copy(
                src_ref=gt.at[:, pl.ds(pl.multiple_of(peer_q * share, share), share), :],
                dst_ref=rs_got.at[o - 1],
                send_sem=rs_send.at[o - 1], recv_sem=rs_recv.at[o - 1],
                device_id={"shot": hi_id * n_q + peer_q}, device_id_type=MESH,
            )
        )
    for one in firsts:
        one.start()
    final_out = pltpu.make_async_copy(fin.at[:, 0:NB], fin_hbm.at[:, :, 0], fin_sem.at[0])
    final_out.start()

    def turn_history(k, carry):
        for side in range(2):
            block = [hist[k, side * 3 + p] for p in range(3)] + [jnp.zeros((8, NE), F32)]
            turned[:, side * 128 : (side + 1) * 128] = jnp.transpose(jnp.concatenate(block, axis=0))
        hist_t[k] = turned[pl.ds(pl.multiple_of(s_id * share, share), share), :]
        return carry

    lax.fori_loop(0, 2 * HIST, turn_history, 0)

    mine = gt[:, pl.ds(pl.multiple_of(q_id * share, share), share), :]
    for o, one in enumerate(firsts):
        one.wait_recv()
        mine = mine + rs_got[o]
    rs_mid[...] = mine
    seconds = []
    for o in range(1, n_hi):
        seconds.append(
            pltpu.make_async_remote_copy(
                src_ref=rs_mid.at[(hi_id + o) % n_hi],
                dst_ref=rs_last.at[o - 1],
                send_sem=rs_send.at[n_q - 2 + o], recv_sem=rs_recv.at[n_q - 2 + o],
                device_id={"shot": ((hi_id + o) % n_hi) * n_q + q_id}, device_id_type=MESH,
            )
        )
    for one in seconds:
        one.start()

    def collected(value, copies, got):
        sums = [value, None, None, None]
        for k, one in enumerate(copies):
            one.wait_recv()
            at = (k + 1) % 4
            sums[at] = got[k] if sums[at] is None else sums[at] + got[k]
        sums = [one for one in sums if one is not None]
        while len(sums) > 1:
            sums = sums[2:] + [sums[0] + sums[1]]
        return sums[0]

    vector = collected(vector, planes, plane_got)
    line_src[...] = vector
    lines = [
        pltpu.make_async_remote_copy(
            src_ref=line_src, dst_ref=line_got.at[k], send_sem=line_send.at[k], recv_sem=line_recv.at[k],
            device_id=peer, device_id_type=MESH,
        )
        for k, peer in enumerate(line_peers)
    ]
    for one in lines:
        one.start()
    total = rs_mid[hi_id]
    for t in range(2):
        down, up = halo_copies(t)

        @pl.when(has_below)
        def _():
            down.wait_send()

        @pl.when(has_above)
        def _():
            up.wait_send()

    for one in planes + firsts:
        one.wait_send()
    final_out.wait()
    for o, one in enumerate(seconds):
        one.wait_recv()
        total = total + rs_last[o]
    vector = collected(vector, lines, line_got)

    scal[...] = jnp.transpose(jnp.broadcast_to(vector, (NE, NE)))

    def num(k):
        return scal[k : k + 1, :]

    def sy(i, j):
        return num(i * HIST + j)

    over = [1.0 / sy(i, i) for i in range(HIST)]
    gamma = sy(HIST - 1, HIST - 1) / num(yy_row[HIST - 1, HIST - 1])
    alphas = [None] * HIST
    for i in reversed(range(HIST)):
        value = num(120 + i)
        for j in reversed(range(i + 1, HIST)):
            value = value - alphas[j] * sy(i, j)
        alphas[i] = value * over[i]
    rest = []
    for i in range(HIST):
        value = num(112 + i)
        for j in range(HIST):
            value = value - alphas[j] * num(yy_row[i, j])
        value = gamma * value
        for j in range(i):
            value = value + rest[j] * sy(j, i)
        rest.append(alphas[i] - value * over[i])

    sides = []
    for side in range(2):
        lanes = slice(side * 128, (side + 1) * 128)
        acc = -total[:, lanes]
        for i in range(HIST):
            acc = acc + alphas[i] * hist_t[HIST + i, :, lanes]
        acc = gamma * acc
        for i in range(HIST):
            acc = acc - rest[i] * hist_t[i, :, lanes]
        sides.append(acc)
    for p in range(NM):
        at = (p % 3) * AP
        dir_ref[p] = sides[p // 3][:, at : at + NB]

    for one in seconds + lines:
        one.wait_send()


def shards(
    dims,
    adjoint_state,
    forward_states,
    material,
    coupling,
    metric,
    face_normals,
    face_scale,
    face_neighbours,
    face_orientation,
    send_faces,
    history_steps,
    history_changes,
):
    n_hi, n_q, n_x, n_zl = dims
    share = NE // (n_hi * n_q)
    n_plane, n_line = n_q * n_x, n_hi * n_zl
    vmem = pl.BlockSpec(memory_space=pltpu.VMEM)
    hbm = pl.BlockSpec(memory_space=pltpu.HBM)
    dma = pltpu.SemaphoreType.DMA
    i32 = jnp.int32
    final, direction = pl.pallas_call(
        functools.partial(body, dims),
        out_shape=(
            jax.ShapeDtypeStruct((NF, NB, 1, NE), F32),
            jax.ShapeDtypeStruct((NM, share, NB), F32),
        ),
        in_specs=[hbm] * 14,
        out_specs=(hbm, vmem),
        scratch_shapes=[
            pltpu.VMEM((2 * HIST, NM, AP, NE), F32),
            pltpu.VMEM((NF, AP, NE), F32),
            pltpu.VMEM((3, NM, NF, NF), F32),
            pltpu.VMEM((3, 3, NE), F32),
            pltpu.VMEM((3, 4, NE), F32),
            pltpu.VMEM((4, NE), F32),
            pltpu.VMEM((4, NE), i32),
            pltpu.VMEM((4, NE), i32),
            pltpu.VMEM((1, NE), i32),
            pltpu.VMEM((128, 3 * KP), BF16),
            pltpu.VMEM((KP, 192), BF16),
            pltpu.VMEM((NF, KP, NE), F32),
            pltpu.VMEM((2, NF, KP, NE), F32),
            pltpu.VMEM((AP * FP, NE), F32),
            pltpu.VMEM((AP * KP, NE), F32),
            pltpu.VMEM((2, AP * NM * FP, NE), F32),
            pltpu.VMEM((AP * FP, NE), F32),
            pltpu.VMEM((64 * FP, NE), F32),
            pltpu.VMEM((NM, AP, NE), F32),
            pltpu.VMEM((480, 512), BF16),
            pltpu.VMEM((512, NE), BF16),
            pltpu.VMEM((640, 512), BF16),
            pltpu.VMEM((240, 512), F32),
            pltpu.VMEM((2, NE, NE), F32),
            pltpu.VMEM((2, NE, NE), F32),
            pltpu.VMEM((2, NE, NE), F32),
            pltpu.VMEM((2, NE, NE), F32),
            pltpu.VMEM((NM * FP, 3 * KP), F32),
            pltpu.VMEM((NM * FP, 3 * KP), BF16),
            pltpu.VMEM((NM * FP, 3 * KP), BF16),
            pltpu.VMEM((256, NE), F32),
            pltpu.VMEM((n_hi, n_q * share, 256), F32),
            pltpu.VMEM((n_q - 1, n_hi, share, 256), F32),
            pltpu.VMEM((n_hi, share, 256), F32),
            pltpu.VMEM((n_hi - 1, share, 256), F32),
            pltpu.VMEM((NE, NE), F32),
            pltpu.VMEM((NE, 256), F32),
            pltpu.VMEM((2 * HIST, share, 256), F32),
            pltpu.VMEM((1, NE), F32),
            pltpu.VMEM((n_plane - 1, 1, NE), F32),
            pltpu.VMEM((1, NE), F32),
            pltpu.VMEM((n_line - 1, 1, NE), F32),
            pltpu.VMEM((NE, NE), F32),
            dma((15,)),
            dma((1,)),
            dma((2, 2)),
            dma((2, 2)),
            dma((n_q + n_hi - 2,)),
            dma((n_q + n_hi - 2,)),
            pltpu.SemaphoreType.REGULAR((3,)),
            dma((n_plane - 1,)),
            dma((n_plane - 1,)),
            dma((n_line - 1,)),
            dma((n_line - 1,)),
        ],
        compiler_params=pltpu.CompilerParams(
            collective_id=0, has_side_effects=True, vmem_limit_bytes=63 * 2**20
        ),
    )(
        jnp.transpose(adjoint_state, (1, 2, 0, 3)), jnp.transpose(forward_states[0], (1, 2, 0, 3)),
        material, history_steps, history_changes,
        coupling, metric, face_normals, face_scale, face_neighbours, face_orientation,
        send_faces.reshape(1, -1), jnp.asarray(deriv_table()), jnp.asarray(lift_table()),
    )
    return jnp.transpose(final, (2, 0, 1, 3)), jnp.transpose(direction, (0, 2, 1))


def dims_of(mesh):
    n_shot, n_mesh = mesh.shape["shot"], mesh.shape["mesh"]
    n_x = 4 if n_mesh >= 16 else 2
    return 2, n_shot // 2, n_x, n_mesh // n_x


def solution(mesh):
    placed = (
        P("shot", None, None, "mesh"),
        P("shot", None, None, None, "mesh"),
        P(None, None, "mesh"),
        P(),
        P(None, None, "mesh"),
        P(None, None, "mesh"),
        P(None, "mesh"),
        P(None, "mesh"),
        P(None, "mesh"),
        P("mesh"),
        P(None, None, None, "mesh"),
        P(None, None, None, "mesh"),
    )
    return jax.shard_map(
        functools.partial(shards, dims_of(mesh)),
        mesh=mesh,
        in_specs=placed,
        out_specs=(P("shot", None, None, "mesh"), P(None, None, ("mesh", "shot"))),
        check_vma=False,
    )
```

```python
import functools
import math

import jax
import jax.numpy as jnp
import ml_dtypes
import numpy as np
from jax import lax
from jax.experimental import pallas as pl
from jax.experimental.pallas import tpu as pltpu
from jax.sharding import PartitionSpec as P

F32 = jnp.float32
BF16 = jnp.bfloat16
STEP_SIZE = 0.02
MESH = pl.DeviceIdType.MESH

NF = 13
FP = 16
NB = 35
AP = 40
KP = 48
NFN = 15
NM = 6
NE = 128
HIST = 5


def invert_matrix(matrix):
    order_count = matrix.shape[0]
    working = np.concatenate([matrix * 1.0, np.eye(order_count)], axis=1)
    for column in range(order_count):
        pivot_row = column + int(np.argmax(np.abs(working[column:, column])))
        working[[column, pivot_row]] = working[[pivot_row, column]]
        working[column] = working[column] / working[column, column]
        for target in range(order_count):
            if target != column:
                working[target] = working[target] - working[target, column] * working[column]
    return working[:, order_count:]


def basis_tables():
    points = [
        (across, along, upward)
        for upward in range(5)
        for along in range(5 - upward)
        for across in range(5 - upward - along)
    ]
    exponents = np.array(points) * 1.0
    coords = exponents / 4.0
    vander = np.prod(coords[:, None, :] ** exponents[None, :, :], axis=2)
    inverse = invert_matrix(vander)
    derivs = []
    for direction_axis in range(3):
        lowered = np.maximum(exponents - np.eye(3)[direction_axis], 0.0)
        slopes = exponents[None, :, direction_axis] * np.prod(
            coords[:, None, :] ** lowered[None, :, :], axis=2
        )
        derivs.append(slopes @ inverse)
    moments = np.array(
        [
            [
                math.factorial(first[0] + second[0])
                * math.factorial(first[1] + second[1])
                * math.factorial(first[2] + second[2])
                / math.factorial(sum(first) + sum(second) + 3)
                for second in points
            ]
            for first in points
        ]
    )
    mass_matrix = inverse.T @ moments @ inverse
    lattice = [(across, along) for along in range(5) for across in range(5 - along)]
    lattice_powers = np.array(lattice) * 1.0
    face_vander = np.prod((lattice_powers / 4.0)[:, None, :] ** lattice_powers[None, :, :], axis=2)
    face_inverse = invert_matrix(face_vander)
    face_moments = np.array(
        [
            [
                math.factorial(first[0] + second[0])
                * math.factorial(first[1] + second[1])
                / math.factorial(sum(first) + sum(second) + 2)
                for second in lattice
            ]
            for first in lattice
        ]
    )
    face_mass = face_inverse.T @ face_moments @ face_inverse
    numbers = {point: number for number, point in enumerate(points)}
    face_points = [
        [(across, along, 0) for across, along in lattice],
        [(across, 0, along) for across, along in lattice],
        [(0, across, along) for across, along in lattice],
        [(across, along, 4 - across - along) for across, along in lattice],
    ]
    face_nodes = np.array(
        [[numbers[point] for point in listing] for listing in face_points], np.int32
    )
    mass_inverse = invert_matrix(mass_matrix)
    lift_tables = []
    for face_number in range(4):
        selector = np.eye(35)[face_nodes[face_number]]
        lift_tables.append(mass_inverse @ selector.T @ face_mass)
    orderings = [(0, 1, 2), (1, 2, 0), (2, 0, 1), (1, 0, 2), (0, 2, 1), (2, 1, 0)]
    lattice_numbers = {point: number for number, point in enumerate(lattice)}
    triples = [(across, along, 4 - across - along) for across, along in lattice]
    turn_nodes = np.array(
        [
            [lattice_numbers[triple[ordering[0]], triple[ordering[1]]] for triple in triples]
            for ordering in orderings
        ],
        np.int32,
    )
    return (
        np.stack(derivs).astype(np.float32),
        np.stack(lift_tables).astype(np.float32),
        face_nodes,
        turn_nodes,
    )


DERIVS, LIFTS, FACE_NODES, TURN = basis_tables()


def np_split(table):
    high = table.astype(ml_dtypes.bfloat16)
    low = (table - high.astype(np.float32)).astype(ml_dtypes.bfloat16)
    return np.concatenate([high, high, low], axis=1)


def deriv_table():
    table = np.zeros((128, KP), np.float32)
    for r in range(3):
        table[r * AP : r * AP + NB, :NB] = DERIVS[r]
    return np_split(table)


def lift_table():
    table = np.zeros((KP, 64), np.float32)
    for x in range(4):
        table[:NB, x * 16 : x * 16 + NFN] = LIFTS[x]
    return np_split(table)


def split(x):
    high = x.astype(BF16)
    low = (x - high.astype(F32)).astype(BF16)
    return high, low


def stack3(x):
    high, low = split(x)
    return jnp.concatenate([high, low, high], axis=0)


def mm(a, b):
    return jnp.dot(a, b, preferred_element_type=F32)


def grad_row(p):
    return (p // 3) * 128 + (p % 3) * AP


def body(
    dims,
    adj_hbm, fwd_hbm, mat_hbm, hs_hbm, hy_hbm,
    cpl_hbm, metric_hbm, normals_hbm, scale_hbm, nbr_hbm, orient_hbm, send_hbm, deriv3_hbm, lift3_hbm,
    fin_hbm, dir_ref,
    hist, fin, cpl, metric, normals, scale, nbr, orient, send, deriv3, lift3,
    lam_b, fwd_b, lam_a, spat, mixg, vol, flux, matp,
    trace, oh_send, oh_nbr, outer,
    msg_d, msg_u, got_d, got_u,
    padded, ct_v, ct_g,
    grads, gt, rs_got, rs_mid, rs_last, prods, turned, hist_t,
    plane_src, plane_got, line_src, line_got, scal,
    load_sem, fin_sem, halo_send, halo_recv, rs_send, rs_recv, known, plane_send, plane_recv, line_send, line_recv,
):
    n_hi, n_q, n_x, n_zl = dims
    n_shot, n_mesh = n_hi * n_q, n_x * n_zl
    n_plane, n_line = n_q * n_x, n_hi * n_zl
    share = NE // n_shot
    s_id = lax.axis_index("shot")
    m_id = lax.axis_index("mesh")
    hi_id, q_id = s_id // n_q, s_id % n_q
    zl_id, x_id = m_id // n_x, m_id % n_x
    has_below = m_id > 0
    has_above = m_id < n_mesh - 1

    plane_peers, line_peers = [], []
    for k in range(1, n_plane):
        other = (q_id * n_x + x_id + k) % n_plane
        plane_peers.append({"shot": hi_id * n_q + other // n_x, "mesh": zl_id * n_x + other % n_x})
    for k in range(1, n_line):
        other = (hi_id * n_zl + zl_id + k) % n_line
        line_peers.append({"shot": (other // n_zl) * n_q + q_id, "mesh": (other % n_zl) * n_x + x_id})

    barrier = pltpu.get_barrier_semaphore()

    @pl.when(has_below)
    def _():
        pl.semaphore_signal(barrier, inc=1, device_id={"mesh": m_id - 1}, device_id_type=MESH)

    @pl.when(has_above)
    def _():
        pl.semaphore_signal(barrier, inc=1, device_id={"mesh": m_id + 1}, device_id_type=MESH)

    def at_plane(step_x, step_q, flip):
        y_id, c_id = q_id // 2, q_id % 2
        other_q = ((y_id + step_q) % (n_q // 2)) * 2 + (c_id + flip) % 2
        return {"shot": hi_id * n_q + other_q, "mesh": zl_id * n_x + (x_id + step_x) % n_x}

    def at_line(step):
        return line_peers[step % n_line - 1]

    core = at_plane(0, 0, 1)
    rounds = [
        [core, at_plane(1, 0, 0), at_plane(n_x - 1, 0, 0), at_plane(0, 1, 0), at_plane(0, n_q // 2 - 1, 0), at_line(1), at_line(-1)],
        [at_plane(2, 0, 0), at_plane(0, 2, 0), at_line(2), at_line(-2)],
        [core, at_line(4), at_line(-4)],
    ]
    for peer in rounds[0]:
        pl.semaphore_signal(barrier, inc=1, device_id=peer, device_id_type=MESH)

    def tell(k):
        for peer in rounds[k]:
            pl.semaphore_signal(known.at[k], inc=1, device_id=peer, device_id_type=MESH)

    def hear(k):
        pl.semaphore_wait(known.at[k], len(rounds[k]))

    for f in range(NF):
        lam_b[f, 32:KP, :] = jnp.zeros((KP - 32, NE), F32)
    pairs = [
        (adj_hbm.at[:, :, 0], lam_b.at[:, 0:NB]),
        (send_hbm, send),
        (deriv3_hbm, deriv3),
        (metric_hbm, metric),
        (cpl_hbm, cpl),
        (mat_hbm, matp.at[:, 0:NB]),
        (nbr_hbm, nbr),
        (orient_hbm, orient),
        (normals_hbm, normals),
        (scale_hbm, scale),
        (fwd_hbm.at[:, :, 0], fwd_b.at[0, :, 0:NB]),
        (lift3_hbm, lift3),
        (fwd_hbm.at[:, :, 1], fwd_b.at[1, :, 0:NB]),
        (hs_hbm, hist.at[0:HIST, :, 0:NB]),
        (hy_hbm, hist.at[HIST : 2 * HIST, :, 0:NB]),
    ]
    loads = [pltpu.make_async_copy(src, dst, load_sem.at[k]) for k, (src, dst) in enumerate(pairs)]
    loads[0].start()
    loads[1].start()
    matp[:, 32:AP, :] = jnp.zeros((NM, AP - 32, NE), F32)
    for t in range(2):
        for f in range(NF):
            fwd_b[t, f, 32:KP, :] = jnp.zeros((KP - 32, NE), F32)
    for k in range(2 * HIST):
        hist[k, :, 32:AP, :] = jnp.zeros((NM, AP - 32, NE), F32)
    for one in loads[2:]:
        one.start()

    lam_a[...] = jnp.zeros(lam_a.shape, F32)

    @pl.when(jnp.logical_not(has_below))
    def _():
        got_u[...] = jnp.zeros(got_u.shape, F32)

    @pl.when(jnp.logical_not(has_above))
    def _():
        got_d[...] = jnp.zeros(got_d.shape, F32)

    lane = lax.broadcasted_iota(jnp.int32, (FP, NE), 1)
    low_half = lane < 64
    filled = lax.broadcasted_iota(jnp.int32, (FP, NE), 0) < NF

    def derivative(field):
        for first in range(0, NF, 2):
            group = range(first, min(first + 2, NF))
            out = mm(deriv3[...], jnp.concatenate([stack3(field[f]) for f in group], axis=1))
            for i, f in enumerate(group):
                slab = [out[r * AP : (r + 1) * AP, i * NE : (i + 1) * NE] for r in range(3)]
                for d in range(3):
                    s = metric[0, d : d + 1, :] * slab[0]
                    s = s + metric[1, d : d + 1, :] * slab[1]
                    s = s + metric[2, d : d + 1, :] * slab[2]
                    spat[pl.ds(d * FP + f, AP, stride=KP), :] = s

    def mixed(table, base):
        parts = []
        for j in range(8):
            at = pl.multiple_of((base + j) * KP, KP)
            parts.append(stack3(spat[pl.ds(at, KP), :]))
        return mm(table[...], jnp.concatenate(parts, axis=1))

    def volume():
        derivative(lam_b)

        def block(i, carry):
            base = pl.multiple_of(i * 8, 8)
            mix = mixed(ct_v, base)
            params = [matp[p, pl.ds(base, 8), :] for p in range(NM)]
            for j in range(8):
                acc = params[0][j : j + 1, :] * mix[0:FP, j * NE : (j + 1) * NE]
                for p in range(1, NM):
                    acc = acc + params[p][j : j + 1, :] * mix[p * FP : (p + 1) * FP, j * NE : (j + 1) * NE]
                vol[pl.ds(pl.multiple_of((base + j) * FP, FP), FP), :] = acc
            return carry

        lax.fori_loop(0, AP // 8, block, 0)

    def forward_mix(t):
        derivative(fwd_b.at[t])

        def block(i, carry):
            base = pl.multiple_of(i * 8, 8)
            mix = mixed(ct_g, base)
            for j in range(8):
                at = pl.multiple_of((base + j) * NM * FP, NM * FP)
                mixg[t, pl.ds(at, NM * FP), :] = mix[:, j * NE : (j + 1) * NE]
            return carry

        lax.fori_loop(0, AP // 8, block, 0)

    def times_lam(i, carry):
        lam = lam_a[pl.ds(pl.multiple_of(i * FP, FP), FP), :]
        for p in range(NM):
            at = pl.ds(pl.multiple_of(i * NM * FP + p * FP, FP), FP)
            mixg[0, at, :] = mixg[0, at, :] * lam
        return carry

    def kernel_sum(i, carry):
        base = pl.multiple_of(i * 8, 8)
        for p in range(NM):
            rows_out = []
            for j in range(8):
                lam = lam_a[pl.ds(pl.multiple_of((base + j) * FP, FP), FP), :]
                at = pl.ds(pl.multiple_of((base + j) * NM * FP + p * FP, FP), FP)
                both = mixg[0, at, :] + mixg[1, at, :] * lam
                rows_out.append(jnp.sum(both, axis=0, keepdims=True))
            at = pl.ds(pl.multiple_of(grad_row(p) + base, 8), 8)
            grads[at, :] = jnp.concatenate(rows_out, axis=0) * STEP_SIZE
        return carry

    def inner_of(n, x):
        at = int(FACE_NODES[x][n]) * FP
        return lam_a[at : at + FP, :]

    def halo_copies(t):
        down = pltpu.make_async_remote_copy(
            src_ref=msg_d.at[t, :, 0:NF], dst_ref=got_d.at[t, :, 0:NF], send_sem=halo_send.at[t, 0], recv_sem=halo_recv.at[t, 0],
            device_id={"mesh": m_id - 1}, device_id_type=MESH,
        )
        up = pltpu.make_async_remote_copy(
            src_ref=msg_u.at[t, :, 0:NF], dst_ref=got_u.at[t, :, 0:NF], send_sem=halo_send.at[t, 1], recv_sem=halo_recv.at[t, 1],
            device_id={"mesh": m_id + 1}, device_id_type=MESH,
        )
        return down, up

    def send_traces(t):
        for n in range(NFN):
            for x in range(4):
                high, low = split(inner_of(n, x))
                trace[n * FP : (n + 1) * FP, x * NE : (x + 1) * NE] = high
                trace[240 + n * FP : 240 + (n + 1) * FP, x * NE : (x + 1) * NE] = low
        both = mm(trace[...], oh_send[...])
        picked = both[0:240] + both[240:480]
        for j in range(8):
            first = picked[j * FP : (j + 1) * FP]
            if j < 7:
                second = picked[(j + 8) * FP : (j + 9) * FP]
            else:
                second = jnp.zeros((FP, NE), F32)
            msg_d[t, j] = jnp.where(low_half, first, pltpu.roll(second, 64, 1))
            msg_u[t, j] = jnp.where(low_half, pltpu.roll(first, 64, 1), second)
        if t == 0:
            n_wait = len(rounds[0])
            pl.semaphore_wait(barrier, n_wait + has_below.astype(jnp.int32) + has_above.astype(jnp.int32))
        down, up = halo_copies(t)

        @pl.when(has_below)
        def _():
            down.start()

        @pl.when(has_above)
        def _():
            up.start()

        if t == 0:
            tell(0)

    def gather_local():
        local = mm(trace[...], oh_nbr[0:512, :])
        outer[...] = local[0:240] + local[240:480]

    def surface(t):
        down, up = halo_copies(t)

        @pl.when(has_above)
        def _():
            down.wait_recv()

        @pl.when(has_below)
        def _():
            up.wait_recv()

        tops, bottoms = [], []
        for j in range(8):
            above = jnp.where(filled, got_d[t, j], 0.0)
            below = jnp.where(filled, got_u[t, j], 0.0)
            tops.append(jnp.where(low_half, below, pltpu.roll(above, 64, 1)))
            bottoms.append(jnp.where(low_half, pltpu.roll(below, 64, 1), above))
        ghosts = jnp.concatenate(tops + bottoms[:7], axis=0)
        high, low = split(ghosts)
        part = mm(jnp.concatenate([high, low], axis=0), oh_nbr[512:640, :])
        outer[...] = outer[...] + (part[0:240] + part[240:480])

        turns = [jnp.broadcast_to(orient[x : x + 1, :], (FP, NE)) for x in range(4)]
        halves = [0.5 * scale[x : x + 1, :] for x in range(4)]
        for n in range(NFN):
            sources = {}
            for o in range(6):
                sources.setdefault(int(TURN[o][n]), []).append(o)
            sources = list(sources.items())
            jumps, weighted = [], []
            for x in range(4):
                at = sources[0][0] * FP
                value = outer[at : at + FP, x * NE : (x + 1) * NE]
                for node, options in sources[1:]:
                    mask = turns[x] == options[0]
                    for o in options[1:]:
                        mask = mask | (turns[x] == o)
                    value = jnp.where(mask, outer[node * FP : (node + 1) * FP, x * NE : (x + 1) * NE], value)
                jump = value - inner_of(n, x)
                jumps.append(jump)
                weighted.append(
                    stack3(jnp.concatenate([normals[d, x : x + 1, :] * jump for d in range(3)], axis=0))
                )
            mix = mm(ct_v[...], jnp.concatenate(weighted, axis=1))
            for x in range(4):
                node = int(FACE_NODES[x][n])
                acc = jumps[x]
                for p in range(NM):
                    acc = acc + matp[p, node : node + 1, :] * mix[p * FP : (p + 1) * FP, x * NE : (x + 1) * NE]
                at = (x * 16 + n) * FP
                flux[at : at + FP, :] = acc * halves[x]

        for first in range(0, NF, 2):
            group = range(first, min(first + 2, NF))
            rhs = [stack3(flux[pl.ds(g, 64, stride=FP), :]) for g in group]
            out = mm(lift3[...], jnp.concatenate(rhs, axis=1))
            for i, g in enumerate(group):
                change = out[0:AP, i * NE : (i + 1) * NE] + vol[pl.ds(g, AP, stride=FP), :]
                new = lam_b[g, 0:AP, :] + STEP_SIZE * change
                if t == 0:
                    lam_b[g, 0:AP, :] = new
                else:
                    fin[g] = new
                lam_a[pl.ds(g, AP, stride=FP), :] = new

    yy_row = {}
    for i in range(HIST):
        for j in range(i, HIST):
            yy_row[i, j] = yy_row[j, i] = 25 + len([k for k in yy_row if k[0] <= k[1]])

    def dot_rows(i, j):
        acc = hist[i, 0] * hist[j, 0]
        for p in range(1, NM):
            acc = acc + hist[i, p] * hist[j, p]
        return jnp.sum(acc, axis=0, keepdims=True)

    def history():
        prods[...] = jnp.zeros(prods.shape, F32)
        for i in range(HIST):
            for j in range(HIST):
                row = i * HIST + j
                prods[row : row + 1, :] = dot_rows(i, HIST + j)
                if j >= i:
                    row = yy_row[i, j]
                    prods[row : row + 1, :] = dot_rows(HIST + i, HIST + j)

    def selections():
        for k in (6, 7):
            loads[k].wait()
        rows_n = lax.broadcasted_iota(jnp.int32, (640, NE), 0)
        for x in range(4):
            oh_nbr[:, x * NE : (x + 1) * NE] = jnp.where(rows_n == nbr[x : x + 1, :], 1.0, 0.0).astype(BF16)

    def tables():
        loads[4].wait()
        padded[...] = jnp.zeros(padded.shape, F32)
        for p in range(NM):
            for d in range(3):
                padded[p, d * FP : d * FP + NF, 0:NF] = cpl[d, p]
        for p in range(NM):
            flipped = jnp.transpose(padded[p])[0:FP]
            straight = padded[p, 0:FP]
            for d in range(1, 3):
                straight = straight + pltpu.roll(padded[p, d * FP : (d + 1) * FP], d * FP, 1)
            for block, dst in ((flipped, ct_v), (straight, ct_g)):
                high = block.astype(BF16).astype(F32)
                low = pltpu.roll(block - high, 2 * KP, 1)
                first = jnp.where(lane < KP, high, jnp.where(lane < 2 * KP, pltpu.roll(high, KP, 1), low))
                dst[p * FP : (p + 1) * FP, 0:NE] = first.astype(BF16)
                dst[p * FP : (p + 1) * FP, NE : 3 * KP] = low[:, 0 : 3 * KP - NE].astype(BF16)

    def clear(i, carry):
        spat[pl.ds(pl.multiple_of(i * KP, KP), KP), :] = jnp.zeros((KP, NE), F32)
        return carry

    loads[1].wait()
    rows_s = lax.broadcasted_iota(jnp.int32, (512, NE), 0)
    oh_send[...] = jnp.where(rows_s == send[...], 1.0, 0.0).astype(BF16)
    loads[0].wait()
    for f in range(NF):
        lam_a[pl.ds(f, AP, stride=FP), :] = lam_b[f, 0:AP, :]
    send_traces(0)
    tables()
    lax.fori_loop(0, AP, clear, 0)
    for x in range(4):
        flux[(x * 16 + 15) * FP : (x * 16 + 16) * FP, :] = jnp.zeros((FP, NE), F32)
    for k in (2, 3, 5):
        loads[k].wait()
    volume()
    selections()
    gather_local()
    loads[10].wait()
    forward_mix(0)
    for k in (13, 14):
        loads[k].wait()
    history()
    gram = jnp.sum(jnp.transpose(prods[...]), axis=0, keepdims=True) * (1.0 / n_shot)
    for k in (8, 9, 11):
        loads[k].wait()
    surface(0)
    send_traces(1)
    hear(0)
    tell(1)
    gather_local()
    volume()
    hear(1)
    tell(2)
    loads[12].wait()
    forward_mix(1)
    lax.fori_loop(0, AP, times_lam, 0)
    surface(1)

    lax.fori_loop(0, AP // 8, kernel_sum, 0)
    for k in range(2 * HIST):
        acc = hist[k, 0] * grads[0:AP, :]
        for p in range(1, NM):
            acc = acc + hist[k, p] * grads[grad_row(p) : grad_row(p) + AP, :]
        row = 120 + (k // HIST) * 128 + k % HIST
        grads[row : row + 1, :] = jnp.sum(acc, axis=0, keepdims=True)
    left = jnp.transpose(grads[0:128, :])
    right = jnp.transpose(grads[128:256, :])
    row_lane = lax.broadcasted_iota(jnp.int32, (1, NE), 1)
    vector = jnp.where(
        row_lane >= 120,
        jnp.sum(left, axis=0, keepdims=True),
        jnp.where(row_lane >= 112, pltpu.roll(jnp.sum(right, axis=0, keepdims=True), 120, 1), gram),
    )
    plane_src[...] = vector
    hear(2)
    planes = [
        pltpu.make_async_remote_copy(
            src_ref=plane_src, dst_ref=plane_got.at[k], send_sem=plane_send.at[k], recv_sem=plane_recv.at[k],
            device_id=peer, device_id_type=MESH,
        )
        for k, peer in enumerate(plane_peers)
    ]
    for one in planes:
        one.start()

    half = n_q * share
    for h in range(n_hi):
        gt[h, :, 0:128] = left[h * half : (h + 1) * half]
        gt[h, :, 128:256] = right[h * half : (h + 1) * half]
    firsts = []
    for o in range(1, n_q):
        peer_q = (q_id + o) % n_q
        firsts.append(
            pltpu.make_async_remote_copy(
                src_ref=gt.at[:, pl.ds(pl.multiple_of(peer_q * share, share), share), :],
                dst_ref=rs_got.at[o - 1],
                send_sem=rs_send.at[o - 1], recv_sem=rs_recv.at[o - 1],
                device_id={"shot": hi_id * n_q + peer_q}, device_id_type=MESH,
            )
        )
    for one in firsts:
        one.start()
    final_out = pltpu.make_async_copy(fin.at[:, 0:NB], fin_hbm.at[:, :, 0], fin_sem.at[0])
    final_out.start()

    def turn_history(k, carry):
        for side in range(2):
            block = [hist[k, side * 3 + p] for p in range(3)] + [jnp.zeros((8, NE), F32)]
            turned[:, side * 128 : (side + 1) * 128] = jnp.transpose(jnp.concatenate(block, axis=0))
        hist_t[k] = turned[pl.ds(pl.multiple_of(s_id * share, share), share), :]
        return carry

    lax.fori_loop(0, 2 * HIST, turn_history, 0)

    mine = gt[:, pl.ds(pl.multiple_of(q_id * share, share), share), :]
    for o, one in enumerate(firsts):
        one.wait_recv()
        mine = mine + rs_got[o]
    rs_mid[...] = mine
    seconds = []
    for o in range(1, n_hi):
        seconds.append(
            pltpu.make_async_remote_copy(
                src_ref=rs_mid.at[(hi_id + o) % n_hi],
                dst_ref=rs_last.at[o - 1],
                send_sem=rs_send.at[n_q - 2 + o], recv_sem=rs_recv.at[n_q - 2 + o],
                device_id={"shot": ((hi_id + o) % n_hi) * n_q + q_id}, device_id_type=MESH,
            )
        )
    for one in seconds:
        one.start()

    def collected(value, copies, got):
        sums = [value, None, None, None]
        for k, one in enumerate(copies):
            one.wait_recv()
            at = (k + 1) % 4
            sums[at] = got[k] if sums[at] is None else sums[at] + got[k]
        sums = [one for one in sums if one is not None]
        while len(sums) > 1:
            sums = sums[2:] + [sums[0] + sums[1]]
        return sums[0]

    vector = collected(vector, planes, plane_got)
    line_src[...] = vector
    lines = [
        pltpu.make_async_remote_copy(
            src_ref=line_src, dst_ref=line_got.at[k], send_sem=line_send.at[k], recv_sem=line_recv.at[k],
            device_id=peer, device_id_type=MESH,
        )
        for k, peer in enumerate(line_peers)
    ]
    for one in lines:
        one.start()
    total = rs_mid[hi_id]
    for t in range(2):
        down, up = halo_copies(t)

        @pl.when(has_below)
        def _():
            down.wait_send()

        @pl.when(has_above)
        def _():
            up.wait_send()

    for one in planes + firsts:
        one.wait_send()
    final_out.wait()
    for o, one in enumerate(seconds):
        one.wait_recv()
        total = total + rs_last[o]
    vector = collected(vector, lines, line_got)

    scal[...] = jnp.transpose(jnp.broadcast_to(vector, (NE, NE)))

    def num(k):
        return scal[k : k + 1, :]

    def sy(i, j):
        return num(i * HIST + j)

    over = [1.0 / sy(i, i) for i in range(HIST)]
    gamma = sy(HIST - 1, HIST - 1) / num(yy_row[HIST - 1, HIST - 1])
    alphas = [None] * HIST
    for i in reversed(range(HIST)):
        value = num(120 + i)
        for j in reversed(range(i + 1, HIST)):
            value = value - alphas[j] * sy(i, j)
        alphas[i] = value * over[i]
    rest = []
    for i in range(HIST):
        value = num(112 + i)
        for j in range(HIST):
            value = value - alphas[j] * num(yy_row[i, j])
        value = gamma * value
        for j in range(i):
            value = value + rest[j] * sy(j, i)
        rest.append(alphas[i] - value * over[i])

    sides = []
    for side in range(2):
        lanes = slice(side * 128, (side + 1) * 128)
        acc = -total[:, lanes]
        for i in range(HIST):
            acc = acc + alphas[i] * hist_t[HIST + i, :, lanes]
        acc = gamma * acc
        for i in range(HIST):
            acc = acc - rest[i] * hist_t[i, :, lanes]
        sides.append(acc)
    for p in range(NM):
        at = (p % 3) * AP
        dir_ref[p] = sides[p // 3][:, at : at + NB]

    for one in seconds + lines:
        one.wait_send()


def shards(
    dims,
    adjoint_state,
    forward_states,
    material,
    coupling,
    metric,
    face_normals,
    face_scale,
    face_neighbours,
    face_orientation,
    send_faces,
    history_steps,
    history_changes,
):
    n_hi, n_q, n_x, n_zl = dims
    share = NE // (n_hi * n_q)
    n_plane, n_line = n_q * n_x, n_hi * n_zl
    vmem = pl.BlockSpec(memory_space=pltpu.VMEM)
    hbm = pl.BlockSpec(memory_space=pltpu.HBM)
    dma = pltpu.SemaphoreType.DMA
    i32 = jnp.int32
    final, direction = pl.pallas_call(
        functools.partial(body, dims),
        out_shape=(
            jax.ShapeDtypeStruct((NF, NB, 1, NE), F32),
            jax.ShapeDtypeStruct((NM, share, NB), F32),
        ),
        in_specs=[hbm] * 14,
        out_specs=(hbm, vmem),
        scratch_shapes=[
            pltpu.VMEM((2 * HIST, NM, AP, NE), F32),
            pltpu.VMEM((NF, AP, NE), F32),
            pltpu.VMEM((3, NM, NF, NF), F32),
            pltpu.VMEM((3, 3, NE), F32),
            pltpu.VMEM((3, 4, NE), F32),
            pltpu.VMEM((4, NE), F32),
            pltpu.VMEM((4, NE), i32),
            pltpu.VMEM((4, NE), i32),
            pltpu.VMEM((1, NE), i32),
            pltpu.VMEM((128, 3 * KP), BF16),
            pltpu.VMEM((KP, 192), BF16),
            pltpu.VMEM((NF, KP, NE), F32),
            pltpu.VMEM((2, NF, KP, NE), F32),
            pltpu.VMEM((AP * FP, NE), F32),
            pltpu.VMEM((AP * KP, NE), F32),
            pltpu.VMEM((2, AP * NM * FP, NE), F32),
            pltpu.VMEM((AP * FP, NE), F32),
            pltpu.VMEM((64 * FP, NE), F32),
            pltpu.VMEM((NM, AP, NE), F32),
            pltpu.VMEM((480, 512), BF16),
            pltpu.VMEM((512, NE), BF16),
            pltpu.VMEM((640, 512), BF16),
            pltpu.VMEM((240, 512), F32),
            pltpu.VMEM((2, 8, FP, NE), F32),
            pltpu.VMEM((2, 8, FP, NE), F32),
            pltpu.VMEM((2, 8, FP, NE), F32),
            pltpu.VMEM((2, 8, FP, NE), F32),
            pltpu.VMEM((NM, NE, NE), F32),
            pltpu.VMEM((NM * FP, 3 * KP), BF16),
            pltpu.VMEM((NM * FP, 3 * KP), BF16),
            pltpu.VMEM((256, NE), F32),
            pltpu.VMEM((n_hi, n_q * share, 256), F32),
            pltpu.VMEM((n_q - 1, n_hi, share, 256), F32),
            pltpu.VMEM((n_hi, share, 256), F32),
            pltpu.VMEM((n_hi - 1, share, 256), F32),
            pltpu.VMEM((NE, NE), F32),
            pltpu.VMEM((NE, 256), F32),
            pltpu.VMEM((2 * HIST, share, 256), F32),
            pltpu.VMEM((1, NE), F32),
            pltpu.VMEM((n_plane - 1, 1, NE), F32),
            pltpu.VMEM((1, NE), F32),
            pltpu.VMEM((n_line - 1, 1, NE), F32),
            pltpu.VMEM((NE, NE), F32),
            dma((15,)),
            dma((1,)),
            dma((2, 2)),
            dma((2, 2)),
            dma((n_q + n_hi - 2,)),
            dma((n_q + n_hi - 2,)),
            pltpu.SemaphoreType.REGULAR((3,)),
            dma((n_plane - 1,)),
            dma((n_plane - 1,)),
            dma((n_line - 1,)),
            dma((n_line - 1,)),
        ],
        compiler_params=pltpu.CompilerParams(
            collective_id=0, has_side_effects=True, vmem_limit_bytes=63 * 2**20
        ),
    )(
        jnp.transpose(adjoint_state, (1, 2, 0, 3)), jnp.transpose(forward_states[0], (1, 2, 0, 3)),
        material, history_steps, history_changes,
        coupling, metric, face_normals, face_scale, face_neighbours, face_orientation,
        send_faces.reshape(1, -1), jnp.asarray(deriv_table()), jnp.asarray(lift_table()),
    )
    return jnp.transpose(final, (2, 0, 1, 3)), jnp.transpose(direction, (0, 2, 1))


def dims_of(mesh):
    n_shot, n_mesh = mesh.shape["shot"], mesh.shape["mesh"]
    n_x = 4 if n_mesh >= 16 else 2
    return 2, n_shot // 2, n_x, n_mesh // n_x


def solution(mesh):
    placed = (
        P("shot", None, None, "mesh"),
        P("shot", None, None, None, "mesh"),
        P(None, None, "mesh"),
        P(),
        P(None, None, "mesh"),
        P(None, None, "mesh"),
        P(None, "mesh"),
        P(None, "mesh"),
        P(None, "mesh"),
        P("mesh"),
        P(None, None, None, "mesh"),
        P(None, None, None, "mesh"),
    )
    return jax.shard_map(
        functools.partial(shards, dims_of(mesh)),
        mesh=mesh,
        in_specs=placed,
        out_specs=(P("shot", None, None, "mesh"), P(None, None, ("mesh", "shot"))),
        check_vma=False,
    )
```

```python
import functools
import math

import jax
import jax.numpy as jnp
import ml_dtypes
import numpy as np
from jax import lax
from jax.experimental import pallas as pl
from jax.experimental.pallas import tpu as pltpu
from jax.sharding import PartitionSpec as P

F32 = jnp.float32
BF16 = jnp.bfloat16
STEP_SIZE = 0.02
MESH = pl.DeviceIdType.MESH

NF = 13
FP = 16
NB = 35
AP = 40
KP = 48
NFN = 15
NM = 6
NE = 128
HIST = 5


def invert_matrix(matrix):
    order_count = matrix.shape[0]
    working = np.concatenate([matrix * 1.0, np.eye(order_count)], axis=1)
    for column in range(order_count):
        pivot_row = column + int(np.argmax(np.abs(working[column:, column])))
        working[[column, pivot_row]] = working[[pivot_row, column]]
        working[column] = working[column] / working[column, column]
        for target in range(order_count):
            if target != column:
                working[target] = working[target] - working[target, column] * working[column]
    return working[:, order_count:]


def basis_tables():
    points = [
        (across, along, upward)
        for upward in range(5)
        for along in range(5 - upward)
        for across in range(5 - upward - along)
    ]
    exponents = np.array(points) * 1.0
    coords = exponents / 4.0
    vander = np.prod(coords[:, None, :] ** exponents[None, :, :], axis=2)
    inverse = invert_matrix(vander)
    derivs = []
    for direction_axis in range(3):
        lowered = np.maximum(exponents - np.eye(3)[direction_axis], 0.0)
        slopes = exponents[None, :, direction_axis] * np.prod(
            coords[:, None, :] ** lowered[None, :, :], axis=2
        )
        derivs.append(slopes @ inverse)
    moments = np.array(
        [
            [
                math.factorial(first[0] + second[0])
                * math.factorial(first[1] + second[1])
                * math.factorial(first[2] + second[2])
                / math.factorial(sum(first) + sum(second) + 3)
                for second in points
            ]
            for first in points
        ]
    )
    mass_matrix = inverse.T @ moments @ inverse
    lattice = [(across, along) for along in range(5) for across in range(5 - along)]
    lattice_powers = np.array(lattice) * 1.0
    face_vander = np.prod((lattice_powers / 4.0)[:, None, :] ** lattice_powers[None, :, :], axis=2)
    face_inverse = invert_matrix(face_vander)
    face_moments = np.array(
        [
            [
                math.factorial(first[0] + second[0])
                * math.factorial(first[1] + second[1])
                / math.factorial(sum(first) + sum(second) + 2)
                for second in lattice
            ]
            for first in lattice
        ]
    )
    face_mass = face_inverse.T @ face_moments @ face_inverse
    numbers = {point: number for number, point in enumerate(points)}
    face_points = [
        [(across, along, 0) for across, along in lattice],
        [(across, 0, along) for across, along in lattice],
        [(0, across, along) for across, along in lattice],
        [(across, along, 4 - across - along) for across, along in lattice],
    ]
    face_nodes = np.array(
        [[numbers[point] for point in listing] for listing in face_points], np.int32
    )
    mass_inverse = invert_matrix(mass_matrix)
    lift_tables = []
    for face_number in range(4):
        selector = np.eye(35)[face_nodes[face_number]]
        lift_tables.append(mass_inverse @ selector.T @ face_mass)
    orderings = [(0, 1, 2), (1, 2, 0), (2, 0, 1), (1, 0, 2), (0, 2, 1), (2, 1, 0)]
    lattice_numbers = {point: number for number, point in enumerate(lattice)}
    triples = [(across, along, 4 - across - along) for across, along in lattice]
    turn_nodes = np.array(
        [
            [lattice_numbers[triple[ordering[0]], triple[ordering[1]]] for triple in triples]
            for ordering in orderings
        ],
        np.int32,
    )
    return (
        np.stack(derivs).astype(np.float32),
        np.stack(lift_tables).astype(np.float32),
        face_nodes,
        turn_nodes,
    )


DERIVS, LIFTS, FACE_NODES, TURN = basis_tables()


def np_split(table):
    high = table.astype(ml_dtypes.bfloat16)
    low = (table - high.astype(np.float32)).astype(ml_dtypes.bfloat16)
    return np.concatenate([high, high, low], axis=1)


def deriv_table():
    table = np.zeros((128, KP), np.float32)
    for r in range(3):
        table[r * AP : r * AP + NB, :NB] = DERIVS[r]
    return np_split(table)


def lift_table():
    table = np.zeros((KP, 64), np.float32)
    for x in range(4):
        table[:NB, x * 16 : x * 16 + NFN] = LIFTS[x]
    return np_split(table)


def split(x):
    high = x.astype(BF16)
    low = (x - high.astype(F32)).astype(BF16)
    return high, low


def stack3(x):
    high, low = split(x)
    return jnp.concatenate([high, low, high], axis=0)


def mm(a, b):
    return jnp.dot(a, b, preferred_element_type=F32)


def grad_row(p):
    return (p // 3) * 128 + (p % 3) * AP


def body(
    dims,
    adj_hbm, fwd_hbm, mat_hbm, hs_hbm, hy_hbm,
    cpl_hbm, metric_hbm, normals_hbm, scale_hbm, nbr_hbm, orient_hbm, send_hbm, deriv3_hbm, lift3_hbm,
    fin_hbm, dir_ref,
    hist, fin, cpl, metric, normals, scale, nbr, orient, send, deriv3, lift3,
    lam_b, fwd_b, lam_a, spat, mixg, vol, flux, matp,
    trace, oh_send, oh_nbr, outer,
    msg_d, msg_u, got_d, got_u,
    padded, ct_v, ct_g,
    grads, gt, rs_got, rs_mid, rs_last, prods, turned, hist_t,
    plane_src, plane_got, line_src, line_got, scal,
    load_sem, fin_sem, halo_send, halo_recv, rs_send, rs_recv, known, plane_send, plane_recv, line_send, line_recv,
):
    n_hi, n_q, n_x, n_zl = dims
    n_shot, n_mesh = n_hi * n_q, n_x * n_zl
    n_plane, n_line = n_q * n_x, n_hi * n_zl
    share = NE // n_shot
    s_id = lax.axis_index("shot")
    m_id = lax.axis_index("mesh")
    hi_id, q_id = s_id // n_q, s_id % n_q
    zl_id, x_id = m_id // n_x, m_id % n_x
    has_below = m_id > 0
    has_above = m_id < n_mesh - 1

    plane_peers, line_peers = [], []
    for k in range(1, n_plane):
        other = (q_id * n_x + x_id + k) % n_plane
        plane_peers.append({"shot": hi_id * n_q + other // n_x, "mesh": zl_id * n_x + other % n_x})
    for k in range(1, n_line):
        other = (hi_id * n_zl + zl_id + k) % n_line
        line_peers.append({"shot": (other // n_zl) * n_q + q_id, "mesh": (other % n_zl) * n_x + x_id})

    barrier = pltpu.get_barrier_semaphore()

    @pl.when(has_below)
    def _():
        pl.semaphore_signal(barrier, inc=1, device_id={"mesh": m_id - 1}, device_id_type=MESH)

    @pl.when(has_above)
    def _():
        pl.semaphore_signal(barrier, inc=1, device_id={"mesh": m_id + 1}, device_id_type=MESH)

    def at_plane(step_x, step_q, flip):
        y_id, c_id = q_id // 2, q_id % 2
        other_q = ((y_id + step_q) % (n_q // 2)) * 2 + (c_id + flip) % 2
        return {"shot": hi_id * n_q + other_q, "mesh": zl_id * n_x + (x_id + step_x) % n_x}

    def at_line(step):
        return line_peers[step % n_line - 1]

    core = at_plane(0, 0, 1)
    rounds = [
        [core, at_plane(1, 0, 0), at_plane(n_x - 1, 0, 0), at_plane(0, 1, 0), at_plane(0, n_q // 2 - 1, 0), at_line(1), at_line(-1)],
        [at_plane(2, 0, 0), at_plane(0, 2, 0), at_line(2), at_line(-2)],
        [core, at_line(4), at_line(-4)],
    ]
    for peer in rounds[0]:
        pl.semaphore_signal(barrier, inc=1, device_id=peer, device_id_type=MESH)

    def tell(k):
        for peer in rounds[k]:
            pl.semaphore_signal(known.at[k], inc=1, device_id=peer, device_id_type=MESH)

    def hear(k):
        pl.semaphore_wait(known.at[k], len(rounds[k]))

    for f in range(NF):
        lam_b[f, 32:KP, :] = jnp.zeros((KP - 32, NE), F32)
    pairs = [
        (adj_hbm.at[:, :, 0], lam_b.at[:, 0:NB]),
        (send_hbm, send),
        (deriv3_hbm, deriv3),
        (metric_hbm, metric),
        (cpl_hbm, cpl),
        (mat_hbm, matp.at[:, 0:NB]),
        (nbr_hbm, nbr),
        (orient_hbm, orient),
        (normals_hbm, normals),
        (scale_hbm, scale),
        (fwd_hbm.at[:, :, 0], fwd_b.at[0, :, 0:NB]),
        (lift3_hbm, lift3),
        (fwd_hbm.at[:, :, 1], fwd_b.at[1, :, 0:NB]),
        (hs_hbm, hist.at[0:HIST, :, 0:NB]),
        (hy_hbm, hist.at[HIST : 2 * HIST, :, 0:NB]),
    ]
    loads = [pltpu.make_async_copy(src, dst, load_sem.at[k]) for k, (src, dst) in enumerate(pairs)]
    loads[0].start()
    loads[1].start()
    matp[:, 32:AP, :] = jnp.zeros((NM, AP - 32, NE), F32)
    for t in range(2):
        for f in range(NF):
            fwd_b[t, f, 32:KP, :] = jnp.zeros((KP - 32, NE), F32)
    for k in range(2 * HIST):
        hist[k, :, 32:AP, :] = jnp.zeros((NM, AP - 32, NE), F32)
    for one in loads[2:]:
        one.start()

    lam_a[...] = jnp.zeros(lam_a.shape, F32)
    grads[120:128, :] = jnp.zeros((8, NE), F32)
    grads[248:256, :] = jnp.zeros((8, NE), F32)

    @pl.when(jnp.logical_not(has_below))
    def _():
        got_u[...] = jnp.zeros(got_u.shape, F32)

    @pl.when(jnp.logical_not(has_above))
    def _():
        got_d[...] = jnp.zeros(got_d.shape, F32)

    lane = lax.broadcasted_iota(jnp.int32, (FP, NE), 1)
    low_half = lane < 64
    filled = lax.broadcasted_iota(jnp.int32, (FP, NE), 0) < NF

    def derivative(field):
        for first in range(0, NF, 2):
            group = range(first, min(first + 2, NF))
            out = mm(deriv3[...], jnp.concatenate([stack3(field[f]) for f in group], axis=1))
            for i, f in enumerate(group):
                slab = [out[r * AP : (r + 1) * AP, i * NE : (i + 1) * NE] for r in range(3)]
                for d in range(3):
                    s = metric[0, d : d + 1, :] * slab[0]
                    s = s + metric[1, d : d + 1, :] * slab[1]
                    s = s + metric[2, d : d + 1, :] * slab[2]
                    spat[pl.ds(d * FP + f, AP, stride=KP), :] = s

    def mixed(table, base):
        parts = []
        for j in range(8):
            at = pl.multiple_of((base + j) * KP, KP)
            parts.append(stack3(spat[pl.ds(at, KP), :]))
        return mm(table[...], jnp.concatenate(parts, axis=1))

    def volume():
        derivative(lam_b)

        def block(i, carry):
            base = pl.multiple_of(i * 8, 8)
            mix = mixed(ct_v, base)
            params = [matp[p, pl.ds(base, 8), :] for p in range(NM)]
            for j in range(8):
                acc = params[0][j : j + 1, :] * mix[0:FP, j * NE : (j + 1) * NE]
                for p in range(1, NM):
                    acc = acc + params[p][j : j + 1, :] * mix[p * FP : (p + 1) * FP, j * NE : (j + 1) * NE]
                vol[pl.ds(pl.multiple_of((base + j) * FP, FP), FP), :] = acc
            return carry

        lax.fori_loop(0, AP // 8, block, 0, unroll=True)

    def forward_mix(t):
        derivative(fwd_b.at[t])

        def block(i, carry):
            base = pl.multiple_of(i * 8, 8)
            mix = mixed(ct_g, base)
            for j in range(8):
                at = pl.multiple_of((base + j) * NM * FP, NM * FP)
                mixg[t, pl.ds(at, NM * FP), :] = mix[:, j * NE : (j + 1) * NE]
            return carry

        lax.fori_loop(0, AP // 8, block, 0, unroll=True)

    sub_row = lax.broadcasted_iota(jnp.int32, (8, NE), 0)

    def tree(tiles):
        for step in (4, 2, 1):
            upper = (sub_row // step) % 2 == 1
            half = len(tiles) // 2
            merged = []
            for one, two in zip(tiles[:half], tiles[half:]):
                one = one + pltpu.roll(one, 8 - step, 0)
                two = two + pltpu.roll(two, step, 0)
                merged.append(jnp.where(upper, two, one))
            tiles = merged
        return tiles[0]

    def kernel_sum(t):
        def block(i, carry):
            base = pl.multiple_of(i * 8, 8)
            for p in range(NM):
                tiles = []
                for j in range(8):
                    lam = lam_a[pl.ds(pl.multiple_of((base + j) * FP, FP), FP), :]
                    at = pl.ds(pl.multiple_of((base + j) * NM * FP + p * FP, FP), FP)
                    both = mixg[t, at, :] * lam
                    tiles.append(both[0:8] + both[8:16])
                at = pl.ds(pl.multiple_of(grad_row(p) + base, 8), 8)
                part = tree(tiles) * STEP_SIZE
                grads[at, :] = part if t == 0 else grads[at, :] + part
            return carry

        lax.fori_loop(0, AP // 8, block, 0, unroll=True)

    def inner_of(n, x):
        at = int(FACE_NODES[x][n]) * FP
        return lam_a[at : at + FP, :]

    def halo_copies(t):
        down = pltpu.make_async_remote_copy(
            src_ref=msg_d.at[t, :, 0:NF], dst_ref=got_d.at[t, :, 0:NF], send_sem=halo_send.at[t, 0], recv_sem=halo_recv.at[t, 0],
            device_id={"mesh": m_id - 1}, device_id_type=MESH,
        )
        up = pltpu.make_async_remote_copy(
            src_ref=msg_u.at[t, :, 0:NF], dst_ref=got_u.at[t, :, 0:NF], send_sem=halo_send.at[t, 1], recv_sem=halo_recv.at[t, 1],
            device_id={"mesh": m_id + 1}, device_id_type=MESH,
        )
        return down, up

    def send_traces(t):
        for n in range(NFN):
            for x in range(4):
                high, low = split(inner_of(n, x))
                trace[n * FP : (n + 1) * FP, x * NE : (x + 1) * NE] = high
                trace[240 + n * FP : 240 + (n + 1) * FP, x * NE : (x + 1) * NE] = low
        both = mm(trace[...], oh_send[...])
        picked = both[0:240] + both[240:480]
        for j in range(8):
            first = picked[j * FP : (j + 1) * FP]
            if j < 7:
                second = picked[(j + 8) * FP : (j + 9) * FP]
            else:
                second = jnp.zeros((FP, NE), F32)
            msg_d[t, j] = jnp.where(low_half, first, pltpu.roll(second, 64, 1))
            msg_u[t, j] = jnp.where(low_half, pltpu.roll(first, 64, 1), second)
        if t == 0:
            n_wait = len(rounds[0])
            pl.semaphore_wait(barrier, n_wait + has_below.astype(jnp.int32) + has_above.astype(jnp.int32))
        down, up = halo_copies(t)

        @pl.when(has_below)
        def _():
            down.start()

        @pl.when(has_above)
        def _():
            up.start()

        if t == 0:
            tell(0)

    def gather_local():
        local = mm(trace[...], oh_nbr[0:512, :])
        outer[...] = local[0:240] + local[240:480]

    def surface(t):
        down, up = halo_copies(t)

        @pl.when(has_above)
        def _():
            down.wait_recv()

        @pl.when(has_below)
        def _():
            up.wait_recv()

        tops, bottoms = [], []
        for j in range(8):
            above = jnp.where(filled, got_d[t, j], 0.0)
            below = jnp.where(filled, got_u[t, j], 0.0)
            tops.append(jnp.where(low_half, below, pltpu.roll(above, 64, 1)))
            bottoms.append(jnp.where(low_half, pltpu.roll(below, 64, 1), above))
        ghosts = jnp.concatenate(tops + bottoms[:7], axis=0)
        high, low = split(ghosts)
        part = mm(jnp.concatenate([high, low], axis=0), oh_nbr[512:640, :])
        outer[...] = outer[...] + (part[0:240] + part[240:480])

        turns = [jnp.broadcast_to(orient[x : x + 1, :], (FP, NE)) for x in range(4)]
        halves = [0.5 * scale[x : x + 1, :] for x in range(4)]
        for n in range(NFN):
            sources = {}
            for o in range(6):
                sources.setdefault(int(TURN[o][n]), []).append(o)
            sources = list(sources.items())
            jumps, weighted = [], []
            for x in range(4):
                at = sources[0][0] * FP
                value = outer[at : at + FP, x * NE : (x + 1) * NE]
                for node, options in sources[1:]:
                    mask = turns[x] == options[0]
                    for o in options[1:]:
                        mask = mask | (turns[x] == o)
                    value = jnp.where(mask, outer[node * FP : (node + 1) * FP, x * NE : (x + 1) * NE], value)
                jump = value - inner_of(n, x)
                jumps.append(jump)
                weighted.append(
                    stack3(jnp.concatenate([normals[d, x : x + 1, :] * jump for d in range(3)], axis=0))
                )
            mix = mm(ct_v[...], jnp.concatenate(weighted, axis=1))
            for x in range(4):
                node = int(FACE_NODES[x][n])
                acc = jumps[x]
                for p in range(NM):
                    acc = acc + matp[p, node : node + 1, :] * mix[p * FP : (p + 1) * FP, x * NE : (x + 1) * NE]
                at = (x * 16 + n) * FP
                flux[at : at + FP, :] = acc * halves[x]

        for first in range(0, NF, 2):
            group = range(first, min(first + 2, NF))
            rhs = [stack3(flux[pl.ds(g, 64, stride=FP), :]) for g in group]
            out = mm(lift3[...], jnp.concatenate(rhs, axis=1))
            for i, g in enumerate(group):
                change = out[0:AP, i * NE : (i + 1) * NE] + vol[pl.ds(g, AP, stride=FP), :]
                new = lam_b[g, 0:AP, :] + STEP_SIZE * change
                if t == 0:
                    lam_b[g, 0:AP, :] = new
                else:
                    fin[g] = new
                lam_a[pl.ds(g, AP, stride=FP), :] = new

    yy_row = {}
    for i in range(HIST):
        for j in range(i, HIST):
            yy_row[i, j] = yy_row[j, i] = 25 + len([k for k in yy_row if k[0] <= k[1]])

    def dot_rows(i, j):
        acc = hist[i, 0] * hist[j, 0]
        for p in range(1, NM):
            acc = acc + hist[i, p] * hist[j, p]
        return jnp.sum(acc, axis=0, keepdims=True)

    def history():
        prods[...] = jnp.zeros(prods.shape, F32)
        for i in range(HIST):
            for j in range(HIST):
                row = i * HIST + j
                prods[row : row + 1, :] = dot_rows(i, HIST + j)
                if j >= i:
                    row = yy_row[i, j]
                    prods[row : row + 1, :] = dot_rows(HIST + i, HIST + j)

    def selections():
        for k in (6, 7):
            loads[k].wait()
        rows_n = lax.broadcasted_iota(jnp.int32, (640, NE), 0)
        for x in range(4):
            oh_nbr[:, x * NE : (x + 1) * NE] = jnp.where(rows_n == nbr[x : x + 1, :], 1.0, 0.0).astype(BF16)

    def tables():
        loads[4].wait()
        padded[...] = jnp.zeros(padded.shape, F32)
        for p in range(NM):
            for d in range(3):
                padded[p, d * FP : d * FP + NF, 0:NF] = cpl[d, p]
        for p in range(NM):
            flipped = jnp.transpose(padded[p])[0:FP]
            straight = padded[p, 0:FP]
            for d in range(1, 3):
                straight = straight + pltpu.roll(padded[p, d * FP : (d + 1) * FP], d * FP, 1)
            for block, dst in ((flipped, ct_v), (straight, ct_g)):
                high = block.astype(BF16).astype(F32)
                low = pltpu.roll(block - high, 2 * KP, 1)
                first = jnp.where(lane < KP, high, jnp.where(lane < 2 * KP, pltpu.roll(high, KP, 1), low))
                dst[p * FP : (p + 1) * FP, 0:NE] = first.astype(BF16)
                dst[p * FP : (p + 1) * FP, NE : 3 * KP] = low[:, 0 : 3 * KP - NE].astype(BF16)

    def clear(i, carry):
        spat[pl.ds(pl.multiple_of(i * KP, KP), KP), :] = jnp.zeros((KP, NE), F32)
        return carry

    loads[1].wait()
    rows_s = lax.broadcasted_iota(jnp.int32, (512, NE), 0)
    oh_send[...] = jnp.where(rows_s == send[...], 1.0, 0.0).astype(BF16)
    loads[0].wait()
    for f in range(NF):
        lam_a[pl.ds(f, AP, stride=FP), :] = lam_b[f, 0:AP, :]
    send_traces(0)
    tables()
    lax.fori_loop(0, AP, clear, 0, unroll=8)
    for x in range(4):
        flux[(x * 16 + 15) * FP : (x * 16 + 16) * FP, :] = jnp.zeros((FP, NE), F32)
    for k in (2, 3, 5):
        loads[k].wait()
    volume()
    selections()
    gather_local()
    loads[10].wait()
    forward_mix(0)
    for k in (13, 14):
        loads[k].wait()
    history()
    gram = jnp.sum(jnp.transpose(prods[...]), axis=0, keepdims=True) * (1.0 / n_shot)
    for k in (8, 9, 11):
        loads[k].wait()
    surface(0)
    send_traces(1)
    hear(0)
    tell(1)
    gather_local()
    volume()
    hear(1)
    tell(2)
    loads[12].wait()
    forward_mix(1)
    kernel_sum(0)
    surface(1)

    kernel_sum(1)
    for k in range(2 * HIST):
        acc = hist[k, 0] * grads[0:AP, :]
        for p in range(1, NM):
            acc = acc + hist[k, p] * grads[grad_row(p) : grad_row(p) + AP, :]
        row = 120 + (k // HIST) * 128 + k % HIST
        grads[row : row + 1, :] = jnp.sum(acc, axis=0, keepdims=True)
    left = jnp.transpose(grads[0:128, :])
    right = jnp.transpose(grads[128:256, :])
    row_lane = lax.broadcasted_iota(jnp.int32, (1, NE), 1)
    vector = jnp.where(
        row_lane >= 120,
        jnp.sum(left, axis=0, keepdims=True),
        jnp.where(row_lane >= 112, pltpu.roll(jnp.sum(right, axis=0, keepdims=True), 120, 1), gram),
    )
    plane_src[...] = vector
    hear(2)
    planes = [
        pltpu.make_async_remote_copy(
            src_ref=plane_src, dst_ref=plane_got.at[k], send_sem=plane_send.at[k], recv_sem=plane_recv.at[k],
            device_id=peer, device_id_type=MESH,
        )
        for k, peer in enumerate(plane_peers)
    ]
    for one in planes:
        one.start()

    half = n_q * share
    for h in range(n_hi):
        gt[h, :, 0:128] = left[h * half : (h + 1) * half]
        gt[h, :, 128:256] = right[h * half : (h + 1) * half]
    firsts = []
    for o in range(1, n_q):
        peer_q = (q_id + o) % n_q
        firsts.append(
            pltpu.make_async_remote_copy(
                src_ref=gt.at[:, pl.ds(pl.multiple_of(peer_q * share, share), share), :],
                dst_ref=rs_got.at[o - 1],
                send_sem=rs_send.at[o - 1], recv_sem=rs_recv.at[o - 1],
                device_id={"shot": hi_id * n_q + peer_q}, device_id_type=MESH,
            )
        )
    for one in firsts:
        one.start()
    final_out = pltpu.make_async_copy(fin.at[:, 0:NB], fin_hbm.at[:, :, 0], fin_sem.at[0])
    final_out.start()

    def turn_history(k, carry):
        for side in range(2):
            block = [hist[k, side * 3 + p] for p in range(3)] + [jnp.zeros((8, NE), F32)]
            turned[:, side * 128 : (side + 1) * 128] = jnp.transpose(jnp.concatenate(block, axis=0))
        hist_t[k] = turned[pl.ds(pl.multiple_of(s_id * share, share), share), :]
        return carry

    lax.fori_loop(0, 2 * HIST, turn_history, 0, unroll=2)

    mine = gt[:, pl.ds(pl.multiple_of(q_id * share, share), share), :]
    for o, one in enumerate(firsts):
        one.wait_recv()
        mine = mine + rs_got[o]
    rs_mid[...] = mine
    seconds = []
    for o in range(1, n_hi):
        seconds.append(
            pltpu.make_async_remote_copy(
                src_ref=rs_mid.at[(hi_id + o) % n_hi],
                dst_ref=rs_last.at[o - 1],
                send_sem=rs_send.at[n_q - 2 + o], recv_sem=rs_recv.at[n_q - 2 + o],
                device_id={"shot": ((hi_id + o) % n_hi) * n_q + q_id}, device_id_type=MESH,
            )
        )
    for one in seconds:
        one.start()

    def collected(value, copies, got):
        sums = [value, None, None, None]
        for k, one in enumerate(copies):
            one.wait_recv()
            at = (k + 1) % 4
            sums[at] = got[k] if sums[at] is None else sums[at] + got[k]
        sums = [one for one in sums if one is not None]
        while len(sums) > 1:
            sums = sums[2:] + [sums[0] + sums[1]]
        return sums[0]

    vector = collected(vector, planes, plane_got)
    line_src[...] = vector
    lines = [
        pltpu.make_async_remote_copy(
            src_ref=line_src, dst_ref=line_got.at[k], send_sem=line_send.at[k], recv_sem=line_recv.at[k],
            device_id=peer, device_id_type=MESH,
        )
        for k, peer in enumerate(line_peers)
    ]
    for one in lines:
        one.start()
    total = rs_mid[hi_id]
    for t in range(2):
        down, up = halo_copies(t)

        @pl.when(has_below)
        def _():
            down.wait_send()

        @pl.when(has_above)
        def _():
            up.wait_send()

    for one in planes + firsts:
        one.wait_send()
    final_out.wait()
    for o, one in enumerate(seconds):
        one.wait_recv()
        total = total + rs_last[o]
    vector = collected(vector, lines, line_got)

    scal[...] = jnp.transpose(jnp.broadcast_to(vector, (NE, NE)))

    def num(k):
        return scal[k : k + 1, :]

    def sy(i, j):
        return num(i * HIST + j)

    over = [1.0 / sy(i, i) for i in range(HIST)]
    gamma = sy(HIST - 1, HIST - 1) / num(yy_row[HIST - 1, HIST - 1])
    alphas = [None] * HIST
    for i in reversed(range(HIST)):
        value = num(120 + i)
        for j in reversed(range(i + 1, HIST)):
            value = value - alphas[j] * sy(i, j)
        alphas[i] = value * over[i]
    rest = []
    for i in range(HIST):
        value = num(112 + i)
        for j in range(HIST):
            value = value - alphas[j] * num(yy_row[i, j])
        value = gamma * value
        for j in range(i):
            value = value + rest[j] * sy(j, i)
        rest.append(alphas[i] - value * over[i])

    sides = []
    for side in range(2):
        lanes = slice(side * 128, (side + 1) * 128)
        acc = -total[:, lanes]
        for i in range(HIST):
            acc = acc + alphas[i] * hist_t[HIST + i, :, lanes]
        acc = gamma * acc
        for i in range(HIST):
            acc = acc - rest[i] * hist_t[i, :, lanes]
        sides.append(acc)
    for p in range(NM):
        at = (p % 3) * AP
        dir_ref[p] = sides[p // 3][:, at : at + NB]

    for one in seconds + lines:
        one.wait_send()


def shards(
    dims,
    adjoint_state,
    forward_states,
    material,
    coupling,
    metric,
    face_normals,
    face_scale,
    face_neighbours,
    face_orientation,
    send_faces,
    history_steps,
    history_changes,
):
    n_hi, n_q, n_x, n_zl = dims
    share = NE // (n_hi * n_q)
    n_plane, n_line = n_q * n_x, n_hi * n_zl
    vmem = pl.BlockSpec(memory_space=pltpu.VMEM)
    hbm = pl.BlockSpec(memory_space=pltpu.HBM)
    dma = pltpu.SemaphoreType.DMA
    i32 = jnp.int32
    final, direction = pl.pallas_call(
        functools.partial(body, dims),
        out_shape=(
            jax.ShapeDtypeStruct((NF, NB, 1, NE), F32),
            jax.ShapeDtypeStruct((NM, share, NB), F32),
        ),
        in_specs=[hbm] * 14,
        out_specs=(hbm, vmem),
        scratch_shapes=[
            pltpu.VMEM((2 * HIST, NM, AP, NE), F32),
            pltpu.VMEM((NF, AP, NE), F32),
            pltpu.VMEM((3, NM, NF, NF), F32),
            pltpu.VMEM((3, 3, NE), F32),
            pltpu.VMEM((3, 4, NE), F32),
            pltpu.VMEM((4, NE), F32),
            pltpu.VMEM((4, NE), i32),
            pltpu.VMEM((4, NE), i32),
            pltpu.VMEM((1, NE), i32),
            pltpu.VMEM((128, 3 * KP), BF16),
            pltpu.VMEM((KP, 192), BF16),
            pltpu.VMEM((NF, KP, NE), F32),
            pltpu.VMEM((2, NF, KP, NE), F32),
            pltpu.VMEM((AP * FP, NE), F32),
            pltpu.VMEM((AP * KP, NE), F32),
            pltpu.VMEM((2, AP * NM * FP, NE), F32),
            pltpu.VMEM((AP * FP, NE), F32),
            pltpu.VMEM((64 * FP, NE), F32),
            pltpu.VMEM((NM, AP, NE), F32),
            pltpu.VMEM((480, 512), BF16),
            pltpu.VMEM((512, NE), BF16),
            pltpu.VMEM((640, 512), BF16),
            pltpu.VMEM((240, 512), F32),
            pltpu.VMEM((2, 8, FP, NE), F32),
            pltpu.VMEM((2, 8, FP, NE), F32),
            pltpu.VMEM((2, 8, FP, NE), F32),
            pltpu.VMEM((2, 8, FP, NE), F32),
            pltpu.VMEM((NM, NE, NE), F32),
            pltpu.VMEM((NM * FP, 3 * KP), BF16),
            pltpu.VMEM((NM * FP, 3 * KP), BF16),
            pltpu.VMEM((256, NE), F32),
            pltpu.VMEM((n_hi, n_q * share, 256), F32),
            pltpu.VMEM((n_q - 1, n_hi, share, 256), F32),
            pltpu.VMEM((n_hi, share, 256), F32),
            pltpu.VMEM((n_hi - 1, share, 256), F32),
            pltpu.VMEM((NE, NE), F32),
            pltpu.VMEM((NE, 256), F32),
            pltpu.VMEM((2 * HIST, share, 256), F32),
            pltpu.VMEM((1, NE), F32),
            pltpu.VMEM((n_plane - 1, 1, NE), F32),
            pltpu.VMEM((1, NE), F32),
            pltpu.VMEM((n_line - 1, 1, NE), F32),
            pltpu.VMEM((NE, NE), F32),
            dma((15,)),
            dma((1,)),
            dma((2, 2)),
            dma((2, 2)),
            dma((n_q + n_hi - 2,)),
            dma((n_q + n_hi - 2,)),
            pltpu.SemaphoreType.REGULAR((3,)),
            dma((n_plane - 1,)),
            dma((n_plane - 1,)),
            dma((n_line - 1,)),
            dma((n_line - 1,)),
        ],
        compiler_params=pltpu.CompilerParams(
            collective_id=0, has_side_effects=True, vmem_limit_bytes=63 * 2**20
        ),
    )(
        jnp.transpose(adjoint_state, (1, 2, 0, 3)), jnp.transpose(forward_states[0], (1, 2, 0, 3)),
        material, history_steps, history_changes,
        coupling, metric, face_normals, face_scale, face_neighbours, face_orientation,
        send_faces.reshape(1, -1), jnp.asarray(deriv_table()), jnp.asarray(lift_table()),
    )
    return jnp.transpose(final, (2, 0, 1, 3)), jnp.transpose(direction, (0, 2, 1))


def dims_of(mesh):
    n_shot, n_mesh = mesh.shape["shot"], mesh.shape["mesh"]
    n_x = 4 if n_mesh >= 16 else 2
    return 2, n_shot // 2, n_x, n_mesh // n_x


def solution(mesh):
    placed = (
        P("shot", None, None, "mesh"),
        P("shot", None, None, None, "mesh"),
        P(None, None, "mesh"),
        P(),
        P(None, None, "mesh"),
        P(None, None, "mesh"),
        P(None, "mesh"),
        P(None, "mesh"),
        P(None, "mesh"),
        P("mesh"),
        P(None, None, None, "mesh"),
        P(None, None, None, "mesh"),
    )
    return jax.shard_map(
        functools.partial(shards, dims_of(mesh)),
        mesh=mesh,
        in_specs=placed,
        out_specs=(P("shot", None, None, "mesh"), P(None, None, ("mesh", "shot"))),
        check_vma=False,
    )
```

```python
import functools
import math

import jax
import jax.numpy as jnp
import ml_dtypes
import numpy as np
from jax import lax
from jax.experimental import pallas as pl
from jax.experimental.pallas import tpu as pltpu
from jax.sharding import PartitionSpec as P

F32 = jnp.float32
BF16 = jnp.bfloat16
STEP_SIZE = 0.02
MESH = pl.DeviceIdType.MESH

NF = 13
FP = 16
NB = 35
AP = 40
KP = 48
NFN = 15
NM = 6
NE = 128
HIST = 5


def invert_matrix(matrix):
    order_count = matrix.shape[0]
    working = np.concatenate([matrix * 1.0, np.eye(order_count)], axis=1)
    for column in range(order_count):
        pivot_row = column + int(np.argmax(np.abs(working[column:, column])))
        working[[column, pivot_row]] = working[[pivot_row, column]]
        working[column] = working[column] / working[column, column]
        for target in range(order_count):
            if target != column:
                working[target] = working[target] - working[target, column] * working[column]
    return working[:, order_count:]


def basis_tables():
    points = [
        (across, along, upward)
        for upward in range(5)
        for along in range(5 - upward)
        for across in range(5 - upward - along)
    ]
    exponents = np.array(points) * 1.0
    coords = exponents / 4.0
    vander = np.prod(coords[:, None, :] ** exponents[None, :, :], axis=2)
    inverse = invert_matrix(vander)
    derivs = []
    for direction_axis in range(3):
        lowered = np.maximum(exponents - np.eye(3)[direction_axis], 0.0)
        slopes = exponents[None, :, direction_axis] * np.prod(
            coords[:, None, :] ** lowered[None, :, :], axis=2
        )
        derivs.append(slopes @ inverse)
    moments = np.array(
        [
            [
                math.factorial(first[0] + second[0])
                * math.factorial(first[1] + second[1])
                * math.factorial(first[2] + second[2])
                / math.factorial(sum(first) + sum(second) + 3)
                for second in points
            ]
            for first in points
        ]
    )
    mass_matrix = inverse.T @ moments @ inverse
    lattice = [(across, along) for along in range(5) for across in range(5 - along)]
    lattice_powers = np.array(lattice) * 1.0
    face_vander = np.prod((lattice_powers / 4.0)[:, None, :] ** lattice_powers[None, :, :], axis=2)
    face_inverse = invert_matrix(face_vander)
    face_moments = np.array(
        [
            [
                math.factorial(first[0] + second[0])
                * math.factorial(first[1] + second[1])
                / math.factorial(sum(first) + sum(second) + 2)
                for second in lattice
            ]
            for first in lattice
        ]
    )
    face_mass = face_inverse.T @ face_moments @ face_inverse
    numbers = {point: number for number, point in enumerate(points)}
    face_points = [
        [(across, along, 0) for across, along in lattice],
        [(across, 0, along) for across, along in lattice],
        [(0, across, along) for across, along in lattice],
        [(across, along, 4 - across - along) for across, along in lattice],
    ]
    face_nodes = np.array(
        [[numbers[point] for point in listing] for listing in face_points], np.int32
    )
    mass_inverse = invert_matrix(mass_matrix)
    lift_tables = []
    for face_number in range(4):
        selector = np.eye(35)[face_nodes[face_number]]
        lift_tables.append(mass_inverse @ selector.T @ face_mass)
    orderings = [(0, 1, 2), (1, 2, 0), (2, 0, 1), (1, 0, 2), (0, 2, 1), (2, 1, 0)]
    lattice_numbers = {point: number for number, point in enumerate(lattice)}
    triples = [(across, along, 4 - across - along) for across, along in lattice]
    turn_nodes = np.array(
        [
            [lattice_numbers[triple[ordering[0]], triple[ordering[1]]] for triple in triples]
            for ordering in orderings
        ],
        np.int32,
    )
    return (
        np.stack(derivs).astype(np.float32),
        np.stack(lift_tables).astype(np.float32),
        face_nodes,
        turn_nodes,
    )


DERIVS, LIFTS, FACE_NODES, TURN = basis_tables()


def np_split(table):
    high = table.astype(ml_dtypes.bfloat16)
    low = (table - high.astype(np.float32)).astype(ml_dtypes.bfloat16)
    return np.concatenate([high, high, low], axis=1)


def deriv_table():
    table = np.zeros((128, KP), np.float32)
    for r in range(3):
        table[r * AP : r * AP + NB, :NB] = DERIVS[r]
    return np_split(table)


def lift_table():
    table = np.zeros((KP, 64), np.float32)
    for x in range(4):
        table[:NB, x * 16 : x * 16 + NFN] = LIFTS[x]
    return np_split(table)


def split(x):
    high = x.astype(BF16)
    low = (x - high.astype(F32)).astype(BF16)
    return high, low


def stack3(x):
    high, low = split(x)
    return jnp.concatenate([high, low, high], axis=0)


def mm(a, b):
    return jnp.dot(a, b, preferred_element_type=F32)


def grad_row(p):
    return (p // 3) * 128 + (p % 3) * AP


def body(
    dims,
    adj_hbm, fwd_hbm, mat_hbm, hs_hbm, hy_hbm,
    cpl_hbm, metric_hbm, normals_hbm, scale_hbm, nbr_hbm, orient_hbm, send_hbm, deriv3_hbm, lift3_hbm,
    fin_hbm, dir_ref,
    hist, fin, cpl, metric, normals, scale, nbr, orient, send, deriv3, lift3,
    lam_b, fwd_b, lam_a, spat, mixg, vol, flux, matp,
    trace, oh_send, oh_nbr, outer,
    msg_d, msg_u, got_d, got_u,
    padded, ct_v, ct_g,
    grads, gt, rs_got, rs_mid, rs_last, prods, turned, hist_t,
    plane_src, plane_got, line_src, line_got, scal,
    load_sem, fin_sem, halo_send, halo_recv, rs_send, rs_recv, known, plane_send, plane_recv, line_send, line_recv,
):
    n_hi, n_q, n_x, n_zl = dims
    n_shot, n_mesh = n_hi * n_q, n_x * n_zl
    n_plane, n_line = n_q * n_x, n_hi * n_zl
    share = NE // n_shot
    s_id = lax.axis_index("shot")
    m_id = lax.axis_index("mesh")
    hi_id, q_id = s_id // n_q, s_id % n_q
    zl_id, x_id = m_id // n_x, m_id % n_x
    has_below = m_id > 0
    has_above = m_id < n_mesh - 1

    plane_peers, line_peers = [], []
    for k in range(1, n_plane):
        other = (q_id * n_x + x_id + k) % n_plane
        plane_peers.append({"shot": hi_id * n_q + other // n_x, "mesh": zl_id * n_x + other % n_x})
    for k in range(1, n_line):
        other = (hi_id * n_zl + zl_id + k) % n_line
        line_peers.append({"shot": (other // n_zl) * n_q + q_id, "mesh": (other % n_zl) * n_x + x_id})

    barrier = pltpu.get_barrier_semaphore()

    @pl.when(has_below)
    def _():
        pl.semaphore_signal(barrier, inc=1, device_id={"mesh": m_id - 1}, device_id_type=MESH)

    @pl.when(has_above)
    def _():
        pl.semaphore_signal(barrier, inc=1, device_id={"mesh": m_id + 1}, device_id_type=MESH)

    def at_plane(step_x, step_q, flip):
        y_id, c_id = q_id // 2, q_id % 2
        other_q = ((y_id + step_q) % (n_q // 2)) * 2 + (c_id + flip) % 2
        return {"shot": hi_id * n_q + other_q, "mesh": zl_id * n_x + (x_id + step_x) % n_x}

    def at_line(step):
        return line_peers[step % n_line - 1]

    core = at_plane(0, 0, 1)
    rounds = [
        [core, at_plane(1, 0, 0), at_plane(n_x - 1, 0, 0), at_plane(0, 1, 0), at_plane(0, n_q // 2 - 1, 0), at_line(1), at_line(-1)],
        [at_plane(2, 0, 0), at_plane(0, 2, 0), at_line(2), at_line(-2)],
        [core, at_line(4), at_line(-4)],
    ]
    for peer in rounds[0]:
        pl.semaphore_signal(barrier, inc=1, device_id=peer, device_id_type=MESH)

    def tell(k):
        for peer in rounds[k]:
            pl.semaphore_signal(known.at[k], inc=1, device_id=peer, device_id_type=MESH)

    def hear(k):
        pl.semaphore_wait(known.at[k], len(rounds[k]))

    for f in range(NF):
        lam_b[f, 32:KP, :] = jnp.zeros((KP - 32, NE), F32)
    pairs = [
        (adj_hbm.at[:, :, 0], lam_b.at[:, 0:NB]),
        (send_hbm, send),
        (deriv3_hbm, deriv3),
        (metric_hbm, metric),
        (cpl_hbm, cpl),
        (mat_hbm, matp.at[:, 0:NB]),
        (nbr_hbm, nbr),
        (orient_hbm, orient),
        (normals_hbm, normals),
        (scale_hbm, scale),
        (fwd_hbm.at[:, :, 0], fwd_b.at[0, :, 0:NB]),
        (lift3_hbm, lift3),
        (fwd_hbm.at[:, :, 1], fwd_b.at[1, :, 0:NB]),
        (hs_hbm, hist.at[0:HIST, :, 0:NB]),
        (hy_hbm, hist.at[HIST : 2 * HIST, :, 0:NB]),
    ]
    loads = [pltpu.make_async_copy(src, dst, load_sem.at[k]) for k, (src, dst) in enumerate(pairs)]
    loads[0].start()
    loads[1].start()
    matp[:, 32:AP, :] = jnp.zeros((NM, AP - 32, NE), F32)
    for t in range(2):
        for f in range(NF):
            fwd_b[t, f, 32:KP, :] = jnp.zeros((KP - 32, NE), F32)
    for k in range(2 * HIST):
        hist[k, :, 32:AP, :] = jnp.zeros((NM, AP - 32, NE), F32)
    for one in loads[2:]:
        one.start()

    lam_a[...] = jnp.zeros(lam_a.shape, F32)
    grads[120:128, :] = jnp.zeros((8, NE), F32)
    grads[248:256, :] = jnp.zeros((8, NE), F32)

    @pl.when(jnp.logical_not(has_below))
    def _():
        got_u[...] = jnp.zeros(got_u.shape, F32)

    @pl.when(jnp.logical_not(has_above))
    def _():
        got_d[...] = jnp.zeros(got_d.shape, F32)

    lane = lax.broadcasted_iota(jnp.int32, (FP, NE), 1)
    low_half = lane < 64
    filled = lax.broadcasted_iota(jnp.int32, (FP, NE), 0) < NF

    def derivative(field):
        for first in range(0, NF, 2):
            group = range(first, min(first + 2, NF))
            out = mm(deriv3[...], jnp.concatenate([stack3(field[f]) for f in group], axis=1))
            for i, f in enumerate(group):
                slab = [out[r * AP : (r + 1) * AP, i * NE : (i + 1) * NE] for r in range(3)]
                for d in range(3):
                    s = metric[0, d : d + 1, :] * slab[0]
                    s = s + metric[1, d : d + 1, :] * slab[1]
                    s = s + metric[2, d : d + 1, :] * slab[2]
                    spat[pl.ds(d * FP + f, AP, stride=KP), :] = s

    def mixed(table, base):
        parts = []
        for j in range(8):
            at = pl.multiple_of((base + j) * KP, KP)
            parts.append(stack3(spat[pl.ds(at, KP), :]))
        return mm(table[...], jnp.concatenate(parts, axis=1))

    def volume():
        derivative(lam_b)

        def block(i, carry):
            base = pl.multiple_of(i * 8, 8)
            mix = mixed(ct_v, base)
            params = [matp[p, pl.ds(base, 8), :] for p in range(NM)]
            for j in range(8):
                acc = params[0][j : j + 1, :] * mix[0:FP, j * NE : (j + 1) * NE]
                for p in range(1, NM):
                    acc = acc + params[p][j : j + 1, :] * mix[p * FP : (p + 1) * FP, j * NE : (j + 1) * NE]
                vol[pl.ds(pl.multiple_of((base + j) * FP, FP), FP), :] = acc
            return carry

        lax.fori_loop(0, AP // 8, block, 0, unroll=True)

    def forward_mix(t):
        derivative(fwd_b.at[t])

        def block(i, carry):
            base = pl.multiple_of(i * 8, 8)
            mix = mixed(ct_g, base)
            for j in range(8):
                at = pl.multiple_of((base + j) * NM * FP, NM * FP)
                mixg[t, pl.ds(at, NM * FP), :] = mix[:, j * NE : (j + 1) * NE]
            return carry

        lax.fori_loop(0, AP // 8, block, 0, unroll=True)

    sub_row = lax.broadcasted_iota(jnp.int32, (8, NE), 0)

    def tree(tiles):
        for step in (4, 2, 1):
            upper = (sub_row // step) % 2 == 1
            half = len(tiles) // 2
            merged = []
            for one, two in zip(tiles[:half], tiles[half:]):
                one = one + pltpu.roll(one, 8 - step, 0)
                two = two + pltpu.roll(two, step, 0)
                merged.append(jnp.where(upper, two, one))
            tiles = merged
        return tiles[0]

    def kernel_sum(t):
        def block(i, carry):
            base = pl.multiple_of(i * 8, 8)
            for p in range(NM):
                tiles = []
                for j in range(8):
                    lam = lam_a[pl.ds(pl.multiple_of((base + j) * FP, FP), FP), :]
                    at = pl.ds(pl.multiple_of((base + j) * NM * FP + p * FP, FP), FP)
                    both = mixg[t, at, :] * lam
                    tiles.append(both[0:8] + both[8:16])
                at = pl.ds(pl.multiple_of(grad_row(p) + base, 8), 8)
                part = tree(tiles) * STEP_SIZE
                grads[at, :] = part if t == 0 else grads[at, :] + part
            return carry

        lax.fori_loop(0, AP // 8, block, 0, unroll=True)

    def inner_of(n, x):
        at = int(FACE_NODES[x][n]) * FP
        return lam_a[at : at + FP, :]

    def halo_copies(t):
        down = pltpu.make_async_remote_copy(
            src_ref=msg_d.at[t, :, 0:NF], dst_ref=got_d.at[t, :, 0:NF], send_sem=halo_send.at[t, 0], recv_sem=halo_recv.at[t, 0],
            device_id={"mesh": m_id - 1}, device_id_type=MESH,
        )
        up = pltpu.make_async_remote_copy(
            src_ref=msg_u.at[t, :, 0:NF], dst_ref=got_u.at[t, :, 0:NF], send_sem=halo_send.at[t, 1], recv_sem=halo_recv.at[t, 1],
            device_id={"mesh": m_id + 1}, device_id_type=MESH,
        )
        return down, up

    def send_traces(t):
        for n in range(NFN):
            for x in range(4):
                high, low = split(inner_of(n, x))
                trace[n * FP : (n + 1) * FP, x * NE : (x + 1) * NE] = high
                trace[240 + n * FP : 240 + (n + 1) * FP, x * NE : (x + 1) * NE] = low
        both = mm(trace[...], oh_send[...])
        picked = both[0:240] + both[240:480]
        for j in range(8):
            first = picked[j * FP : (j + 1) * FP]
            if j < 7:
                second = picked[(j + 8) * FP : (j + 9) * FP]
            else:
                second = jnp.zeros((FP, NE), F32)
            msg_d[t, j] = jnp.where(low_half, first, pltpu.roll(second, 64, 1))
            msg_u[t, j] = jnp.where(low_half, pltpu.roll(first, 64, 1), second)
        if t == 0:
            n_wait = len(rounds[0])
            pl.semaphore_wait(barrier, n_wait + has_below.astype(jnp.int32) + has_above.astype(jnp.int32))
        down, up = halo_copies(t)

        @pl.when(has_below)
        def _():
            down.start()

        @pl.when(has_above)
        def _():
            up.start()

        if t == 0:
            tell(0)

    def gather_local():
        local = mm(trace[...], oh_nbr[0:512, :])
        outer[...] = local[0:240] + local[240:480]

    def surface(t):
        down, up = halo_copies(t)

        @pl.when(has_above)
        def _():
            down.wait_recv()

        @pl.when(has_below)
        def _():
            up.wait_recv()

        tops, bottoms = [], []
        for j in range(8):
            above = jnp.where(filled, got_d[t, j], 0.0)
            below = jnp.where(filled, got_u[t, j], 0.0)
            tops.append(jnp.where(low_half, below, pltpu.roll(above, 64, 1)))
            bottoms.append(jnp.where(low_half, pltpu.roll(below, 64, 1), above))
        ghosts = jnp.concatenate(tops + bottoms[:7], axis=0)
        high, low = split(ghosts)
        part = mm(jnp.concatenate([high, low], axis=0), oh_nbr[512:640, :])
        outer[...] = outer[...] + (part[0:240] + part[240:480])

        turns = [jnp.broadcast_to(orient[x : x + 1, :], (FP, NE)) for x in range(4)]
        halves = [0.5 * scale[x : x + 1, :] for x in range(4)]
        for n in range(NFN):
            sources = {}
            for o in range(6):
                sources.setdefault(int(TURN[o][n]), []).append(o)
            sources = list(sources.items())
            jumps, weighted = [], []
            for x in range(4):
                at = sources[0][0] * FP
                value = outer[at : at + FP, x * NE : (x + 1) * NE]
                for node, options in sources[1:]:
                    mask = turns[x] == options[0]
                    for o in options[1:]:
                        mask = mask | (turns[x] == o)
                    value = jnp.where(mask, outer[node * FP : (node + 1) * FP, x * NE : (x + 1) * NE], value)
                jump = value - inner_of(n, x)
                jumps.append(jump)
                weighted.append(
                    stack3(jnp.concatenate([normals[d, x : x + 1, :] * jump for d in range(3)], axis=0))
                )
            mix = mm(ct_v[...], jnp.concatenate(weighted, axis=1))
            for x in range(4):
                node = int(FACE_NODES[x][n])
                acc = jumps[x]
                for p in range(NM):
                    acc = acc + matp[p, node : node + 1, :] * mix[p * FP : (p + 1) * FP, x * NE : (x + 1) * NE]
                at = (x * 16 + n) * FP
                flux[at : at + FP, :] = acc * halves[x]

        for first in range(0, NF, 2):
            group = range(first, min(first + 2, NF))
            rhs = [stack3(flux[pl.ds(g, 64, stride=FP), :]) for g in group]
            out = mm(lift3[...], jnp.concatenate(rhs, axis=1))
            for i, g in enumerate(group):
                change = out[0:AP, i * NE : (i + 1) * NE] + vol[pl.ds(g, AP, stride=FP), :]
                new = lam_b[g, 0:AP, :] + STEP_SIZE * change
                if t == 0:
                    lam_b[g, 0:AP, :] = new
                else:
                    fin[g] = new
                lam_a[pl.ds(g, AP, stride=FP), :] = new

    yy_row = {}
    for i in range(HIST):
        for j in range(i, HIST):
            yy_row[i, j] = yy_row[j, i] = 25 + len([k for k in yy_row if k[0] <= k[1]])

    def dot_rows(i, j):
        acc = hist[i, 0] * hist[j, 0]
        for p in range(1, NM):
            acc = acc + hist[i, p] * hist[j, p]
        return jnp.sum(acc, axis=0, keepdims=True)

    def history():
        prods[...] = jnp.zeros(prods.shape, F32)
        for i in range(HIST):
            for j in range(HIST):
                row = i * HIST + j
                prods[row : row + 1, :] = dot_rows(i, HIST + j)
                if j >= i:
                    row = yy_row[i, j]
                    prods[row : row + 1, :] = dot_rows(HIST + i, HIST + j)

    def selections():
        for k in (6, 7):
            loads[k].wait()
        rows_n = lax.broadcasted_iota(jnp.int32, (640, NE), 0)
        for x in range(4):
            oh_nbr[:, x * NE : (x + 1) * NE] = jnp.where(rows_n == nbr[x : x + 1, :], 1.0, 0.0).astype(BF16)

    def tables():
        loads[4].wait()
        padded[...] = jnp.zeros(padded.shape, F32)
        for p in range(NM):
            for d in range(3):
                padded[p, d * FP : d * FP + NF, 0:NF] = cpl[d, p]
        for p in range(NM):
            flipped = jnp.transpose(padded[p])[0:FP]
            straight = padded[p, 0:FP]
            for d in range(1, 3):
                straight = straight + pltpu.roll(padded[p, d * FP : (d + 1) * FP], d * FP, 1)
            for block, dst in ((flipped, ct_v), (straight, ct_g)):
                high = block.astype(BF16).astype(F32)
                low = pltpu.roll(block - high, 2 * KP, 1)
                first = jnp.where(lane < KP, high, jnp.where(lane < 2 * KP, pltpu.roll(high, KP, 1), low))
                dst[p * FP : (p + 1) * FP, 0:NE] = first.astype(BF16)
                dst[p * FP : (p + 1) * FP, NE : 3 * KP] = low[:, 0 : 3 * KP - NE].astype(BF16)

    def clear(i, carry):
        spat[pl.ds(pl.multiple_of(i * KP, KP), KP), :] = jnp.zeros((KP, NE), F32)
        return carry

    loads[1].wait()
    rows_s = lax.broadcasted_iota(jnp.int32, (512, NE), 0)
    oh_send[...] = jnp.where(rows_s == send[...], 1.0, 0.0).astype(BF16)
    loads[0].wait()
    for f in range(NF):
        lam_a[pl.ds(f, AP, stride=FP), :] = lam_b[f, 0:AP, :]
    send_traces(0)
    tables()
    lax.fori_loop(0, AP, clear, 0, unroll=8)
    for x in range(4):
        flux[(x * 16 + 15) * FP : (x * 16 + 16) * FP, :] = jnp.zeros((FP, NE), F32)
    for k in (2, 3, 5):
        loads[k].wait()
    volume()
    selections()
    gather_local()
    loads[10].wait()
    forward_mix(0)
    for k in (13, 14):
        loads[k].wait()
    history()
    gram = jnp.sum(jnp.transpose(prods[...]), axis=0, keepdims=True) * (1.0 / n_shot)
    for k in (8, 9, 11):
        loads[k].wait()
    surface(0)
    send_traces(1)
    hear(0)
    tell(1)
    gather_local()
    volume()
    hear(1)
    tell(2)
    loads[12].wait()
    forward_mix(1)
    kernel_sum(0)
    surface(1)

    kernel_sum(1)
    for k in range(2 * HIST):
        acc = hist[k, 0] * grads[0:AP, :]
        for p in range(1, NM):
            acc = acc + hist[k, p] * grads[grad_row(p) : grad_row(p) + AP, :]
        row = 120 + (k // HIST) * 128 + k % HIST
        grads[row : row + 1, :] = jnp.sum(acc, axis=0, keepdims=True)
    left = jnp.transpose(grads[0:128, :])
    right = jnp.transpose(grads[128:256, :])
    row_lane = lax.broadcasted_iota(jnp.int32, (1, NE), 1)
    vector = jnp.where(
        row_lane >= 120,
        jnp.sum(left, axis=0, keepdims=True),
        jnp.where(row_lane >= 112, pltpu.roll(jnp.sum(right, axis=0, keepdims=True), 120, 1), gram),
    )
    plane_src[...] = vector
    hear(2)
    planes = [
        pltpu.make_async_remote_copy(
            src_ref=plane_src, dst_ref=plane_got.at[k], send_sem=plane_send.at[k], recv_sem=plane_recv.at[k],
            device_id=peer, device_id_type=MESH,
        )
        for k, peer in enumerate(plane_peers)
    ]
    for one in planes:
        one.start()

    half = n_q * share
    for h in range(n_hi):
        gt[h, :, 0:128] = left[h * half : (h + 1) * half]
        gt[h, :, 128:256] = right[h * half : (h + 1) * half]
    firsts = []
    for o in range(1, n_q):
        peer_q = (q_id + o) % n_q
        firsts.append(
            pltpu.make_async_remote_copy(
                src_ref=gt.at[:, pl.ds(pl.multiple_of(peer_q * share, share), share), :],
                dst_ref=rs_got.at[o - 1],
                send_sem=rs_send.at[o - 1], recv_sem=rs_recv.at[o - 1],
                device_id={"shot": hi_id * n_q + peer_q}, device_id_type=MESH,
            )
        )
    for one in firsts:
        one.start()
    final_out = pltpu.make_async_copy(fin.at[:, 0:NB], fin_hbm.at[:, :, 0], fin_sem.at[0])
    final_out.start()

    def turn_history(k, carry):
        for side in range(2):
            block = [hist[k, side * 3 + p] for p in range(3)] + [jnp.zeros((8, NE), F32)]
            turned[:, side * 128 : (side + 1) * 128] = jnp.transpose(jnp.concatenate(block, axis=0))
        hist_t[k] = turned[pl.ds(pl.multiple_of(s_id * share, share), share), :]
        return carry

    lax.fori_loop(0, 2 * HIST, turn_history, 0, unroll=2)

    def collected(value, copies, got):
        sums = [value, None, None, None]
        for k, one in enumerate(copies):
            one.wait_recv()
            at = (k + 1) % 4
            sums[at] = got[k] if sums[at] is None else sums[at] + got[k]
        sums = [one for one in sums if one is not None]
        while len(sums) > 1:
            sums = sums[2:] + [sums[0] + sums[1]]
        return sums[0]

    vector = collected(vector, planes, plane_got)
    line_src[...] = vector
    lines = [
        pltpu.make_async_remote_copy(
            src_ref=line_src, dst_ref=line_got.at[k], send_sem=line_send.at[k], recv_sem=line_recv.at[k],
            device_id=peer, device_id_type=MESH,
        )
        for k, peer in enumerate(line_peers)
    ]
    for one in lines:
        one.start()
    mine = gt[:, pl.ds(pl.multiple_of(q_id * share, share), share), :]
    for o, one in enumerate(firsts):
        one.wait_recv()
        mine = mine + rs_got[o]
    rs_mid[...] = mine
    seconds = []
    for o in range(1, n_hi):
        seconds.append(
            pltpu.make_async_remote_copy(
                src_ref=rs_mid.at[(hi_id + o) % n_hi],
                dst_ref=rs_last.at[o - 1],
                send_sem=rs_send.at[n_q - 2 + o], recv_sem=rs_recv.at[n_q - 2 + o],
                device_id={"shot": ((hi_id + o) % n_hi) * n_q + q_id}, device_id_type=MESH,
            )
        )
    for one in seconds:
        one.start()
    total = rs_mid[hi_id]
    for t in range(2):
        down, up = halo_copies(t)

        @pl.when(has_below)
        def _():
            down.wait_send()

        @pl.when(has_above)
        def _():
            up.wait_send()

    for one in planes + firsts:
        one.wait_send()
    final_out.wait()
    for o, one in enumerate(seconds):
        one.wait_recv()
        total = total + rs_last[o]
    vector = collected(vector, lines, line_got)

    scal[...] = jnp.transpose(jnp.broadcast_to(vector, (NE, NE)))

    def num(k):
        return scal[k : k + 1, :]

    def sy(i, j):
        return num(i * HIST + j)

    over = [1.0 / sy(i, i) for i in range(HIST)]
    gamma = sy(HIST - 1, HIST - 1) / num(yy_row[HIST - 1, HIST - 1])
    alphas = [None] * HIST
    for i in reversed(range(HIST)):
        value = num(120 + i)
        for j in reversed(range(i + 1, HIST)):
            value = value - alphas[j] * sy(i, j)
        alphas[i] = value * over[i]
    rest = []
    for i in range(HIST):
        value = num(112 + i)
        for j in range(HIST):
            value = value - alphas[j] * num(yy_row[i, j])
        value = gamma * value
        for j in range(i):
            value = value + rest[j] * sy(j, i)
        rest.append(alphas[i] - value * over[i])

    sides = []
    for side in range(2):
        lanes = slice(side * 128, (side + 1) * 128)
        acc = -total[:, lanes]
        for i in range(HIST):
            acc = acc + alphas[i] * hist_t[HIST + i, :, lanes]
        acc = gamma * acc
        for i in range(HIST):
            acc = acc - rest[i] * hist_t[i, :, lanes]
        sides.append(acc)
    for p in range(NM):
        at = (p % 3) * AP
        dir_ref[p] = sides[p // 3][:, at : at + NB]

    for one in seconds + lines:
        one.wait_send()


def shards(
    dims,
    adjoint_state,
    forward_states,
    material,
    coupling,
    metric,
    face_normals,
    face_scale,
    face_neighbours,
    face_orientation,
    send_faces,
    history_steps,
    history_changes,
):
    n_hi, n_q, n_x, n_zl = dims
    share = NE // (n_hi * n_q)
    n_plane, n_line = n_q * n_x, n_hi * n_zl
    vmem = pl.BlockSpec(memory_space=pltpu.VMEM)
    hbm = pl.BlockSpec(memory_space=pltpu.HBM)
    dma = pltpu.SemaphoreType.DMA
    i32 = jnp.int32
    final, direction = pl.pallas_call(
        functools.partial(body, dims),
        out_shape=(
            jax.ShapeDtypeStruct((NF, NB, 1, NE), F32),
            jax.ShapeDtypeStruct((NM, share, NB), F32),
        ),
        in_specs=[hbm] * 14,
        out_specs=(hbm, vmem),
        scratch_shapes=[
            pltpu.VMEM((2 * HIST, NM, AP, NE), F32),
            pltpu.VMEM((NF, AP, NE), F32),
            pltpu.VMEM((3, NM, NF, NF), F32),
            pltpu.VMEM((3, 3, NE), F32),
            pltpu.VMEM((3, 4, NE), F32),
            pltpu.VMEM((4, NE), F32),
            pltpu.VMEM((4, NE), i32),
            pltpu.VMEM((4, NE), i32),
            pltpu.VMEM((1, NE), i32),
            pltpu.VMEM((128, 3 * KP), BF16),
            pltpu.VMEM((KP, 192), BF16),
            pltpu.VMEM((NF, KP, NE), F32),
            pltpu.VMEM((2, NF, KP, NE), F32),
            pltpu.VMEM((AP * FP, NE), F32),
            pltpu.VMEM((AP * KP, NE), F32),
            pltpu.VMEM((2, AP * NM * FP, NE), F32),
            pltpu.VMEM((AP * FP, NE), F32),
            pltpu.VMEM((64 * FP, NE), F32),
            pltpu.VMEM((NM, AP, NE), F32),
            pltpu.VMEM((480, 512), BF16),
            pltpu.VMEM((512, NE), BF16),
            pltpu.VMEM((640, 512), BF16),
            pltpu.VMEM((240, 512), F32),
            pltpu.VMEM((2, 8, FP, NE), F32),
            pltpu.VMEM((2, 8, FP, NE), F32),
            pltpu.VMEM((2, 8, FP, NE), F32),
            pltpu.VMEM((2, 8, FP, NE), F32),
            pltpu.VMEM((NM, NE, NE), F32),
            pltpu.VMEM((NM * FP, 3 * KP), BF16),
            pltpu.VMEM((NM * FP, 3 * KP), BF16),
            pltpu.VMEM((256, NE), F32),
            pltpu.VMEM((n_hi, n_q * share, 256), F32),
            pltpu.VMEM((n_q - 1, n_hi, share, 256), F32),
            pltpu.VMEM((n_hi, share, 256), F32),
            pltpu.VMEM((n_hi - 1, share, 256), F32),
            pltpu.VMEM((NE, NE), F32),
            pltpu.VMEM((NE, 256), F32),
            pltpu.VMEM((2 * HIST, share, 256), F32),
            pltpu.VMEM((1, NE), F32),
            pltpu.VMEM((n_plane - 1, 1, NE), F32),
            pltpu.VMEM((1, NE), F32),
            pltpu.VMEM((n_line - 1, 1, NE), F32),
            pltpu.VMEM((NE, NE), F32),
            dma((15,)),
            dma((1,)),
            dma((2, 2)),
            dma((2, 2)),
            dma((n_q + n_hi - 2,)),
            dma((n_q + n_hi - 2,)),
            pltpu.SemaphoreType.REGULAR((3,)),
            dma((n_plane - 1,)),
            dma((n_plane - 1,)),
            dma((n_line - 1,)),
            dma((n_line - 1,)),
        ],
        compiler_params=pltpu.CompilerParams(
            collective_id=0, has_side_effects=True, vmem_limit_bytes=63 * 2**20
        ),
    )(
        jnp.transpose(adjoint_state, (1, 2, 0, 3)), jnp.transpose(forward_states[0], (1, 2, 0, 3)),
        material, history_steps, history_changes,
        coupling, metric, face_normals, face_scale, face_neighbours, face_orientation,
        send_faces.reshape(1, -1), jnp.asarray(deriv_table()), jnp.asarray(lift_table()),
    )
    return jnp.transpose(final, (2, 0, 1, 3)), jnp.transpose(direction, (0, 2, 1))


def dims_of(mesh):
    n_shot, n_mesh = mesh.shape["shot"], mesh.shape["mesh"]
    n_x = 4 if n_mesh >= 16 else 2
    return 2, n_shot // 2, n_x, n_mesh // n_x


def solution(mesh):
    placed = (
        P("shot", None, None, "mesh"),
        P("shot", None, None, None, "mesh"),
        P(None, None, "mesh"),
        P(),
        P(None, None, "mesh"),
        P(None, None, "mesh"),
        P(None, "mesh"),
        P(None, "mesh"),
        P(None, "mesh"),
        P("mesh"),
        P(None, None, None, "mesh"),
        P(None, None, None, "mesh"),
    )
    return jax.shard_map(
        functools.partial(shards, dims_of(mesh)),
        mesh=mesh,
        in_specs=placed,
        out_specs=(P("shot", None, None, "mesh"), P(None, None, ("mesh", "shot"))),
        check_vma=False,
    )
```

```python
import functools
import math

import jax
import jax.numpy as jnp
import ml_dtypes
import numpy as np
from jax import lax
from jax.experimental import pallas as pl
from jax.experimental.pallas import tpu as pltpu
from jax.sharding import PartitionSpec as P

F32 = jnp.float32
BF16 = jnp.bfloat16
STEP_SIZE = 0.02
MESH = pl.DeviceIdType.MESH

NF = 13
FP = 16
NB = 35
AP = 40
KP = 48
NFN = 15
NM = 6
NE = 128
HIST = 5


def invert_matrix(matrix):
    order_count = matrix.shape[0]
    working = np.concatenate([matrix * 1.0, np.eye(order_count)], axis=1)
    for column in range(order_count):
        pivot_row = column + int(np.argmax(np.abs(working[column:, column])))
        working[[column, pivot_row]] = working[[pivot_row, column]]
        working[column] = working[column] / working[column, column]
        for target in range(order_count):
            if target != column:
                working[target] = working[target] - working[target, column] * working[column]
    return working[:, order_count:]


def basis_tables():
    points = [
        (across, along, upward)
        for upward in range(5)
        for along in range(5 - upward)
        for across in range(5 - upward - along)
    ]
    exponents = np.array(points) * 1.0
    coords = exponents / 4.0
    vander = np.prod(coords[:, None, :] ** exponents[None, :, :], axis=2)
    inverse = invert_matrix(vander)
    derivs = []
    for direction_axis in range(3):
        lowered = np.maximum(exponents - np.eye(3)[direction_axis], 0.0)
        slopes = exponents[None, :, direction_axis] * np.prod(
            coords[:, None, :] ** lowered[None, :, :], axis=2
        )
        derivs.append(slopes @ inverse)
    moments = np.array(
        [
            [
                math.factorial(first[0] + second[0])
                * math.factorial(first[1] + second[1])
                * math.factorial(first[2] + second[2])
                / math.factorial(sum(first) + sum(second) + 3)
                for second in points
            ]
            for first in points
        ]
    )
    mass_matrix = inverse.T @ moments @ inverse
    lattice = [(across, along) for along in range(5) for across in range(5 - along)]
    lattice_powers = np.array(lattice) * 1.0
    face_vander = np.prod((lattice_powers / 4.0)[:, None, :] ** lattice_powers[None, :, :], axis=2)
    face_inverse = invert_matrix(face_vander)
    face_moments = np.array(
        [
            [
                math.factorial(first[0] + second[0])
                * math.factorial(first[1] + second[1])
                / math.factorial(sum(first) + sum(second) + 2)
                for second in lattice
            ]
            for first in lattice
        ]
    )
    face_mass = face_inverse.T @ face_moments @ face_inverse
    numbers = {point: number for number, point in enumerate(points)}
    face_points = [
        [(across, along, 0) for across, along in lattice],
        [(across, 0, along) for across, along in lattice],
        [(0, across, along) for across, along in lattice],
        [(across, along, 4 - across - along) for across, along in lattice],
    ]
    face_nodes = np.array(
        [[numbers[point] for point in listing] for listing in face_points], np.int32
    )
    mass_inverse = invert_matrix(mass_matrix)
    lift_tables = []
    for face_number in range(4):
        selector = np.eye(35)[face_nodes[face_number]]
        lift_tables.append(mass_inverse @ selector.T @ face_mass)
    orderings = [(0, 1, 2), (1, 2, 0), (2, 0, 1), (1, 0, 2), (0, 2, 1), (2, 1, 0)]
    lattice_numbers = {point: number for number, point in enumerate(lattice)}
    triples = [(across, along, 4 - across - along) for across, along in lattice]
    turn_nodes = np.array(
        [
            [lattice_numbers[triple[ordering[0]], triple[ordering[1]]] for triple in triples]
            for ordering in orderings
        ],
        np.int32,
    )
    return (
        np.stack(derivs).astype(np.float32),
        np.stack(lift_tables).astype(np.float32),
        face_nodes,
        turn_nodes,
    )


DERIVS, LIFTS, FACE_NODES, TURN = basis_tables()


def np_split(table):
    high = table.astype(ml_dtypes.bfloat16)
    low = (table - high.astype(np.float32)).astype(ml_dtypes.bfloat16)
    return np.concatenate([high, high, low], axis=1)


def deriv_table():
    table = np.zeros((128, KP), np.float32)
    for r in range(3):
        table[r * AP : r * AP + NB, :NB] = DERIVS[r]
    return np_split(table)


def lift_table():
    table = np.zeros((KP, 64), np.float32)
    for x in range(4):
        table[:NB, x * 16 : x * 16 + NFN] = LIFTS[x]
    return np_split(table)


def split(x):
    high = x.astype(BF16)
    low = (x - high.astype(F32)).astype(BF16)
    return high, low


def stack3(x):
    high, low = split(x)
    return jnp.concatenate([high, low, high], axis=0)


def mm(a, b):
    return jnp.dot(a, b, preferred_element_type=F32)


def grad_row(p):
    return (p // 3) * 128 + (p % 3) * AP


def body(
    dims,
    adj_hbm, fwd_hbm, mat_hbm, hs_hbm, hy_hbm,
    cpl_hbm, metric_hbm, normals_hbm, scale_hbm, nbr_hbm, orient_hbm, send_hbm, deriv3_hbm, lift3_hbm,
    fin_hbm, dir_ref,
    hist, fin, cpl, metric, normals, scale, nbr, orient, send, deriv3, lift3,
    lam_b, fwd_b, lam_a, spat, mixg, vol, flux, matp,
    trace, oh_send, oh_nbr, outer,
    msg_d, msg_u, got_d, got_u,
    padded, ct_v, ct_g,
    grads, gt, rs_got, rs_mid, rs_last, prods, turned, hist_t,
    plane_src, plane_got, line_src, line_got, scal,
    load_sem, fin_sem, halo_send, halo_recv, rs_send, rs_recv, known, plane_send, plane_recv, line_send, line_recv,
):
    n_hi, n_q, n_x, n_zl = dims
    n_shot, n_mesh = n_hi * n_q, n_x * n_zl
    n_plane, n_line = n_q * n_x, n_hi * n_zl
    share = NE // n_shot
    s_id = lax.axis_index("shot")
    m_id = lax.axis_index("mesh")
    hi_id, q_id = s_id // n_q, s_id % n_q
    zl_id, x_id = m_id // n_x, m_id % n_x
    has_below = m_id > 0
    has_above = m_id < n_mesh - 1

    plane_peers, line_peers = [], []
    for k in range(1, n_plane):
        other = (q_id * n_x + x_id + k) % n_plane
        plane_peers.append({"shot": hi_id * n_q + other // n_x, "mesh": zl_id * n_x + other % n_x})
    for k in range(1, n_line):
        other = (hi_id * n_zl + zl_id + k) % n_line
        line_peers.append({"shot": (other // n_zl) * n_q + q_id, "mesh": (other % n_zl) * n_x + x_id})

    barrier = pltpu.get_barrier_semaphore()

    @pl.when(has_below)
    def _():
        pl.semaphore_signal(barrier, inc=1, device_id={"mesh": m_id - 1}, device_id_type=MESH)

    @pl.when(has_above)
    def _():
        pl.semaphore_signal(barrier, inc=1, device_id={"mesh": m_id + 1}, device_id_type=MESH)

    def at_plane(step_x, step_q, flip):
        y_id, c_id = q_id // 2, q_id % 2
        other_q = ((y_id + step_q) % (n_q // 2)) * 2 + (c_id + flip) % 2
        return {"shot": hi_id * n_q + other_q, "mesh": zl_id * n_x + (x_id + step_x) % n_x}

    def at_line(step):
        return line_peers[step % n_line - 1]

    core = at_plane(0, 0, 1)
    rounds = [
        [core, at_plane(1, 0, 0), at_plane(n_x - 1, 0, 0), at_plane(0, 1, 0), at_plane(0, n_q // 2 - 1, 0), at_line(1), at_line(-1)],
        [at_plane(2, 0, 0), at_plane(0, 2, 0), at_line(2), at_line(-2)],
        [core, at_line(4), at_line(-4)],
    ]
    def tell(k):
        for peer in rounds[k]:
            pl.semaphore_signal(known.at[k], inc=1, device_id=peer, device_id_type=MESH)

    def hear(k):
        pl.semaphore_wait(known.at[k], len(rounds[k]))

    for f in range(NF):
        lam_b[f, 32:KP, :] = jnp.zeros((KP - 32, NE), F32)
    pairs = [
        (adj_hbm.at[:, :, 0], lam_b.at[:, 0:NB]),
        (send_hbm, send),
        (deriv3_hbm, deriv3),
        (metric_hbm, metric),
        (cpl_hbm, cpl),
        (mat_hbm, matp.at[:, 0:NB]),
        (nbr_hbm, nbr),
        (orient_hbm, orient),
        (normals_hbm, normals),
        (scale_hbm, scale),
        (fwd_hbm.at[:, :, 0], fwd_b.at[0, :, 0:NB]),
        (lift3_hbm, lift3),
        (fwd_hbm.at[:, :, 1], fwd_b.at[1, :, 0:NB]),
        (hs_hbm, hist.at[0:HIST, :, 0:NB]),
        (hy_hbm, hist.at[HIST : 2 * HIST, :, 0:NB]),
    ]
    loads = [pltpu.make_async_copy(src, dst, load_sem.at[k]) for k, (src, dst) in enumerate(pairs)]
    loads[0].start()
    loads[1].start()
    for peer in rounds[0]:
        pl.semaphore_signal(barrier, inc=1, device_id=peer, device_id_type=MESH)

    matp[:, 32:AP, :] = jnp.zeros((NM, AP - 32, NE), F32)
    for t in range(2):
        for f in range(NF):
            fwd_b[t, f, 32:KP, :] = jnp.zeros((KP - 32, NE), F32)
    for k in range(2 * HIST):
        hist[k, :, 32:AP, :] = jnp.zeros((NM, AP - 32, NE), F32)
    for one in loads[2:]:
        one.start()

    lam_a[...] = jnp.zeros(lam_a.shape, F32)
    grads[120:128, :] = jnp.zeros((8, NE), F32)
    grads[248:256, :] = jnp.zeros((8, NE), F32)

    @pl.when(jnp.logical_not(has_below))
    def _():
        got_u[...] = jnp.zeros(got_u.shape, F32)

    @pl.when(jnp.logical_not(has_above))
    def _():
        got_d[...] = jnp.zeros(got_d.shape, F32)

    lane = lax.broadcasted_iota(jnp.int32, (FP, NE), 1)
    low_half = lane < 64
    filled = lax.broadcasted_iota(jnp.int32, (FP, NE), 0) < NF

    def derivative(field):
        for first in range(0, NF, 2):
            group = range(first, min(first + 2, NF))
            out = mm(deriv3[...], jnp.concatenate([stack3(field[f]) for f in group], axis=1))
            for i, f in enumerate(group):
                slab = [out[r * AP : (r + 1) * AP, i * NE : (i + 1) * NE] for r in range(3)]
                for d in range(3):
                    s = metric[0, d : d + 1, :] * slab[0]
                    s = s + metric[1, d : d + 1, :] * slab[1]
                    s = s + metric[2, d : d + 1, :] * slab[2]
                    spat[pl.ds(d * FP + f, AP, stride=KP), :] = s

    def mixed(table, base):
        parts = []
        for j in range(8):
            at = pl.multiple_of((base + j) * KP, KP)
            parts.append(stack3(spat[pl.ds(at, KP), :]))
        return mm(table[...], jnp.concatenate(parts, axis=1))

    def volume():
        derivative(lam_b)

        def block(i, carry):
            base = pl.multiple_of(i * 8, 8)
            mix = mixed(ct_v, base)
            params = [matp[p, pl.ds(base, 8), :] for p in range(NM)]
            for j in range(8):
                acc = params[0][j : j + 1, :] * mix[0:FP, j * NE : (j + 1) * NE]
                for p in range(1, NM):
                    acc = acc + params[p][j : j + 1, :] * mix[p * FP : (p + 1) * FP, j * NE : (j + 1) * NE]
                vol[pl.ds(pl.multiple_of((base + j) * FP, FP), FP), :] = acc
            return carry

        lax.fori_loop(0, AP // 8, block, 0, unroll=True)

    def forward_mix(t):
        derivative(fwd_b.at[t])

        def block(i, carry):
            base = pl.multiple_of(i * 8, 8)
            mix = mixed(ct_g, base)
            for j in range(8):
                at = pl.multiple_of((base + j) * NM * FP, NM * FP)
                mixg[t, pl.ds(at, NM * FP), :] = mix[:, j * NE : (j + 1) * NE]
            return carry

        lax.fori_loop(0, AP // 8, block, 0, unroll=True)

    sub_row = lax.broadcasted_iota(jnp.int32, (8, NE), 0)

    def tree(tiles):
        for step in (4, 2, 1):
            upper = (sub_row // step) % 2 == 1
            half = len(tiles) // 2
            merged = []
            for one, two in zip(tiles[:half], tiles[half:]):
                one = one + pltpu.roll(one, 8 - step, 0)
                two = two + pltpu.roll(two, step, 0)
                merged.append(jnp.where(upper, two, one))
            tiles = merged
        return tiles[0]

    def kernel_sum(t):
        def block(i, carry):
            base = pl.multiple_of(i * 8, 8)
            for p in range(NM):
                tiles = []
                for j in range(8):
                    lam = lam_a[pl.ds(pl.multiple_of((base + j) * FP, FP), FP), :]
                    at = pl.ds(pl.multiple_of((base + j) * NM * FP + p * FP, FP), FP)
                    both = mixg[t, at, :] * lam
                    tiles.append(both[0:8] + both[8:16])
                at = pl.ds(pl.multiple_of(grad_row(p) + base, 8), 8)
                part = tree(tiles) * STEP_SIZE
                grads[at, :] = part if t == 0 else grads[at, :] + part
            return carry

        lax.fori_loop(0, AP // 8, block, 0, unroll=True)

    def inner_of(n, x):
        at = int(FACE_NODES[x][n]) * FP
        return lam_a[at : at + FP, :]

    def halo_copies(t):
        down = pltpu.make_async_remote_copy(
            src_ref=msg_d.at[t, :, 0:NF], dst_ref=got_d.at[t, :, 0:NF], send_sem=halo_send.at[t, 0], recv_sem=halo_recv.at[t, 0],
            device_id={"mesh": m_id - 1}, device_id_type=MESH,
        )
        up = pltpu.make_async_remote_copy(
            src_ref=msg_u.at[t, :, 0:NF], dst_ref=got_u.at[t, :, 0:NF], send_sem=halo_send.at[t, 1], recv_sem=halo_recv.at[t, 1],
            device_id={"mesh": m_id + 1}, device_id_type=MESH,
        )
        return down, up

    def send_traces(t):
        for n in range(NFN):
            for x in range(4):
                high, low = split(inner_of(n, x))
                trace[n * FP : (n + 1) * FP, x * NE : (x + 1) * NE] = high
                trace[240 + n * FP : 240 + (n + 1) * FP, x * NE : (x + 1) * NE] = low
        both = mm(trace[...], oh_send[...])
        picked = both[0:240] + both[240:480]
        halves = []
        for j in range(8):
            first = picked[j * FP : (j + 1) * FP]
            if j < 7:
                second = picked[(j + 8) * FP : (j + 9) * FP]
            else:
                second = jnp.zeros((FP, NE), F32)
            halves.append((first, second))
            msg_d[t, j] = jnp.where(low_half, first, pltpu.roll(second, 64, 1))
        if t == 0:
            n_wait = len(rounds[0])
            pl.semaphore_wait(barrier, n_wait + has_below.astype(jnp.int32) + has_above.astype(jnp.int32))
        down, up = halo_copies(t)

        @pl.when(has_below)
        def _():
            down.start()

        for j, (first, second) in enumerate(halves):
            msg_u[t, j] = jnp.where(low_half, pltpu.roll(first, 64, 1), second)

        @pl.when(has_above)
        def _():
            up.start()

        if t == 0:
            tell(0)

    def gather_local():
        local = mm(trace[...], oh_nbr[0:512, :])
        outer[...] = local[0:240] + local[240:480]

    def surface(t):
        down, up = halo_copies(t)

        @pl.when(has_above)
        def _():
            down.wait_recv()

        @pl.when(has_below)
        def _():
            up.wait_recv()

        tops, bottoms = [], []
        for j in range(8):
            above = jnp.where(filled, got_d[t, j], 0.0)
            below = jnp.where(filled, got_u[t, j], 0.0)
            tops.append(jnp.where(low_half, below, pltpu.roll(above, 64, 1)))
            bottoms.append(jnp.where(low_half, pltpu.roll(below, 64, 1), above))
        ghosts = jnp.concatenate(tops + bottoms[:7], axis=0)
        high, low = split(ghosts)
        part = mm(jnp.concatenate([high, low], axis=0), oh_nbr[512:640, :])
        outer[...] = outer[...] + (part[0:240] + part[240:480])

        turns = [jnp.broadcast_to(orient[x : x + 1, :], (FP, NE)) for x in range(4)]
        halves = [0.5 * scale[x : x + 1, :] for x in range(4)]
        for n in range(NFN):
            sources = {}
            for o in range(6):
                sources.setdefault(int(TURN[o][n]), []).append(o)
            sources = list(sources.items())
            jumps, weighted = [], []
            for x in range(4):
                at = sources[0][0] * FP
                value = outer[at : at + FP, x * NE : (x + 1) * NE]
                for node, options in sources[1:]:
                    mask = turns[x] == options[0]
                    for o in options[1:]:
                        mask = mask | (turns[x] == o)
                    value = jnp.where(mask, outer[node * FP : (node + 1) * FP, x * NE : (x + 1) * NE], value)
                jump = value - inner_of(n, x)
                jumps.append(jump)
                weighted.append(
                    stack3(jnp.concatenate([normals[d, x : x + 1, :] * jump for d in range(3)], axis=0))
                )
            mix = mm(ct_v[...], jnp.concatenate(weighted, axis=1))
            for x in range(4):
                node = int(FACE_NODES[x][n])
                acc = jumps[x]
                for p in range(NM):
                    acc = acc + matp[p, node : node + 1, :] * mix[p * FP : (p + 1) * FP, x * NE : (x + 1) * NE]
                at = (x * 16 + n) * FP
                flux[at : at + FP, :] = acc * halves[x]

        for first in range(0, NF, 2):
            group = range(first, min(first + 2, NF))
            rhs = [stack3(flux[pl.ds(g, 64, stride=FP), :]) for g in group]
            out = mm(lift3[...], jnp.concatenate(rhs, axis=1))
            for i, g in enumerate(group):
                change = out[0:AP, i * NE : (i + 1) * NE] + vol[pl.ds(g, AP, stride=FP), :]
                new = lam_b[g, 0:AP, :] + STEP_SIZE * change
                if t == 0:
                    lam_b[g, 0:AP, :] = new
                else:
                    fin[g] = new
                lam_a[pl.ds(g, AP, stride=FP), :] = new

    yy_row = {}
    for i in range(HIST):
        for j in range(i, HIST):
            yy_row[i, j] = yy_row[j, i] = 25 + len([k for k in yy_row if k[0] <= k[1]])

    def dot_rows(i, j):
        acc = hist[i, 0] * hist[j, 0]
        for p in range(1, NM):
            acc = acc + hist[i, p] * hist[j, p]
        return jnp.sum(acc, axis=0, keepdims=True)

    def history():
        prods[...] = jnp.zeros(prods.shape, F32)
        for i in range(HIST):
            for j in range(HIST):
                row = i * HIST + j
                prods[row : row + 1, :] = dot_rows(i, HIST + j)
                if j >= i:
                    row = yy_row[i, j]
                    prods[row : row + 1, :] = dot_rows(HIST + i, HIST + j)

    def selections():
        for k in (6, 7):
            loads[k].wait()
        rows_n = lax.broadcasted_iota(jnp.int32, (640, NE), 0)
        for x in range(4):
            oh_nbr[:, x * NE : (x + 1) * NE] = jnp.where(rows_n == nbr[x : x + 1, :], 1.0, 0.0).astype(BF16)

    def tables():
        loads[4].wait()
        padded[...] = jnp.zeros(padded.shape, F32)
        for p in range(NM):
            for d in range(3):
                padded[p, d * FP : d * FP + NF, 0:NF] = cpl[d, p]
        for p in range(NM):
            flipped = jnp.transpose(padded[p])[0:FP]
            straight = padded[p, 0:FP]
            for d in range(1, 3):
                straight = straight + pltpu.roll(padded[p, d * FP : (d + 1) * FP], d * FP, 1)
            for block, dst in ((flipped, ct_v), (straight, ct_g)):
                high = block.astype(BF16).astype(F32)
                low = pltpu.roll(block - high, 2 * KP, 1)
                first = jnp.where(lane < KP, high, jnp.where(lane < 2 * KP, pltpu.roll(high, KP, 1), low))
                dst[p * FP : (p + 1) * FP, 0:NE] = first.astype(BF16)
                dst[p * FP : (p + 1) * FP, NE : 3 * KP] = low[:, 0 : 3 * KP - NE].astype(BF16)

    def clear(i, carry):
        spat[pl.ds(pl.multiple_of(i * KP, KP), KP), :] = jnp.zeros((KP, NE), F32)
        return carry

    loads[1].wait()
    rows_s = lax.broadcasted_iota(jnp.int32, (512, NE), 0)
    oh_send[...] = jnp.where(rows_s == send[...], 1.0, 0.0).astype(BF16)
    loads[0].wait()
    for f in range(NF):
        lam_a[pl.ds(f, AP, stride=FP), :] = lam_b[f, 0:AP, :]
    send_traces(0)
    tables()
    lax.fori_loop(0, AP, clear, 0, unroll=8)
    for x in range(4):
        flux[(x * 16 + 15) * FP : (x * 16 + 16) * FP, :] = jnp.zeros((FP, NE), F32)
    for k in (2, 3, 5):
        loads[k].wait()
    volume()
    selections()
    gather_local()
    loads[10].wait()
    forward_mix(0)
    for k in (13, 14):
        loads[k].wait()
    history()
    gram = jnp.sum(jnp.transpose(prods[...]), axis=0, keepdims=True) * (1.0 / n_shot)
    for k in (8, 9, 11):
        loads[k].wait()
    surface(0)
    send_traces(1)
    hear(0)
    tell(1)
    gather_local()
    volume()
    hear(1)
    tell(2)
    loads[12].wait()
    forward_mix(1)
    kernel_sum(0)
    surface(1)

    kernel_sum(1)
    for k in range(2 * HIST):
        acc = hist[k, 0] * grads[0:AP, :]
        for p in range(1, NM):
            acc = acc + hist[k, p] * grads[grad_row(p) : grad_row(p) + AP, :]
        row = 120 + (k // HIST) * 128 + k % HIST
        grads[row : row + 1, :] = jnp.sum(acc, axis=0, keepdims=True)
    left = jnp.transpose(grads[0:128, :])
    right = jnp.transpose(grads[128:256, :])
    row_lane = lax.broadcasted_iota(jnp.int32, (1, NE), 1)
    vector = jnp.where(
        row_lane >= 120,
        jnp.sum(left, axis=0, keepdims=True),
        jnp.where(row_lane >= 112, pltpu.roll(jnp.sum(right, axis=0, keepdims=True), 120, 1), gram),
    )
    plane_src[...] = vector
    hear(2)
    planes = [
        pltpu.make_async_remote_copy(
            src_ref=plane_src, dst_ref=plane_got.at[k], send_sem=plane_send.at[k], recv_sem=plane_recv.at[k],
            device_id=peer, device_id_type=MESH,
        )
        for k, peer in enumerate(plane_peers)
    ]
    for one in planes:
        one.start()

    half = n_q * share
    for h in range(n_hi):
        gt[h, :, 0:128] = left[h * half : (h + 1) * half]
        gt[h, :, 128:256] = right[h * half : (h + 1) * half]
    firsts = []
    for o in range(1, n_q):
        peer_q = (q_id + o) % n_q
        firsts.append(
            pltpu.make_async_remote_copy(
                src_ref=gt.at[:, pl.ds(pl.multiple_of(peer_q * share, share), share), :],
                dst_ref=rs_got.at[o - 1],
                send_sem=rs_send.at[o - 1], recv_sem=rs_recv.at[o - 1],
                device_id={"shot": hi_id * n_q + peer_q}, device_id_type=MESH,
            )
        )
    for one in firsts:
        one.start()
    final_out = pltpu.make_async_copy(fin.at[:, 0:NB], fin_hbm.at[:, :, 0], fin_sem.at[0])
    final_out.start()

    def turn_history(k, carry):
        for side in range(2):
            block = [hist[k, side * 3 + p] for p in range(3)] + [jnp.zeros((8, NE), F32)]
            turned[:, side * 128 : (side + 1) * 128] = jnp.transpose(jnp.concatenate(block, axis=0))
        hist_t[k] = turned[pl.ds(pl.multiple_of(s_id * share, share), share), :]
        return carry

    lax.fori_loop(0, 2 * HIST, turn_history, 0, unroll=2)

    mine = gt[:, pl.ds(pl.multiple_of(q_id * share, share), share), :]
    for o, one in enumerate(firsts):
        one.wait_recv()
        mine = mine + rs_got[o]
    rs_mid[...] = mine
    seconds = []
    for o in range(1, n_hi):
        seconds.append(
            pltpu.make_async_remote_copy(
                src_ref=rs_mid.at[(hi_id + o) % n_hi],
                dst_ref=rs_last.at[o - 1],
                send_sem=rs_send.at[n_q - 2 + o], recv_sem=rs_recv.at[n_q - 2 + o],
                device_id={"shot": ((hi_id + o) % n_hi) * n_q + q_id}, device_id_type=MESH,
            )
        )
    for one in seconds:
        one.start()

    def collected(value, copies, got):
        sums = [value, None, None, None]
        for k, one in enumerate(copies):
            one.wait_recv()
            at = (k + 1) % 4
            sums[at] = got[k] if sums[at] is None else sums[at] + got[k]
        sums = [one for one in sums if one is not None]
        while len(sums) > 1:
            sums = sums[2:] + [sums[0] + sums[1]]
        return sums[0]

    vector = collected(vector, planes, plane_got)
    line_src[...] = vector
    lines = [
        pltpu.make_async_remote_copy(
            src_ref=line_src, dst_ref=line_got.at[k], send_sem=line_send.at[k], recv_sem=line_recv.at[k],
            device_id=peer, device_id_type=MESH,
        )
        for k, peer in enumerate(line_peers)
    ]
    for one in lines:
        one.start()
    total = rs_mid[hi_id]
    for t in range(2):
        down, up = halo_copies(t)

        @pl.when(has_below)
        def _():
            down.wait_send()

        @pl.when(has_above)
        def _():
            up.wait_send()

    for one in planes + firsts:
        one.wait_send()
    final_out.wait()
    for o, one in enumerate(seconds):
        one.wait_recv()
        total = total + rs_last[o]
    vector = collected(vector, lines, line_got)

    scal[...] = jnp.transpose(jnp.broadcast_to(vector, (NE, NE)))

    def num(k):
        return scal[k : k + 1, :]

    def sy(i, j):
        return num(i * HIST + j)

    over = [1.0 / sy(i, i) for i in range(HIST)]
    gamma = sy(HIST - 1, HIST - 1) / num(yy_row[HIST - 1, HIST - 1])
    alphas = [None] * HIST
    for i in reversed(range(HIST)):
        value = num(120 + i)
        for j in reversed(range(i + 1, HIST)):
            value = value - alphas[j] * sy(i, j)
        alphas[i] = value * over[i]
    rest = []
    for i in range(HIST):
        value = num(112 + i)
        for j in range(HIST):
            value = value - alphas[j] * num(yy_row[i, j])
        value = gamma * value
        for j in range(i):
            value = value + rest[j] * sy(j, i)
        rest.append(alphas[i] - value * over[i])

    sides = []
    for side in range(2):
        lanes = slice(side * 128, (side + 1) * 128)
        acc = -total[:, lanes]
        for i in range(HIST):
            acc = acc + alphas[i] * hist_t[HIST + i, :, lanes]
        acc = gamma * acc
        for i in range(HIST):
            acc = acc - rest[i] * hist_t[i, :, lanes]
        sides.append(acc)
    for p in range(NM):
        at = (p % 3) * AP
        dir_ref[p] = sides[p // 3][:, at : at + NB]

    for one in seconds + lines:
        one.wait_send()


def shards(
    dims,
    adjoint_state,
    forward_states,
    material,
    coupling,
    metric,
    face_normals,
    face_scale,
    face_neighbours,
    face_orientation,
    send_faces,
    history_steps,
    history_changes,
):
    n_hi, n_q, n_x, n_zl = dims
    share = NE // (n_hi * n_q)
    n_plane, n_line = n_q * n_x, n_hi * n_zl
    vmem = pl.BlockSpec(memory_space=pltpu.VMEM)
    hbm = pl.BlockSpec(memory_space=pltpu.HBM)
    dma = pltpu.SemaphoreType.DMA
    i32 = jnp.int32
    final, direction = pl.pallas_call(
        functools.partial(body, dims),
        out_shape=(
            jax.ShapeDtypeStruct((NF, NB, 1, NE), F32),
            jax.ShapeDtypeStruct((NM, share, NB), F32),
        ),
        in_specs=[hbm] * 14,
        out_specs=(hbm, vmem),
        scratch_shapes=[
            pltpu.VMEM((2 * HIST, NM, AP, NE), F32),
            pltpu.VMEM((NF, AP, NE), F32),
            pltpu.VMEM((3, NM, NF, NF), F32),
            pltpu.VMEM((3, 3, NE), F32),
            pltpu.VMEM((3, 4, NE), F32),
            pltpu.VMEM((4, NE), F32),
            pltpu.VMEM((4, NE), i32),
            pltpu.VMEM((4, NE), i32),
            pltpu.VMEM((1, NE), i32),
            pltpu.VMEM((128, 3 * KP), BF16),
            pltpu.VMEM((KP, 192), BF16),
            pltpu.VMEM((NF, KP, NE), F32),
            pltpu.VMEM((2, NF, KP, NE), F32),
            pltpu.VMEM((AP * FP, NE), F32),
            pltpu.VMEM((AP * KP, NE), F32),
            pltpu.VMEM((2, AP * NM * FP, NE), F32),
            pltpu.VMEM((AP * FP, NE), F32),
            pltpu.VMEM((64 * FP, NE), F32),
            pltpu.VMEM((NM, AP, NE), F32),
            pltpu.VMEM((480, 512), BF16),
            pltpu.VMEM((512, NE), BF16),
            pltpu.VMEM((640, 512), BF16),
            pltpu.VMEM((240, 512), F32),
            pltpu.VMEM((2, 8, FP, NE), F32),
            pltpu.VMEM((2, 8, FP, NE), F32),
            pltpu.VMEM((2, 8, FP, NE), F32),
            pltpu.VMEM((2, 8, FP, NE), F32),
            pltpu.VMEM((NM, NE, NE), F32),
            pltpu.VMEM((NM * FP, 3 * KP), BF16),
            pltpu.VMEM((NM * FP, 3 * KP), BF16),
            pltpu.VMEM((256, NE), F32),
            pltpu.VMEM((n_hi, n_q * share, 256), F32),
            pltpu.VMEM((n_q - 1, n_hi, share, 256), F32),
            pltpu.VMEM((n_hi, share, 256), F32),
            pltpu.VMEM((n_hi - 1, share, 256), F32),
            pltpu.VMEM((NE, NE), F32),
            pltpu.VMEM((NE, 256), F32),
            pltpu.VMEM((2 * HIST, share, 256), F32),
            pltpu.VMEM((1, NE), F32),
            pltpu.VMEM((n_plane - 1, 1, NE), F32),
            pltpu.VMEM((1, NE), F32),
            pltpu.VMEM((n_line - 1, 1, NE), F32),
            pltpu.VMEM((NE, NE), F32),
            dma((15,)),
            dma((1,)),
            dma((2, 2)),
            dma((2, 2)),
            dma((n_q + n_hi - 2,)),
            dma((n_q + n_hi - 2,)),
            pltpu.SemaphoreType.REGULAR((3,)),
            dma((n_plane - 1,)),
            dma((n_plane - 1,)),
            dma((n_line - 1,)),
            dma((n_line - 1,)),
        ],
        compiler_params=pltpu.CompilerParams(
            collective_id=0, has_side_effects=True, vmem_limit_bytes=63 * 2**20
        ),
    )(
        jnp.transpose(adjoint_state, (1, 2, 0, 3)), jnp.transpose(forward_states[0], (1, 2, 0, 3)),
        material, history_steps, history_changes,
        coupling, metric, face_normals, face_scale, face_neighbours, face_orientation,
        send_faces.reshape(1, -1), jnp.asarray(deriv_table()), jnp.asarray(lift_table()),
    )
    return jnp.transpose(final, (2, 0, 1, 3)), jnp.transpose(direction, (0, 2, 1))


def dims_of(mesh):
    n_shot, n_mesh = mesh.shape["shot"], mesh.shape["mesh"]
    n_x = 4 if n_mesh >= 16 else 2
    return 2, n_shot // 2, n_x, n_mesh // n_x


def solution(mesh):
    placed = (
        P("shot", None, None, "mesh"),
        P("shot", None, None, None, "mesh"),
        P(None, None, "mesh"),
        P(),
        P(None, None, "mesh"),
        P(None, None, "mesh"),
        P(None, "mesh"),
        P(None, "mesh"),
        P(None, "mesh"),
        P("mesh"),
        P(None, None, None, "mesh"),
        P(None, None, None, "mesh"),
    )
    return jax.shard_map(
        functools.partial(shards, dims_of(mesh)),
        mesh=mesh,
        in_specs=placed,
        out_specs=(P("shot", None, None, "mesh"), P(None, None, ("mesh", "shot"))),
        check_vma=False,
    )
```
